32 devices in a mesh: cells: 32 (over z, y, x, core).
Axes of the slice: x: 2, y: 2, z: 4, core: 2. Of those that a mesh axis runs over, the one named last changes fastest.
Arguments:
- block: bfloat16 [6912, 128], P('cells'), may hold values from -6 to 6
- cell_matrix: bfloat16 [32, 343, 343], P('cells'), may hold values from -1 to 3
- connectivity: int32 [32, 343], P('cells'), may hold values from 0 to 342, as said below
- potential: float32 [10976], P('cells'), may hold values from -1.5 to 1.5
- locked: bfloat16 [6912, 704], P('cells'), may hold values from -0.078125 to 0.078125
Outputs:
- filtered: bfloat16 [6912, 128], P('cells')
- intersection: float32 [704, 128], replicated
The draws below stay inside these ranges and needn't reach their ends.
Inputs may be any that keep to these rules, and one draw needn't show every extreme that they name: `connectivity`: A partition's 1 row list each of its 1 x 1 x 1 cells once, in some order; a row gives the local slots of that sixth-order hexahedron's 343 nodes, in some order, where a node with local coordinates (i, j, k), each from 0 to 6, has slot (i * 7 + j) * 7 + k; neighbouring cells share nodes.
All inputs are finite; a program needn't handle non-finite values.
Results may differ from the reference program's by a relative error of at most 0.0067.
Values may be sent and summed in bfloat16 or wider, within the bound.
No kernel may reach another device: no remote copies, remote signals or barrier semaphores. Data moves between devices by JAX's collectives and lax.ppermute only.
A program may use at most 64 MiB of HBM per device.

```python
import math
import jax
import jax.numpy as jnp
from jax import lax

NPC = 343
STATES = 128
LOCKED = 704
CB = 1
GRID_Y = 4
GRID_Z = 4
CELLS_DEV = 1
SIDE = 7
NODE_DEV = 343
ALL_CELLS = 32
NODES = 6912
SLOTS = 10976
N_CELLS = 32


def draw_cell_matrix(key, part):
    key_offdiag = jax.random.fold_in(key, 11)
    key_diagonal = jax.random.fold_in(key, 12)
    spread = 0.6 / math.sqrt(NPC)
    offdiag = jnp.clip(jax.random.normal(key_offdiag, (ALL_CELLS, NPC, NPC), jnp.float32), -6.0, 6.0) * spread
    diagonal = jax.random.uniform(key_diagonal, (ALL_CELLS, NPC), jnp.float32, 0.5, 1.5)
    identity = jnp.eye(NPC, dtype=jnp.float32)
    return (offdiag + diagonal[:, :, None] * identity).astype(jnp.bfloat16)


def node_order(order_key):
    return jax.random.permutation(order_key, NPC).astype(jnp.int32)


def draw_connectivity(key, part):
    within = jnp.arange(NPC, dtype=jnp.int32)
    node_u = within // 49
    node_v = within // 7 % 7
    node_w = within % 7
    cell_ids = jnp.arange(CELLS_DEV, dtype=jnp.int32)
    cell_a = cell_ids // (CB * CB)
    cell_b = cell_ids // CB % CB
    cell_c = cell_ids % CB
    slot_table = ((6 * cell_a[:, None] + node_u[None, :]) * SIDE + 6 * cell_b[:, None] + node_v[None, :]) * SIDE + 6 * cell_c[:, None] + node_w[None, :]

    def one_part(part_key):
        cell_order = jax.random.permutation(jax.random.fold_in(part_key, 1), CELLS_DEV).astype(jnp.int32)
        orders = jax.vmap(node_order)(jax.random.split(jax.random.fold_in(part_key, 2), CELLS_DEV))
        chosen = jnp.take(slot_table, cell_order, axis=0)
        return jnp.take_along_axis(chosen, orders, axis=1)
    part_keys = jax.random.split(jax.random.fold_in(key, 21), ALL_CELLS // CELLS_DEV)
    return jax.vmap(one_part)(part_keys).reshape(ALL_CELLS, NPC).astype(jnp.int32)


def steps_of(stream_key, shape, shards, low, largest):
    def one(axis_at, shards_of):
        heights = jax.random.uniform(jax.random.fold_in(jax.random.fold_in(stream_key, 6), axis_at), (shards_of,), jnp.float32, low / len(shards), largest / len(shards))
        return jnp.repeat(jnp.exp(heights), shape[axis_at] // shards_of).reshape((-1,) + (1,) * (len(shape) - axis_at - 1))

    gain = one(*shards[0])
    for cut in shards[1:]:
        gain = gain * one(*cut)
    return gain


def centred(stream_key, shape, scale, limit, cuts=(), kind=jnp.bfloat16):
    entries = jax.random.normal(stream_key, shape, jnp.float32) * scale
    if len(cuts) > 0:
        entries = steps_of(stream_key, shape, cuts, -0.22, 0.18) * entries
    return jnp.clip(entries, min=-limit, max=limit).astype(kind)


def setup_inputs(seed: int = 0) -> dict:
    streams_of = jax.random.split(jax.random.key(seed), 6)
    block = centred(streams_of[0], (NODES, STATES), 1.0, 6.0, ((0, 32),))
    cell_matrix = draw_cell_matrix(jax.random.fold_in(streams_of[5], 71), 0)
    connectivity = draw_connectivity(jax.random.fold_in(streams_of[5], 71), 0)
    potential = jnp.clip(jax.random.uniform(streams_of[3], (SLOTS,), jnp.float32, -1.5, 1.5) * steps_of(streams_of[3], (SLOTS,), ((0, 32),), -0.4, 0.0), -1.5, 1.5)
    locked = centred(streams_of[4], (NODES, LOCKED), NODES ** -0.5, 0.078125, ((0, 32),))
    return {"block": block, "cell_matrix": cell_matrix, "connectivity": connectivity, "potential": potential, "locked": locked}


chebyshev_coeffs = ((-1.0 / 7.0, 0.0), (-7.0 / 41.0, 8.0 / 41.0), (-41.0 / 259.0, 28.0 / 259.0))
centre = 6.0


def cell_terms(local_rows, matrices, links, lumped):
    gathered = jnp.take(local_rows, links, axis=0).astype(jnp.float32)
    products = jnp.einsum("cij,cjs->cis", matrices.astype(jnp.float32), gathered)
    summed = jnp.zeros((NODE_DEV, STATES), jnp.float32).at[links.reshape(-1)].add(products.reshape(-1, STATES))
    return summed + lumped[:, None] * local_rows.astype(jnp.float32)


def advance(applied, previous, older, coeffs):
    return (coeffs[0] * (applied - centre * previous.astype(jnp.float32)) - coeffs[1] * older.astype(jnp.float32)).astype(jnp.bfloat16)


def reference(block, cell_matrix, connectivity, potential, locked):
    edge = 6 * CB
    grid_x = N_CELLS // (GRID_Y * GRID_Z)
    matrices = cell_matrix.reshape(N_CELLS, CELLS_DEV, NPC, NPC)
    links = connectivity.reshape(N_CELLS, CELLS_DEV, NPC)
    lumped = potential.reshape(N_CELLS, NODE_DEV)
    window = (SIDE, SIDE, SIDE, STATES)

    def apply_operator(states):
        grid = states.reshape(grid_x, GRID_Y, GRID_Z, edge, edge, edge, STATES)
        grid = grid.transpose(0, 3, 1, 4, 2, 5, 6).reshape(grid_x * edge, GRID_Y * edge, GRID_Z * edge, STATES)
        padded = jnp.pad(grid, ((1, 0), (1, 0), (1, 0), (0, 0)))

        def one_part(index, total):
            part = jnp.asarray(index).astype(jnp.int32)
            part_x = part // (GRID_Y * GRID_Z)
            part_y = (part // GRID_Z) % GRID_Y
            part_z = part % GRID_Z
            start = (part_x * edge, part_y * edge, part_z * edge, jnp.zeros((), jnp.int32))
            local_rows = lax.dynamic_slice(padded, start, window).reshape(NODE_DEV, STATES)
            partial_value = cell_terms(local_rows, matrices[part], links[part], lumped[part])
            updated = lax.dynamic_slice(total, start, window) + partial_value.reshape(window)
            return lax.dynamic_update_slice(total, updated, start)

        total = lax.fori_loop(0, N_CELLS, one_part, jnp.zeros(padded.shape, jnp.float32))
        owned = total[1:, 1:, 1:].reshape(grid_x, edge, GRID_Y, edge, GRID_Z, edge, STATES)
        return owned.transpose(0, 2, 4, 1, 3, 5, 6).reshape(NODES, STATES)

    older = block
    current = block
    for coeffs in chebyshev_coeffs:
        following = advance(apply_operator(current), current, older, coeffs)
        older = current
        current = following
    filtered = current
    intersection = jnp.einsum("nl,ns->ls", locked.astype(jnp.float32), filtered.astype(jnp.float32))
    return filtered, intersection
```

```python
import jax
import jax.numpy as jnp
from jax import lax
from jax.sharding import PartitionSpec as P

GRID_Y = 4
GRID_Z = 4
SIDE = 7
AXIS = "cells"

chebyshev_coeffs = ((-1.0 / 7.0, 0.0), (-7.0 / 41.0, 8.0 / 41.0), (-41.0 / 259.0, 28.0 / 259.0))
centre = 6.0


class Grid:
    def __init__(self):
        self.devices = lax.axis_size(AXIS)
        self.counts = (self.devices // (GRID_Y * GRID_Z), GRID_Y, GRID_Z)
        self.stride = (GRID_Y * GRID_Z, GRID_Z, 1)
        position = lax.axis_index(AXIS)
        self.coords = tuple(
            position // self.stride[d] % self.counts[d] for d in range(3)
        )

    def coord_of(self, device, dim):
        return device // self.stride[dim] % self.counts[dim]

    def up(self, value, dim):
        by = self.stride[dim]
        pairs = [
            (i, i + by)
            for i in range(self.devices)
            if self.coord_of(i, dim) + 1 < self.counts[dim]
        ]
        return lax.ppermute(value, AXIS, pairs)

    def down(self, value, dim):
        by = self.stride[dim]
        pairs = [
            (i, i - by) for i in range(self.devices) if self.coord_of(i, dim) > 0
        ]
        return lax.ppermute(value, AXIS, pairs)

    def swapped(self, low, high, dim, odd):
        by = self.stride[dim]
        pairs = []
        for i in range(self.devices):
            c = self.coord_of(i, dim)
            if c % 2 == odd and c + 1 < self.counts[dim]:
                pairs += [(i, i + by), (i + by, i)]
        lower = self.coords[dim] % 2 == odd
        arrived = lax.ppermute(jnp.where(lower, high, low), AXIS, pairs)
        zero = jnp.zeros_like(arrived)
        return jnp.where(lower, zero, arrived), jnp.where(lower, arrived, zero)


def plane(field, dim, at):
    return lax.slice_in_dim(field, at, at + 1, axis=dim)


def with_ends(field, dim, low, high):
    last = field.shape[dim] - 1
    parts = [
        plane(field, dim, 0) if low is None else low,
        lax.slice_in_dim(field, 1, last, axis=dim),
        plane(field, dim, last) if high is None else high,
    ]
    return jnp.concatenate(parts, axis=dim)


def slots_matrix(cell_matrix, connectivity, slot_count):
    total = None
    for c in range(cell_matrix.shape[0]):
        chosen = (
            connectivity[c][:, None] == jnp.arange(slot_count, dtype=jnp.int32)[None, :]
        ).astype(jnp.bfloat16)
        rows = lax.dot_general(
            chosen, cell_matrix[c], (((0,), (0,)), ((), ())), preferred_element_type=jnp.float32
        ).astype(jnp.bfloat16)
        both = jnp.dot(rows, chosen, preferred_element_type=jnp.float32)
        total = both if total is None else total + both
    return total.astype(jnp.bfloat16)


def summed_everywhere(value):
    n = lax.axis_size(AXIS)
    rows, columns = value.shape
    per = -(-rows // n)
    padded = jnp.pad(value.astype(jnp.bfloat16), ((0, n * per - rows), (0, 0)))
    dealt = lax.all_to_all(padded.reshape(n, per, columns), AXIS, 0, 0)
    mine = jnp.sum(dealt.astype(jnp.float32), axis=0).astype(jnp.bfloat16)
    back = lax.all_to_all(jnp.broadcast_to(mine[None], (n, per, columns)), AXIS, 0, 0)
    return back.reshape(n * per, columns)[:rows].astype(jnp.float32)


def per_device(block, cell_matrix, connectivity, potential, locked):
    owned_rows, columns = block.shape
    slot_count = potential.shape[0]
    edge = SIDE - 1
    grid = Grid()
    shape = (SIDE, SIDE, SIDE, columns)
    matrix = slots_matrix(cell_matrix, connectivity, slot_count)
    lumped = potential[:, None]

    field = (
        jnp.zeros(shape, jnp.bfloat16)
        .at[1:, 1:, 1:]
        .set(block.reshape(edge, edge, edge, columns))
    )
    for dim in range(3):
        field = with_ends(field, dim, grid.up(plane(field, dim, SIDE - 1), dim), None)

    inside = jnp.ones((SIDE, SIDE, SIDE, 1), jnp.bool_)
    for dim in range(3):
        at = lax.broadcasted_iota(jnp.int32, (SIDE, SIDE, SIDE, 1), dim)
        inside = inside & ((at > 0) | (grid.coords[dim] > 0))

    older = field
    current = field
    steps = len(chebyshev_coeffs)
    for step, coeffs in enumerate(chebyshev_coeffs):
        rows = current.reshape(slot_count, columns)
        partial = jnp.dot(matrix, rows, preferred_element_type=jnp.float32)
        partial = (partial + lumped * rows.astype(jnp.float32)).reshape(shape)
        for dim in (2, 1, 0):
            low, high = plane(partial, dim, 0), plane(partial, dim, SIDE - 1)
            if step < steps - 1:
                low16, high16 = low.astype(jnp.bfloat16), high.astype(jnp.bfloat16)
                for odd in (0, 1):
                    if grid.counts[dim] > odd + 1:
                        to_low, to_high = grid.swapped(low16, high16, dim, odd)
                        low = low + to_low.astype(jnp.float32)
                        high = high + to_high.astype(jnp.float32)
                partial = with_ends(partial, dim, low, high)
            else:
                arrived = grid.down(low.astype(jnp.bfloat16), dim)
                partial = with_ends(partial, dim, None, high + arrived.astype(jnp.float32))
        following = coeffs[0] * (partial - centre * current.astype(jnp.float32)) - coeffs[
            1
        ] * older.astype(jnp.float32)
        following = jnp.where(inside, following, 0.0).astype(jnp.bfloat16)
        older = current
        current = following
    filtered = current[1:, 1:, 1:].reshape(owned_rows, columns)
    partial_intersection = jnp.einsum(
        "nl,ns->ls", locked, filtered, preferred_element_type=jnp.float32
    )
    return filtered, summed_everywhere(partial_intersection)


def solution(mesh):
    in_specs = (
        P(AXIS, None),
        P(AXIS, None, None),
        P(AXIS, None),
        P(AXIS),
        P(AXIS, None),
    )
    out_specs = (P(AXIS, None), P())
    return jax.shard_map(
        per_device, mesh=mesh, in_specs=in_specs, out_specs=out_specs, check_vma=False
    )
```

```python
import jax
import jax.numpy as jnp
from jax import lax
from jax.sharding import PartitionSpec as P

GRID_Y = 4
GRID_Z = 4
SIDE = 7
AXIS = "cells"

chebyshev_coeffs = ((-1.0 / 7.0, 0.0), (-7.0 / 41.0, 8.0 / 41.0), (-41.0 / 259.0, 28.0 / 259.0))
centre = 6.0


class Grid:
    def __init__(self):
        self.devices = lax.axis_size(AXIS)
        self.counts = (self.devices // (GRID_Y * GRID_Z), GRID_Y, GRID_Z)
        self.stride = (GRID_Y * GRID_Z, GRID_Z, 1)
        position = lax.axis_index(AXIS)
        self.coords = tuple(
            position // self.stride[d] % self.counts[d] for d in range(3)
        )

    def coord_of(self, device, dim):
        return device // self.stride[dim] % self.counts[dim]

    def swapped(self, low, high, dim, odd):
        by = self.stride[dim]
        pairs = []
        for i in range(self.devices):
            c = self.coord_of(i, dim)
            if c % 2 == odd and c + 1 < self.counts[dim]:
                pairs += [(i, i + by), (i + by, i)]
        lower = self.coords[dim] % 2 == odd
        arrived = lax.ppermute(jnp.where(lower, high, low), AXIS, pairs)
        zero = jnp.zeros_like(arrived)
        return jnp.where(lower, zero, arrived), jnp.where(lower, arrived, zero)

    def exchanged(self, low, high, dim):
        to_low, to_high = self.swapped(low, high, dim, 0)
        if self.counts[dim] > 2:
            more_low, more_high = self.swapped(low, high, dim, 1)
            to_low, to_high = to_low + more_low, to_high + more_high
        return to_low, to_high


def plane(field, dim, at):
    return lax.slice_in_dim(field, at, at + 1, axis=dim)


def with_ends(field, dim, low, high):
    last = field.shape[dim] - 1
    parts = [
        plane(field, dim, 0) if low is None else low,
        lax.slice_in_dim(field, 1, last, axis=dim),
        plane(field, dim, last) if high is None else high,
    ]
    return jnp.concatenate(parts, axis=dim)


def slots_matrix(cell_matrix, connectivity, slot_count):
    total = None
    for c in range(cell_matrix.shape[0]):
        chosen = (
            connectivity[c][:, None] == jnp.arange(slot_count, dtype=jnp.int32)[None, :]
        ).astype(jnp.bfloat16)
        rows = lax.dot_general(
            chosen, cell_matrix[c], (((0,), (0,)), ((), ())), preferred_element_type=jnp.float32
        ).astype(jnp.bfloat16)
        both = jnp.dot(rows, chosen, preferred_element_type=jnp.float32)
        total = both if total is None else total + both
    return total.astype(jnp.bfloat16)


def summed_everywhere(value):
    n = lax.axis_size(AXIS)
    groups = [list(range(first, n, 2)) for first in range(2)]
    second = lax.axis_index(AXIS) % 2 == 1
    partner = [(i, i ^ 1) for i in range(n)]
    rows, columns = value.shape
    per = -(-rows // n)
    halves = jnp.pad(value, ((0, n * per - rows), (0, 0))).reshape(2, n * per // 2, columns)
    away = jnp.where(second, halves[0], halves[1]).astype(jnp.bfloat16)
    arrived = lax.ppermute(away, AXIS, partner)
    kept = jnp.where(second, halves[1], halves[0]) + arrived.astype(jnp.float32)
    parts = kept.astype(jnp.bfloat16).reshape(n // 2, per, columns)
    dealt = lax.all_to_all(parts, AXIS, 0, 0, axis_index_groups=groups)
    mine = jnp.sum(dealt.astype(jnp.float32), axis=0).astype(jnp.bfloat16)
    back = lax.all_to_all(
        jnp.broadcast_to(mine[None], parts.shape), AXIS, 0, 0, axis_index_groups=groups
    ).reshape(n * per // 2, columns)
    other = lax.ppermute(back, AXIS, partner)
    both = jnp.concatenate([jnp.where(second, other, back), jnp.where(second, back, other)])
    return both[:rows].astype(jnp.float32)


def per_device(block, cell_matrix, connectivity, potential, locked):
    owned_rows, columns = block.shape
    slot_count = potential.shape[0]
    edge = SIDE - 1
    grid = Grid()
    shape = (SIDE, SIDE, SIDE, columns)
    matrix = slots_matrix(cell_matrix, connectivity, slot_count)
    lumped = potential[:, None]

    field = (
        jnp.zeros(shape, jnp.bfloat16)
        .at[1:, 1:, 1:]
        .set(block.reshape(edge, edge, edge, columns))
    )
    for dim in range(3):
        high = plane(field, dim, SIDE - 1)
        field = with_ends(field, dim, grid.exchanged(high, high, dim)[0], None)

    inside = jnp.ones((SIDE, SIDE, SIDE, 1), jnp.bool_)
    for dim in range(3):
        at = lax.broadcasted_iota(jnp.int32, (SIDE, SIDE, SIDE, 1), dim)
        inside = inside & ((at > 0) | (grid.coords[dim] > 0))

    older = field
    current = field
    steps = len(chebyshev_coeffs)
    for step, coeffs in enumerate(chebyshev_coeffs):
        rows = current.reshape(slot_count, columns)
        partial = jnp.dot(matrix, rows, preferred_element_type=jnp.float32)
        partial = (partial + lumped * rows.astype(jnp.float32)).reshape(shape)
        for dim in (2, 1, 0):
            low, high = plane(partial, dim, 0), plane(partial, dim, SIDE - 1)
            to_low, to_high = grid.exchanged(
                low.astype(jnp.bfloat16), high.astype(jnp.bfloat16), dim
            )
            partial = with_ends(
                partial,
                dim,
                None if step == steps - 1 else low + to_low.astype(jnp.float32),
                high + to_high.astype(jnp.float32),
            )
        following = coeffs[0] * (partial - centre * current.astype(jnp.float32)) - coeffs[
            1
        ] * older.astype(jnp.float32)
        following = jnp.where(inside, following, 0.0).astype(jnp.bfloat16)
        older = current
        current = following
    filtered = current[1:, 1:, 1:].reshape(owned_rows, columns)
    partial_intersection = jnp.einsum(
        "nl,ns->ls", locked, filtered, preferred_element_type=jnp.float32
    )
    return filtered, summed_everywhere(partial_intersection)


def solution(mesh):
    in_specs = (
        P(AXIS, None),
        P(AXIS, None, None),
        P(AXIS, None),
        P(AXIS),
        P(AXIS, None),
    )
    out_specs = (P(AXIS, None), P())
    return jax.shard_map(
        per_device, mesh=mesh, in_specs=in_specs, out_specs=out_specs, check_vma=False
    )
```

```python
import jax
import jax.numpy as jnp
from jax import lax
from jax.sharding import PartitionSpec as P

GRID_Y = 4
GRID_Z = 4
SIDE = 7
AXIS = "cells"

chebyshev_coeffs = ((-1.0 / 7.0, 0.0), (-7.0 / 41.0, 8.0 / 41.0), (-41.0 / 259.0, 28.0 / 259.0))
centre = 6.0


class Grid:
    def __init__(self):
        self.devices = lax.axis_size(AXIS)
        self.counts = (self.devices // (GRID_Y * GRID_Z), GRID_Y, GRID_Z)
        self.stride = (GRID_Y * GRID_Z, GRID_Z, 1)
        self.position = lax.axis_index(AXIS)
        self.coords = tuple(
            self.position // self.stride[d] % self.counts[d] for d in range(3)
        )

    def coord_of(self, device, dim):
        return device // self.stride[dim] % self.counts[dim]

    def swapped(self, low, high, dim, odd):
        by = self.stride[dim]
        pairs = []
        for i in range(self.devices):
            c = self.coord_of(i, dim)
            if c % 2 == odd and c + 1 < self.counts[dim]:
                pairs += [(i, i + by), (i + by, i)]
        lower = self.coords[dim] % 2 == odd
        arrived = lax.ppermute(jnp.where(lower, high, low), AXIS, pairs)
        zero = jnp.zeros_like(arrived)
        return jnp.where(lower, zero, arrived), jnp.where(lower, arrived, zero)

    def exchanged(self, low, high, dim):
        to_low, to_high = self.swapped(low, high, dim, 0)
        if self.counts[dim] > 2:
            more_low, more_high = self.swapped(low, high, dim, 1)
            to_low, to_high = to_low + more_low, to_high + more_high
        return to_low, to_high

    def partner(self, value, bit):
        return lax.ppermute(value, AXIS, [(i, i ^ bit) for i in range(self.devices)])

    def has(self, bit):
        return (self.position & bit) != 0


def line_bits():
    bit = GRID_Z // 2
    while bit:
        yield bit
        bit //= 2


def lines_gathered(grid, value):
    held = value[None]
    order = [0]
    for bit in line_bits():
        other = grid.partner(held, bit)
        mine = grid.has(bit)
        held = jnp.concatenate(
            [jnp.where(mine, other, held), jnp.where(mine, held, other)], axis=0
        )
        order = order + [i | bit for i in order]
    return [held[order.index(i)] for i in range(GRID_Z)]


def lines_transposed(grid, value):
    rows, columns = value.shape
    width = columns // GRID_Z
    blocks = [value[:, i * width : (i + 1) * width] for i in range(GRID_Z)]
    half = rows // 2
    for bit in line_bits():
        mine = grid.has(bit)
        lows = [i for i in range(GRID_Z) if not i & bit]
        away = [jnp.where(mine, blocks[i], blocks[i | bit]) for i in lows]
        packed = jnp.concatenate([b[h : h + half] for h in (0, half) for b in away], axis=1)
        arrived = grid.partner(packed, bit)
        for at, i in enumerate(lows):
            first = arrived[:, at * width : (at + 1) * width]
            second = arrived[:, (at + len(lows)) * width : (at + len(lows) + 1) * width]
            came = jnp.concatenate([first, second], axis=0)
            blocks[i], blocks[i | bit] = (
                jnp.where(mine, came, blocks[i]),
                jnp.where(mine, blocks[i | bit], came),
            )
    return jnp.concatenate(blocks, axis=1)


def plane(field, dim, at):
    return lax.slice_in_dim(field, at, at + 1, axis=dim)


def with_ends(field, dim, low, high):
    last = field.shape[dim] - 1
    parts = [
        plane(field, dim, 0) if low is None else low,
        lax.slice_in_dim(field, 1, last, axis=dim),
        plane(field, dim, last) if high is None else high,
    ]
    return jnp.concatenate(parts, axis=dim)


def to_next_partition(value, width):
    kept = value[..., :-width]
    return jnp.concatenate([jnp.zeros_like(value[..., :width]), kept], axis=-1)


def to_previous_partition(value, width):
    kept = value[..., width:]
    return jnp.concatenate([kept, jnp.zeros_like(value[..., :width])], axis=-1)


def slots_matrix(cell_matrix, connectivity, slot_count):
    total = None
    for c in range(cell_matrix.shape[0]):
        chosen = (
            connectivity[c][:, None] == jnp.arange(slot_count, dtype=jnp.int32)[None, :]
        ).astype(jnp.bfloat16)
        rows = lax.dot_general(
            chosen, cell_matrix[c], (((0,), (0,)), ((), ())), preferred_element_type=jnp.float32
        ).astype(jnp.bfloat16)
        both = jnp.dot(rows, chosen, preferred_element_type=jnp.float32)
        total = both if total is None else total + both
    return total.astype(jnp.bfloat16)


def rounded(value):
    return lax.reduce_precision(value, 8, 7).astype(jnp.bfloat16)


def summed_over_lines(grid, value):
    left = grid.devices // GRID_Z
    stride = GRID_Z
    factor = 2
    while left > 1:
        while left % factor:
            factor += 1
        at = grid.position // stride % factor
        terms = [value]
        for turn in range(1, factor):
            pairs = []
            for i in range(grid.devices):
                c = i // stride % factor
                pairs.append((i, i + ((c + turn) % factor - c) * stride))
            terms.append(lax.ppermute(value, AXIS, pairs))
        if factor == 2:
            total = terms[0].astype(jnp.float32) + terms[1].astype(jnp.float32)
        else:
            total = 0.0
            for k in range(factor):
                term = terms[0]
                for turn in range(1, factor):
                    term = jnp.where((at - turn) % factor == k, terms[turn], term)
                total = total + term.astype(jnp.float32)
        value = total.astype(jnp.bfloat16)
        left //= factor
        stride *= factor
    return value


def per_device(block, cell_matrix, connectivity, potential, locked):
    owned_rows, columns = block.shape
    slot_count = potential.shape[0]
    width = columns // GRID_Z
    edge = SIDE - 1
    grid = Grid()
    shape = (SIDE, SIDE, SIDE, columns)

    matrix = slots_matrix(cell_matrix, connectivity, slot_count)
    coarse = rounded(potential)
    fine = rounded(potential - coarse.astype(jnp.float32))
    matrix = jnp.concatenate([matrix, coarse[:, None], fine[:, None]], axis=1)
    matrices = lines_gathered(grid, matrix)
    lane_owner = lax.broadcasted_iota(jnp.int32, (1, columns), 1) // width
    lumped = jnp.zeros((slot_count, columns), jnp.float32)
    for p in range(GRID_Z):
        both = jnp.sum(matrices[p][:, slot_count:].astype(jnp.float32), axis=1, keepdims=True)
        lumped = jnp.where(lane_owner == p, both, lumped)

    mine = lines_transposed(grid, block)
    field = (
        jnp.zeros(shape, jnp.bfloat16)
        .at[1:, 1:, 1:]
        .set(mine.reshape(edge, edge, edge, columns))
    )
    field = with_ends(field, 2, to_next_partition(plane(field, 2, SIDE - 1), width), None)
    for dim in (1, 0):
        high = plane(field, dim, SIDE - 1)
        field = with_ends(field, dim, grid.exchanged(high, high, dim)[0], None)

    inside = jnp.ones(shape, jnp.bool_)
    first = (grid.coords[0] == 0, grid.coords[1] == 0, lane_owner.reshape(1, 1, 1, columns) == 0)
    for dim in range(3):
        at = lax.broadcasted_iota(jnp.int32, shape, dim)
        inside = inside & ~((at == 0) & first[dim])

    older = field
    current = field
    steps = len(chebyshev_coeffs)
    for step, coeffs in enumerate(chebyshev_coeffs):
        rows = current.reshape(slot_count, columns)
        partial = lumped * rows.astype(jnp.float32)
        for p in range(GRID_Z):
            own = jnp.where(lane_owner == p, rows, jnp.zeros_like(rows))
            partial = partial + jnp.dot(
                matrices[p][:, :slot_count], own, preferred_element_type=jnp.float32
            )
        partial = partial.reshape(shape)
        low, high = plane(partial, 2, 0), plane(partial, 2, SIDE - 1)
        partial = with_ends(
            partial,
            2,
            low + to_next_partition(high, width),
            high + to_previous_partition(low, width),
        )
        for dim in (1, 0):
            low, high = plane(partial, dim, 0), plane(partial, dim, SIDE - 1)
            to_low, to_high = grid.exchanged(
                low.astype(jnp.bfloat16), high.astype(jnp.bfloat16), dim
            )
            partial = with_ends(
                partial,
                dim,
                None if step == steps - 1 else low + to_low.astype(jnp.float32),
                high + to_high.astype(jnp.float32),
            )
        following = coeffs[0] * (partial - centre * current.astype(jnp.float32)) - coeffs[
            1
        ] * older.astype(jnp.float32)
        following = rounded(jnp.where(inside, following, 0.0))
        older = current
        current = following
        if step == 0:
            locked, current = lax.optimization_barrier((locked, current))
            all_locked = lines_gathered(grid, locked)
    filtered = current[1:, 1:, 1:].reshape(owned_rows, columns)

    share = jnp.zeros((width, locked.shape[1]), jnp.float32)
    for p in range(GRID_Z):
        share = share + lax.dot_general(
            filtered[:, p * width : (p + 1) * width],
            all_locked[p],
            (((0,), (0,)), ((), ())),
            preferred_element_type=jnp.float32,
        )
    share = summed_over_lines(grid, share.astype(jnp.bfloat16))
    intersection = jnp.concatenate(lines_gathered(grid, share)).T.astype(jnp.float32)
    return lines_transposed(grid, filtered), intersection


def solution(mesh):
    in_specs = (
        P(AXIS, None),
        P(AXIS, None, None),
        P(AXIS, None),
        P(AXIS),
        P(AXIS, None),
    )
    out_specs = (P(AXIS, None), P())
    return jax.shard_map(
        per_device, mesh=mesh, in_specs=in_specs, out_specs=out_specs, check_vma=False
    )
```

```python
import jax
import jax.numpy as jnp
from jax import lax
from jax.sharding import PartitionSpec as P

GRID_Y = 4
GRID_Z = 4
SIDE = 7
AXIS = "cells"

chebyshev_coeffs = ((-1.0 / 7.0, 0.0), (-7.0 / 41.0, 8.0 / 41.0), (-41.0 / 259.0, 28.0 / 259.0))
centre = 6.0


class Grid:
    def __init__(self):
        self.devices = lax.axis_size(AXIS)
        self.counts = (self.devices // (GRID_Y * GRID_Z), GRID_Y, GRID_Z)
        self.stride = (GRID_Y * GRID_Z, GRID_Z, 1)
        self.position = lax.axis_index(AXIS)
        self.coords = tuple(
            self.position // self.stride[d] % self.counts[d] for d in range(3)
        )

    def coord_of(self, device, dim):
        return device // self.stride[dim] % self.counts[dim]

    def swapped(self, low, high, dim, odd):
        by = self.stride[dim]
        pairs = []
        for i in range(self.devices):
            c = self.coord_of(i, dim)
            if c % 2 == odd and c + 1 < self.counts[dim]:
                pairs += [(i, i + by), (i + by, i)]
        lower = self.coords[dim] % 2 == odd
        arrived = lax.ppermute(jnp.where(lower, high, low), AXIS, pairs)
        zero = jnp.zeros_like(arrived)
        return jnp.where(lower, zero, arrived), jnp.where(lower, arrived, zero)

    def exchanged(self, low, high, dim):
        to_low, to_high = self.swapped(low, high, dim, 0)
        if self.counts[dim] > 2:
            more_low, more_high = self.swapped(low, high, dim, 1)
            to_low, to_high = to_low + more_low, to_high + more_high
        return to_low, to_high

    def partner(self, value, bit):
        return lax.ppermute(value, AXIS, [(i, i ^ bit) for i in range(self.devices)])

    def has(self, bit):
        return (self.position & bit) != 0


def line_bits():
    bit = GRID_Z // 2
    while bit:
        yield bit
        bit //= 2


def lines_gathered(grid, value):
    held = value[None]
    order = [0]
    for bit in line_bits():
        other = grid.partner(held, bit)
        mine = grid.has(bit)
        held = jnp.concatenate(
            [jnp.where(mine, other, held), jnp.where(mine, held, other)], axis=0
        )
        order = order + [i | bit for i in order]
    return [held[order.index(i)] for i in range(GRID_Z)]


class Shares:
    def __init__(self, grid, value):
        self.grid = grid
        self.width = value.shape[1] // GRID_Z
        self.half = value.shape[0] // 2
        self.blocks = [
            value[:, i * self.width : (i + 1) * self.width] for i in range(GRID_Z)
        ]

    def packed(self, bit):
        mine = self.grid.has(bit)
        away = [
            jnp.where(mine, self.blocks[i], self.blocks[i | bit])
            for i in range(GRID_Z)
            if not i & bit
        ]
        return jnp.concatenate(
            [b[h : h + self.half] for h in (0, self.half) for b in away], axis=1
        )

    def take(self, bit, arrived):
        mine = self.grid.has(bit)
        lows = [i for i in range(GRID_Z) if not i & bit]
        for at, i in enumerate(lows):
            ends = (at * self.width, (at + len(lows)) * self.width)
            came = jnp.concatenate([arrived[:, e : e + self.width] for e in ends], axis=0)
            self.blocks[i], self.blocks[i | bit] = (
                jnp.where(mine, came, self.blocks[i]),
                jnp.where(mine, self.blocks[i | bit], came),
            )

    def value(self):
        return jnp.concatenate(self.blocks, axis=1)


def plane(field, dim, at):
    return lax.slice_in_dim(field, at, at + 1, axis=dim)


def with_ends(field, dim, low, high):
    last = field.shape[dim] - 1
    parts = [
        plane(field, dim, 0) if low is None else low,
        lax.slice_in_dim(field, 1, last, axis=dim),
        plane(field, dim, last) if high is None else high,
    ]
    return jnp.concatenate(parts, axis=dim)


def to_next_partition(value, width):
    kept = value[..., :-width]
    return jnp.concatenate([jnp.zeros_like(value[..., :width]), kept], axis=-1)


def to_previous_partition(value, width):
    kept = value[..., width:]
    return jnp.concatenate([kept, jnp.zeros_like(value[..., :width])], axis=-1)


def slots_matrix(cell_matrix, connectivity, slot_count):
    total = None
    for c in range(cell_matrix.shape[0]):
        chosen = (
            connectivity[c][:, None] == jnp.arange(slot_count, dtype=jnp.int32)[None, :]
        ).astype(jnp.bfloat16)
        rows = lax.dot_general(
            chosen, cell_matrix[c], (((0,), (0,)), ((), ())), preferred_element_type=jnp.float32
        ).astype(jnp.bfloat16)
        both = jnp.dot(rows, chosen, preferred_element_type=jnp.float32)
        total = both if total is None else total + both
    return total.astype(jnp.bfloat16)


def rounded(value):
    return lax.reduce_precision(value, 8, 7).astype(jnp.bfloat16)


def plus(first, second):
    return (first.astype(jnp.float32) + second.astype(jnp.float32)).astype(jnp.bfloat16)


def summed_along(grid, value, stride, count):
    factor = 2
    while count > 1:
        while count % factor:
            factor += 1
        at = grid.position // stride % factor
        terms = [value]
        for turn in range(1, factor):
            pairs = []
            for i in range(grid.devices):
                c = i // stride % factor
                pairs.append((i, i + ((c + turn) % factor - c) * stride))
            terms.append(lax.ppermute(value, AXIS, pairs))
        if factor == 2:
            value = plus(*terms)
        else:
            total = 0.0
            for k in range(factor):
                term = terms[0]
                for turn in range(1, factor):
                    term = jnp.where((at - turn) % factor == k, terms[turn], term)
                total = total + term.astype(jnp.float32)
            value = total.astype(jnp.bfloat16)
        count //= factor
        stride *= factor
    return value


def per_device(block, cell_matrix, connectivity, potential, locked):
    owned_rows, columns = block.shape
    slot_count = potential.shape[0]
    width = columns // GRID_Z
    edge = SIDE - 1
    grid = Grid()
    shape = (SIDE, SIDE, SIDE, columns)

    matrix = slots_matrix(cell_matrix, connectivity, slot_count)
    coarse = rounded(potential)
    fine = rounded(potential - coarse.astype(jnp.float32))
    matrix = jnp.concatenate([matrix, coarse[:, None], fine[:, None]], axis=1)
    matrices = lines_gathered(grid, matrix)
    lane_owner = lax.broadcasted_iota(jnp.int32, (1, columns), 1) // width
    lumped = jnp.zeros((slot_count, columns), jnp.float32)
    for p in range(GRID_Z):
        both = jnp.sum(matrices[p][:, slot_count:].astype(jnp.float32), axis=1, keepdims=True)
        lumped = jnp.where(lane_owner == p, both, lumped)

    shares = Shares(grid, block)
    for bit in line_bits():
        shares.take(bit, grid.partner(shares.packed(bit), bit))
    field = (
        jnp.zeros(shape, jnp.bfloat16)
        .at[1:, 1:, 1:]
        .set(shares.value().reshape(edge, edge, edge, columns))
    )
    field = with_ends(field, 2, to_next_partition(plane(field, 2, SIDE - 1), width), None)
    for dim in (1, 0):
        high = plane(field, dim, SIDE - 1)
        field = with_ends(field, dim, grid.exchanged(high, high, dim)[0], None)

    inside = jnp.ones(shape, jnp.bool_)
    first = (grid.coords[0] == 0, grid.coords[1] == 0, lane_owner.reshape(1, 1, 1, columns) == 0)
    for dim in range(3):
        at = lax.broadcasted_iota(jnp.int32, shape, dim)
        inside = inside & ~((at == 0) & first[dim])

    locked, field = lax.optimization_barrier((locked, field))
    above = locked[-edge * edge :]
    below = grid.exchanged(above, above, 0)[0]
    locked = jnp.concatenate([below, locked], axis=0)

    older = field
    current = field
    steps = len(chebyshev_coeffs)
    for step, coeffs in enumerate(chebyshev_coeffs):
        rows = current.reshape(slot_count, columns)
        partial = lumped * rows.astype(jnp.float32)
        for p in range(GRID_Z):
            own = jnp.where(lane_owner == p, rows, jnp.zeros_like(rows))
            partial = partial + jnp.dot(
                matrices[p][:, :slot_count], own, preferred_element_type=jnp.float32
            )
        partial = partial.reshape(shape)
        low, high = plane(partial, 2, 0), plane(partial, 2, SIDE - 1)
        partial = with_ends(
            partial,
            2,
            low + to_next_partition(high, width),
            high + to_previous_partition(low, width),
        )
        if step == 0:
            locked, partial = lax.optimization_barrier((locked, partial))
            all_locked = lines_gathered(grid, locked)
        if step == steps - 1:
            break
        for dim in (1, 0):
            low, high = plane(partial, dim, 0), plane(partial, dim, SIDE - 1)
            to_low, to_high = grid.exchanged(
                low.astype(jnp.bfloat16), high.astype(jnp.bfloat16), dim
            )
            partial = with_ends(
                partial,
                dim,
                low + to_low.astype(jnp.float32),
                high + to_high.astype(jnp.float32),
            )
        following = coeffs[0] * (partial - centre * current.astype(jnp.float32)) - coeffs[
            1
        ] * older.astype(jnp.float32)
        following = rounded(jnp.where(inside, following, 0.0))
        older = current
        current = following
        if step == 1:
            current, all_locked = lax.optimization_barrier((current, all_locked))

    low = plane(partial, 1, 0).astype(jnp.bfloat16)
    to_high = grid.exchanged(low, low, 1)[1].astype(jnp.float32)
    partial = with_ends(partial, 1, None, plane(partial, 1, SIDE - 1) + to_high)
    partial = coeffs[0] * partial[:, 1:, 1:].reshape(SIDE, edge * edge, columns)

    def owned(field):
        return field[1:, 1:, 1:].reshape(edge, edge * edge, columns).astype(jnp.float32)

    rest = -coeffs[0] * centre * owned(current) - coeffs[1] * owned(older)
    sums = jnp.concatenate([partial[:1], partial[1:] + rest], axis=0)
    weights = sums.astype(jnp.bfloat16).reshape(SIDE * edge * edge, columns)
    share = 0.0
    for p in range(GRID_Z):
        share = share + lax.dot_general(
            all_locked[p],
            weights[:, p * width : (p + 1) * width],
            (((0,), (0,)), ((), ())),
            preferred_element_type=jnp.float32,
        )
    deep = share.shape[0] // GRID_Z
    share = jnp.concatenate(
        [share[i * deep : (i + 1) * deep] for i in range(GRID_Z)], axis=1
    ).astype(jnp.bfloat16)

    low = sums[0].astype(jnp.bfloat16)
    stride, count = grid.stride[0], grid.counts[0]
    even = grid.coords[0] % 2 == 0
    arrived = grid.partner(jnp.concatenate([share, low], axis=0), stride)
    share = plus(share, arrived[:deep])
    to_high = jnp.where(even, arrived[deep:], jnp.zeros_like(low))
    if count > 2:
        to_high = to_high + grid.swapped(low, low, 0, 1)[1]
    sums = jnp.concatenate(
        [sums[1:edge], sums[edge:] + to_high[None].astype(jnp.float32)], axis=0
    )
    filtered = rounded(sums.reshape(owned_rows, columns))

    share = summed_along(grid, share, grid.stride[1], grid.counts[1])
    share = summed_along(grid, share, stride * 2, count // 2)

    shares = Shares(grid, filtered)
    held = share[None]
    order = [0]
    for bit in line_bits():
        mine = grid.has(bit)
        sent = held.reshape(-1, columns)
        arrived = grid.partner(jnp.concatenate([sent, shares.packed(bit)], axis=0), bit)
        shares.take(bit, arrived[sent.shape[0] :])
        other = arrived[: sent.shape[0]].reshape(held.shape)
        held = jnp.concatenate(
            [jnp.where(mine, other, held), jnp.where(mine, held, other)], axis=0
        )
        order = order + [i | bit for i in order]
    held = [held[order.index(i)] for i in range(GRID_Z)]
    intersection = jnp.concatenate(
        [
            jnp.concatenate([h[:, q * width : (q + 1) * width] for h in held], axis=1)
            for q in range(GRID_Z)
        ],
        axis=0,
    ).astype(jnp.float32)
    return shares.value(), intersection


def solution(mesh):
    in_specs = (
        P(AXIS, None),
        P(AXIS, None, None),
        P(AXIS, None),
        P(AXIS),
        P(AXIS, None),
    )
    out_specs = (P(AXIS, None), P())
    return jax.shard_map(
        per_device, mesh=mesh, in_specs=in_specs, out_specs=out_specs, check_vma=False
    )
```

```python
import jax
import jax.numpy as jnp
from jax import lax
from jax.experimental.layout import Layout, with_layout_constraint
from jax.sharding import PartitionSpec as P

GRID_Y = 4
GRID_Z = 4
SIDE = 7
AXIS = "cells"

chebyshev_coeffs = ((-1.0 / 7.0, 0.0), (-7.0 / 41.0, 8.0 / 41.0), (-41.0 / 259.0, 28.0 / 259.0))
centre = 6.0

PAIRS = GRID_Z // 2


class Grid:
    def __init__(self):
        self.devices = lax.axis_size(AXIS)
        self.counts = (self.devices // (GRID_Y * GRID_Z), GRID_Y, GRID_Z)
        self.stride = (GRID_Y * GRID_Z, GRID_Z, 1)
        self.leaders = range(1, self.devices, 2)
        self.position = lax.axis_index(AXIS)
        self.coords = tuple(
            self.position // self.stride[d] % self.counts[d] for d in range(3)
        )

    def coord_of(self, device, dim):
        return device // self.stride[dim] % self.counts[dim]

    def swapped(self, low, high, dim, odd, everyone=False):
        by = self.stride[dim]
        pairs = []
        for i in range(self.devices) if everyone else self.leaders:
            c = self.coord_of(i, dim)
            if c % 2 == odd and c + 1 < self.counts[dim]:
                pairs += [(i, i + by), (i + by, i)]
        lower = self.coords[dim] % 2 == odd
        arrived = lax.ppermute(jnp.where(lower, high, low), AXIS, pairs)
        zero = jnp.zeros_like(arrived)
        return jnp.where(lower, zero, arrived), jnp.where(lower, arrived, zero)

    def exchanged(self, low, high, dim, everyone=False):
        to_low, to_high = self.swapped(low, high, dim, 0, everyone)
        if self.counts[dim] > 2:
            more_low, more_high = self.swapped(low, high, dim, 1, everyone)
            to_low, to_high = to_low + more_low, to_high + more_high
        return to_low, to_high

    def partner(self, value, bit):
        among = range(self.devices) if bit == 1 else self.leaders
        return lax.ppermute(value, AXIS, [(i, i ^ bit) for i in among])

    def has(self, bit):
        return (self.position & bit) != 0


def line_bits():
    bit = 2
    while bit < GRID_Z:
        yield bit
        bit *= 2


def joined(grid, value, bit):
    other = grid.partner(value, bit)
    mine = grid.has(bit)
    return jnp.stack([jnp.where(mine, other, value), jnp.where(mine, value, other)])


def lines_gathered(grid, value):
    held = joined(grid, value, 1)
    for bit in line_bits():
        held = joined(grid, held, bit).reshape((-1,) + value.shape)
    return [held[i] for i in range(GRID_Z)]


class Shares:
    def __init__(self, grid, blocks):
        self.grid = grid
        self.blocks = blocks

    def away(self, bit):
        mine = self.grid.has(bit)
        b = bit // 2
        return jnp.concatenate(
            [
                jnp.where(mine, self.blocks[i], self.blocks[i | b])
                for i in range(PAIRS)
                if not i & b
            ],
            axis=0,
        )

    def take(self, bit, arrived):
        mine = self.grid.has(bit)
        b = bit // 2
        rows = self.blocks[0].shape[0]
        lows = [i for i in range(PAIRS) if not i & b]
        for at, i in enumerate(lows):
            came = arrived[at * rows : (at + 1) * rows]
            self.blocks[i], self.blocks[i | b] = (
                jnp.where(mine, came, self.blocks[i]),
                jnp.where(mine, self.blocks[i | b], came),
            )


def by_rows(value):
    return with_layout_constraint(value, Layout(major_to_minor=tuple(range(value.ndim))))


def plane(field, dim, at):
    return lax.slice_in_dim(field, at, at + 1, axis=dim)


def with_ends(field, dim, low, high):
    last = field.shape[dim] - 1
    parts = [
        plane(field, dim, 0) if low is None else low,
        lax.slice_in_dim(field, 1, last, axis=dim),
        plane(field, dim, last) if high is None else high,
    ]
    return jnp.concatenate(parts, axis=dim)


def to_next_partition(value, width):
    kept = value[..., :-width]
    return jnp.concatenate([jnp.zeros_like(value[..., :width]), kept], axis=-1)


def to_previous_partition(value, width):
    kept = value[..., width:]
    return jnp.concatenate([kept, jnp.zeros_like(value[..., :width])], axis=-1)


def slots_matrix(cell_matrix, connectivity, slot_count):
    total = None
    for c in range(cell_matrix.shape[0]):
        chosen = (
            connectivity[c][:, None] == jnp.arange(slot_count, dtype=jnp.int32)[None, :]
        ).astype(jnp.bfloat16)
        rows = lax.dot_general(
            chosen, cell_matrix[c], (((0,), (0,)), ((), ())), preferred_element_type=jnp.float32
        ).astype(jnp.bfloat16)
        both = jnp.dot(rows, chosen, preferred_element_type=jnp.float32)
        total = both if total is None else total + both
    return total.astype(jnp.bfloat16)


def rounded(value):
    return lax.reduce_precision(value, 8, 7).astype(jnp.bfloat16)


def plus(first, second):
    return (first.astype(jnp.float32) + second.astype(jnp.float32)).astype(jnp.bfloat16)


def summed_along(grid, value, stride, count):
    factor = 2
    while count > 1:
        while count % factor:
            factor += 1
        at = grid.position // stride % factor
        terms = [value]
        for turn in range(1, factor):
            pairs = []
            for i in grid.leaders:
                c = i // stride % factor
                pairs.append((i, i + ((c + turn) % factor - c) * stride))
            terms.append(lax.ppermute(value, AXIS, pairs))
        if factor == 2:
            value = plus(*terms)
        else:
            total = 0.0
            for k in range(factor):
                term = terms[0]
                for turn in range(1, factor):
                    term = jnp.where((at - turn) % factor == k, terms[turn], term)
                total = total + term.astype(jnp.float32)
            value = total.astype(jnp.bfloat16)
        count //= factor
        stride *= factor
    return value


def per_device(block, cell_matrix, connectivity, potential, locked):
    owned_rows, columns = block.shape
    slot_count = potential.shape[0]
    width = columns // PAIRS
    lanes = width * GRID_Z
    edge = SIDE - 1
    grid = Grid()
    shape = (SIDE, SIDE, SIDE, lanes)

    matrix = slots_matrix(cell_matrix, connectivity, slot_count)
    coarse = rounded(potential)
    fine = rounded(potential - coarse.astype(jnp.float32))
    matrix = jnp.concatenate([matrix, coarse[:, None], fine[:, None]], axis=1)
    matrices = lines_gathered(grid, matrix)
    lane_owner = lax.broadcasted_iota(jnp.int32, (1, lanes), 1) // width
    lumped = jnp.zeros((slot_count, lanes), jnp.float32)
    for p in range(GRID_Z):
        both = jnp.sum(matrices[p][:, slot_count:].astype(jnp.float32), axis=1, keepdims=True)
        lumped = jnp.where(lane_owner == p, both, lumped)

    blocks = joined(grid, block, 1)
    shares = Shares(
        grid,
        [
            jnp.concatenate([b[:, i * width : (i + 1) * width] for b in blocks], axis=1)
            for i in range(PAIRS)
        ],
    )
    for bit in line_bits():
        shares.take(bit, grid.partner(shares.away(bit), bit))
    mine = jnp.concatenate(shares.blocks, axis=1)
    field = (
        jnp.zeros(shape, jnp.bfloat16)
        .at[1:, 1:, 1:]
        .set(mine.reshape(edge, edge, edge, lanes))
    )
    field = with_ends(field, 2, to_next_partition(plane(field, 2, SIDE - 1), width), None)
    for dim in (1, 0):
        high = plane(field, dim, SIDE - 1)
        field = with_ends(field, dim, grid.exchanged(high, high, dim)[0], None)

    inside = jnp.ones(shape, jnp.bool_)
    first = (grid.coords[0] == 0, grid.coords[1] == 0, lane_owner.reshape(1, 1, 1, lanes) == 0)
    for dim in range(3):
        at = lax.broadcasted_iota(jnp.int32, shape, dim)
        inside = inside & ~((at == 0) & first[dim])

    locked, field = lax.optimization_barrier((locked, field))
    above = by_rows(locked[-edge * edge :])
    below = by_rows(grid.exchanged(above, above, 0, True)[0])
    locked = jnp.concatenate([below, locked], axis=0)

    older = field
    current = field
    steps = len(chebyshev_coeffs)
    for step, coeffs in enumerate(chebyshev_coeffs):
        rows = current.reshape(slot_count, lanes)
        partial = lumped * rows.astype(jnp.float32)
        for p in range(GRID_Z):
            own = jnp.where(lane_owner == p, rows, jnp.zeros_like(rows))
            partial = partial + jnp.dot(
                matrices[p][:, :slot_count], own, preferred_element_type=jnp.float32
            )
        partial = partial.reshape(shape)
        low, high = plane(partial, 2, 0), plane(partial, 2, SIDE - 1)
        partial = with_ends(
            partial,
            2,
            low + to_next_partition(high, width),
            high + to_previous_partition(low, width),
        )
        if step == 0:
            locked, partial = lax.optimization_barrier((locked, partial))
            all_locked = lines_gathered(grid, locked)
        if step == steps - 1:
            break
        for dim in (1, 0):
            low, high = plane(partial, dim, 0), plane(partial, dim, SIDE - 1)
            to_low, to_high = grid.exchanged(
                low.astype(jnp.bfloat16), high.astype(jnp.bfloat16), dim
            )
            partial = with_ends(
                partial,
                dim,
                low + to_low.astype(jnp.float32),
                high + to_high.astype(jnp.float32),
            )
        following = coeffs[0] * (partial - centre * current.astype(jnp.float32)) - coeffs[
            1
        ] * older.astype(jnp.float32)
        following = rounded(jnp.where(inside, following, 0.0))
        older = current
        current = following
        if step == 1:
            current, all_locked = lax.optimization_barrier((current, all_locked))

    low = plane(partial, 1, 0).astype(jnp.bfloat16)
    to_high = grid.exchanged(low, low, 1)[1].astype(jnp.float32)
    partial = with_ends(partial, 1, None, plane(partial, 1, SIDE - 1) + to_high)
    partial = coeffs[0] * partial[:, 1:, 1:].reshape(SIDE, edge * edge, lanes)

    def owned(field):
        return field[1:, 1:, 1:].reshape(edge, edge * edge, lanes).astype(jnp.float32)

    rest = -coeffs[0] * centre * owned(current) - coeffs[1] * owned(older)
    sums = jnp.concatenate([partial[:1], partial[1:] + rest], axis=0)
    weights = sums.astype(jnp.bfloat16).reshape(SIDE * edge * edge, lanes)
    share = 0.0
    for p in range(GRID_Z):
        share = share + lax.dot_general(
            all_locked[p],
            weights[:, p * width : (p + 1) * width],
            (((0,), (0,)), ((), ())),
            preferred_element_type=jnp.float32,
        )
    deep = share.shape[0] // PAIRS
    share = jnp.concatenate(
        [share[i * deep : (i + 1) * deep] for i in range(PAIRS)], axis=1
    ).astype(jnp.bfloat16)

    def folded(value):
        return jnp.concatenate(
            [value[:, i : i + columns] for i in range(0, lanes, columns)], axis=0
        )

    low = folded(sums[0].astype(jnp.bfloat16))
    stride, count = grid.stride[0], grid.counts[0]
    even = grid.coords[0] % 2 == 0
    arrived = grid.partner(jnp.concatenate([share, low], axis=0), stride)
    share = plus(share, arrived[:deep])
    to_high = jnp.where(even, arrived[deep:], jnp.zeros_like(low))
    if count > 2:
        to_high = to_high + grid.swapped(low, low, 0, 1)[1]
    to_high = to_high.reshape(lanes // columns, edge * edge, columns)
    to_high = jnp.concatenate(list(to_high), axis=1)
    sums = jnp.concatenate(
        [sums[1:edge], sums[edge:] + to_high[None].astype(jnp.float32)], axis=0
    )
    filtered = rounded(sums.reshape(owned_rows, lanes))

    share = summed_along(grid, share, grid.stride[1], grid.counts[1])
    share = summed_along(grid, share, stride * 2, count // 2)

    shares = Shares(
        grid, [filtered[:, i : i + 2 * width] for i in range(0, lanes, 2 * width)]
    )
    held = share[None]
    for bit in line_bits():
        mine = grid.has(bit)
        sent = held.reshape(-1, columns)
        arrived = grid.partner(jnp.concatenate([sent, shares.away(bit)], axis=0), bit)
        shares.take(bit, arrived[sent.shape[0] :])
        other = arrived[: sent.shape[0]].reshape(held.shape)
        held = jnp.concatenate(
            [jnp.where(mine, other, held), jnp.where(mine, held, other)], axis=0
        )
    first, second = (
        jnp.concatenate([b[:, i : i + width] for b in shares.blocks], axis=1)
        for i in (0, width)
    )
    sent = jnp.concatenate([held.reshape(-1, columns), first], axis=0)
    arrived = grid.partner(sent, 1)
    leader = grid.has(1)
    held = jnp.where(leader, held, arrived[:-owned_rows].reshape(held.shape))
    filtered = jnp.where(leader, second, arrived[-owned_rows:])
    intersection = jnp.concatenate(
        [
            jnp.concatenate([h[:, q * width : (q + 1) * width] for h in held], axis=1)
            for q in range(PAIRS)
        ],
        axis=0,
    ).astype(jnp.float32)
    return filtered, intersection


def solution(mesh):
    in_specs = (
        P(AXIS, None),
        P(AXIS, None, None),
        P(AXIS, None),
        P(AXIS),
        P(AXIS, None),
    )
    out_specs = (P(AXIS, None), P())
    return jax.shard_map(
        per_device, mesh=mesh, in_specs=in_specs, out_specs=out_specs, check_vma=False
    )
```

```python
import jax
import jax.numpy as jnp
from jax import lax
from jax.experimental.layout import Layout, with_layout_constraint
from jax.sharding import PartitionSpec as P

GRID_Y = 4
GRID_Z = 4
SIDE = 7
AXIS = "cells"

chebyshev_coeffs = ((-1.0 / 7.0, 0.0), (-7.0 / 41.0, 8.0 / 41.0), (-41.0 / 259.0, 28.0 / 259.0))
centre = 6.0


class Grid:
    def __init__(self):
        self.devices = lax.axis_size(AXIS)
        self.counts = (self.devices // (GRID_Y * GRID_Z), GRID_Y, GRID_Z)
        self.stride = (GRID_Y * GRID_Z, GRID_Z, 1)
        self.position = lax.axis_index(AXIS)
        self.coords = tuple(
            self.position // self.stride[d] % self.counts[d] for d in range(3)
        )

        flips = self.coords[0] + self.coords[1] + self.coords[2] // 2 + self.coords[2]
        self.share_low = flips % 2 == 1

    def coord_of(self, device, dim):
        return device // self.stride[dim] % self.counts[dim]

    def swapped(self, low, high, dim, odd, raw=False, cross=1):
        count = self.counts[dim]
        pairs = []
        for i in range(self.devices):
            c = self.coord_of(i, dim)
            up = c % 2 == odd
            to = (c + (1 if up else -1)) % count
            pairs.append((i, (i + (to - c) * self.stride[dim]) ^ cross))
        lower = self.coords[dim] % 2 == odd
        arrived = lax.ppermute(jnp.where(lower, high, low), AXIS, pairs)
        if raw:
            return arrived
        zero = jnp.zeros_like(arrived)
        to_low, to_high = jnp.where(lower, zero, arrived), jnp.where(lower, arrived, zero)
        if odd or count % 2:
            to_low = jnp.where(self.coords[dim] > 0, to_low, zero)
            to_high = jnp.where(self.coords[dim] < count - 1, to_high, zero)
        return to_low, to_high

    def exchanged(self, low, high, dim, cross=1):
        to_low, to_high = self.swapped(low, high, dim, 0, cross=cross)
        if self.counts[dim] > 2:
            more_low, more_high = self.swapped(low, high, dim, 1, cross=cross)
            to_low, to_high = to_low + more_low, to_high + more_high
        return to_low, to_high

    def partner(self, value, bits):
        return lax.ppermute(value, AXIS, [(i, i ^ bits) for i in range(self.devices)])

    def has(self, bit):
        return (self.position & bit) != 0


FIRST, SECOND = 3, 1


def placed(near, high, low):
    near = [
        jnp.where(low, near[i ^ 1], near[i]) for i in range(GRID_Z)
    ]
    return [jnp.where(high, near[i ^ 2], near[i]) for i in range(GRID_Z)]


def lines_gathered(grid, value):
    other = grid.partner(value, FIRST)
    both = grid.partner(jnp.stack([value, other]), SECOND)
    return [value, both[0], both[1], other]


def packed(blocks):
    half = blocks[0].shape[0] // 2
    return jnp.concatenate([b[h : h + half] for h in (0, half) for b in blocks], axis=1)


def unpacked(value, width):
    return [
        jnp.concatenate([value[:, e : e + width] for e in (i * width, (i + 2) * width)], axis=0)
        for i in range(2)
    ]


def split(value, parts):
    width = value.shape[1] // parts
    return [value[:, i * width : (i + 1) * width] for i in range(parts)]


def to_shares(grid, block):
    shares = split(block, GRID_Z)
    width = shares[0].shape[1]
    high = grid.has(2)
    kept = [jnp.where(high, shares[2 + i], shares[i]) for i in range(2)]
    away = [jnp.where(high, shares[i], shares[2 + i]) for i in range(2)]
    came = unpacked(grid.partner(packed(away), FIRST), width)
    low = grid.share_low
    own = [jnp.where(low, kept[1], kept[0]), jnp.where(low, came[1], came[0])]
    away = [jnp.where(low, kept[0], kept[1]), jnp.where(low, came[0], came[1])]
    came = unpacked(grid.partner(packed(away), SECOND), width)
    near = [own[0], came[0], came[1], own[1]]
    return jnp.concatenate(placed(near, high, grid.has(1)), axis=1)


def by_rows(value):
    return with_layout_constraint(value, Layout(major_to_minor=tuple(range(value.ndim))))


def plane(field, dim, at):
    return lax.slice_in_dim(field, at, at + 1, axis=dim)


def with_ends(field, dim, low, high):
    last = field.shape[dim] - 1
    parts = [
        plane(field, dim, 0) if low is None else low,
        lax.slice_in_dim(field, 1, last, axis=dim),
        plane(field, dim, last) if high is None else high,
    ]
    return jnp.concatenate(parts, axis=dim)


def to_next_partition(value, width):
    kept = value[..., :-width]
    return jnp.concatenate([jnp.zeros_like(value[..., :width]), kept], axis=-1)


def to_previous_partition(value, width):
    kept = value[..., width:]
    return jnp.concatenate([kept, jnp.zeros_like(value[..., :width])], axis=-1)


def slots_matrix(cell_matrix, connectivity, slot_count):
    total = None
    for c in range(cell_matrix.shape[0]):
        chosen = (
            connectivity[c][:, None] == jnp.arange(slot_count, dtype=jnp.int32)[None, :]
        ).astype(jnp.bfloat16)
        rows = lax.dot_general(
            chosen, cell_matrix[c], (((0,), (0,)), ((), ())), preferred_element_type=jnp.float32
        ).astype(jnp.bfloat16)
        both = jnp.dot(rows, chosen, preferred_element_type=jnp.float32)
        total = both if total is None else total + both
    return total.astype(jnp.bfloat16)


def rounded(value):
    return lax.reduce_precision(value, 8, 7).astype(jnp.bfloat16)


def plus(first, second):
    return (first.astype(jnp.float32) + second.astype(jnp.float32)).astype(jnp.bfloat16)


def summed_along(grid, value, stride, count):
    factor = 2
    while count > 1:
        while count % factor:
            factor += 1
        at = grid.position // stride % factor
        terms = [value]
        for turn in range(1, factor):
            pairs = []
            for i in range(grid.devices):
                c = i // stride % factor
                pairs.append((i, i + ((c + turn) % factor - c) * stride))
            terms.append(lax.ppermute(value, AXIS, pairs))
        if factor == 2:
            value = plus(*terms)
        else:
            total = 0.0
            for k in range(factor):
                term = terms[0]
                for turn in range(1, factor):
                    term = jnp.where((at - turn) % factor == k, terms[turn], term)
                total = total + term.astype(jnp.float32)
            value = total.astype(jnp.bfloat16)
        count //= factor
        stride *= factor
    return value


def per_device(block, cell_matrix, connectivity, potential, locked):
    owned_rows, columns = block.shape
    slot_count = potential.shape[0]
    width = columns // GRID_Z
    edge = SIDE - 1
    grid = Grid()
    shape = (SIDE, SIDE, SIDE, columns)

    matrix = slots_matrix(cell_matrix, connectivity, slot_count)
    coarse = rounded(potential)
    fine = rounded(potential - coarse.astype(jnp.float32))
    matrix = jnp.concatenate([matrix, coarse[:, None], fine[:, None]], axis=1)
    matrices = lines_gathered(grid, matrix)
    lane_owner = lax.broadcasted_iota(jnp.int32, (1, columns), 1) // width
    owner_near = lane_owner ^ grid.coords[2]
    lumped = jnp.zeros((slot_count, columns), jnp.float32)
    for r in range(GRID_Z):
        both = jnp.sum(matrices[r][:, slot_count:].astype(jnp.float32), axis=1, keepdims=True)
        lumped = jnp.where(owner_near == r, both, lumped)

    mine = to_shares(grid, block)
    field = (
        jnp.zeros(shape, jnp.bfloat16)
        .at[1:, 1:, 1:]
        .set(mine.reshape(edge, edge, edge, columns))
    )
    field = with_ends(field, 2, to_next_partition(plane(field, 2, SIDE - 1), width), None)
    for dim in (1, 0):
        high = plane(field, dim, SIDE - 1)
        field = with_ends(field, dim, grid.exchanged(high, high, dim)[0], None)

    inside = jnp.ones(shape, jnp.bool_)
    first = (grid.coords[0] == 0, grid.coords[1] == 0, lane_owner.reshape(1, 1, 1, columns) == 0)
    for dim in range(3):
        at = lax.broadcasted_iota(jnp.int32, shape, dim)
        inside = inside & ~((at == 0) & first[dim])

    locked, field = lax.optimization_barrier((locked, field))
    above = by_rows(locked[-edge * edge :])
    below = by_rows(grid.exchanged(above, above, 0, cross=0)[0])
    locked = jnp.concatenate([below, locked], axis=0)

    older = field
    current = field
    steps = len(chebyshev_coeffs)
    for step, coeffs in enumerate(chebyshev_coeffs):
        rows = current.reshape(slot_count, columns)
        partial = lumped * rows.astype(jnp.float32)
        for r in range(GRID_Z):
            own = jnp.where(owner_near == r, rows, jnp.zeros_like(rows))
            partial = partial + jnp.dot(
                matrices[r][:, :slot_count], own, preferred_element_type=jnp.float32
            )
        partial = partial.reshape(shape)
        low, high = plane(partial, 2, 0), plane(partial, 2, SIDE - 1)
        partial = with_ends(
            partial,
            2,
            low + to_next_partition(high, width),
            high + to_previous_partition(low, width),
        )
        if step == 0:
            locked, partial = lax.optimization_barrier((locked, partial))
            all_locked = lines_gathered(grid, locked)
        if step == steps - 1:
            break
        for dim in (1, 0):
            low, high = plane(partial, dim, 0), plane(partial, dim, SIDE - 1)
            to_low, to_high = grid.exchanged(
                low.astype(jnp.bfloat16), high.astype(jnp.bfloat16), dim
            )
            partial = with_ends(
                partial,
                dim,
                low + to_low.astype(jnp.float32),
                high + to_high.astype(jnp.float32),
            )
        following = coeffs[0] * (partial - centre * current.astype(jnp.float32)) - coeffs[
            1
        ] * older.astype(jnp.float32)
        following = rounded(jnp.where(inside, following, 0.0))
        older = current
        current = following
        if step == 1:
            current, all_locked = lax.optimization_barrier((current, all_locked))

    low = plane(partial, 1, 0).astype(jnp.bfloat16)
    to_high = grid.exchanged(low, low, 1)[1].astype(jnp.float32)
    partial = with_ends(partial, 1, None, plane(partial, 1, SIDE - 1) + to_high)
    partial = coeffs[0] * partial[:, 1:, 1:].reshape(SIDE, edge * edge, columns)

    def owned(field):
        return field[1:, 1:, 1:].reshape(edge, edge * edge, columns).astype(jnp.float32)

    rest = -coeffs[0] * centre * owned(current) - coeffs[1] * owned(older)
    sums = jnp.concatenate([partial[:1], partial[1:] + rest], axis=0)
    weights = sums.astype(jnp.bfloat16).reshape(SIDE * edge * edge, columns)
    share = 0.0
    for r in range(GRID_Z):
        share = share + lax.dot_general(
            all_locked[r],
            jnp.where(owner_near == r, weights, jnp.zeros_like(weights)),
            (((0,), (0,)), ((), ())),
            preferred_element_type=jnp.float32,
        )
    share = sum(split(share, GRID_Z))
    deep = share.shape[0] // GRID_Z
    share = jnp.concatenate(
        [share[i * deep : (i + 1) * deep] for i in range(GRID_Z)], axis=1
    ).astype(jnp.bfloat16)

    low = sums[0].astype(jnp.bfloat16)
    stride, count = grid.stride[0], grid.counts[0]
    even = grid.coords[0] % 2 == 0
    arrived = grid.partner(jnp.concatenate([share, low], axis=0), stride | 1)
    share = plus(share, arrived[:deep])
    to_high = jnp.where(even, arrived[deep:], jnp.zeros_like(low))
    if count > 2:
        to_high = to_high + grid.swapped(low, low, 0, 1)[1]
    sums = jnp.concatenate(
        [sums[1:edge], sums[edge:] + to_high[None].astype(jnp.float32)], axis=0
    )
    filtered = rounded(sums.reshape(owned_rows, columns))

    share = plus(share, grid.swapped(share, share, 1, 0, True))
    share = plus(share, grid.swapped(share, share, 1, 1, True))
    share = summed_along(grid, share, stride * 2, count // 2)

    high, low = grid.has(2), grid.share_low
    near = placed(split(filtered, GRID_Z), high, grid.has(1))
    sent = jnp.concatenate([share, packed([near[3], near[2]])], axis=0)
    arrived = grid.partner(sent, FIRST)
    held = jnp.stack([share, arrived[:deep]])
    came = unpacked(arrived[deep:], width)
    own = [near[0], came[0]]
    away = [near[1], came[1]]
    sent = jnp.concatenate([held.reshape(-1, columns), packed(away)], axis=0)
    arrived = grid.partner(sent, SECOND)
    others = arrived[: 2 * deep].reshape(held.shape)
    came = unpacked(arrived[2 * deep :], width)
    filtered = jnp.concatenate(placed([own[0], came[0], own[1], came[1]], high, low), axis=1)
    held = placed([held[0], others[0], held[1], others[1]], high, low)
    intersection = jnp.concatenate(
        [
            jnp.concatenate([h[:, q * width : (q + 1) * width] for h in held], axis=1)
            for q in range(GRID_Z)
        ],
        axis=0,
    ).astype(jnp.float32)
    return filtered, intersection


def solution(mesh):
    in_specs = (
        P(AXIS, None),
        P(AXIS, None, None),
        P(AXIS, None),
        P(AXIS),
        P(AXIS, None),
    )
    out_specs = (P(AXIS, None), P())
    return jax.shard_map(
        per_device, mesh=mesh, in_specs=in_specs, out_specs=out_specs, check_vma=False
    )
```

```python
import jax
import jax.numpy as jnp
from jax import lax
from jax.experimental.layout import Layout, with_layout_constraint
from jax.sharding import PartitionSpec as P

GRID_Y = 4
GRID_Z = 4
SIDE = 7
AXIS = "cells"

chebyshev_coeffs = ((-1.0 / 7.0, 0.0), (-7.0 / 41.0, 8.0 / 41.0), (-41.0 / 259.0, 28.0 / 259.0))
centre = 6.0


class Grid:
    def __init__(self):
        self.devices = lax.axis_size(AXIS)
        self.counts = (self.devices // (GRID_Y * GRID_Z), GRID_Y, GRID_Z)
        self.stride = (GRID_Y * GRID_Z, GRID_Z, 1)
        self.position = lax.axis_index(AXIS)
        self.coords = tuple(
            self.position // self.stride[d] % self.counts[d] for d in range(3)
        )

        flips = self.coords[0] + self.coords[1] + self.coords[2] // 2 + self.coords[2]
        self.share_low = flips % 2 == 1

    def coord_of(self, device, dim):
        return device // self.stride[dim] % self.counts[dim]

    def swapped(self, low, high, dim, odd, raw=False, cross=1):
        count = self.counts[dim]
        pairs = []
        for i in range(self.devices):
            c = self.coord_of(i, dim)
            up = c % 2 == odd
            to = (c + (1 if up else -1)) % count
            pairs.append((i, (i + (to - c) * self.stride[dim]) ^ cross))
        lower = self.coords[dim] % 2 == odd
        arrived = lax.ppermute(jnp.where(lower, high, low), AXIS, pairs)
        if raw:
            return arrived
        zero = jnp.zeros_like(arrived)
        to_low, to_high = jnp.where(lower, zero, arrived), jnp.where(lower, arrived, zero)
        if odd or count % 2:
            to_low = jnp.where(self.coords[dim] > 0, to_low, zero)
            to_high = jnp.where(self.coords[dim] < count - 1, to_high, zero)
        return to_low, to_high

    def exchanged(self, low, high, dim, cross=1):
        to_low, to_high = self.swapped(low, high, dim, 0, cross=cross)
        if self.counts[dim] > 2:
            more_low, more_high = self.swapped(low, high, dim, 1, cross=cross)
            to_low, to_high = to_low + more_low, to_high + more_high
        return to_low, to_high

    def partner(self, value, bits):
        return lax.ppermute(value, AXIS, [(i, i ^ bits) for i in range(self.devices)])

    def has(self, bit):
        return (self.position & bit) != 0


FIRST, SECOND = 3, 1


def placed(near, high, low):
    near = [
        jnp.where(low, near[i ^ 1], near[i]) for i in range(GRID_Z)
    ]
    return [jnp.where(high, near[i ^ 2], near[i]) for i in range(GRID_Z)]


def packed(blocks):
    half = blocks[0].shape[0] // 2
    return jnp.concatenate([b[h : h + half] for h in (0, half) for b in blocks], axis=1)


def unpacked(value, width):
    return [
        jnp.concatenate([value[:, e : e + width] for e in (i * width, (i + 2) * width)], axis=0)
        for i in range(2)
    ]


def split(value, parts):
    width = value.shape[1] // parts
    return [value[:, i * width : (i + 1) * width] for i in range(parts)]


def to_shares(grid, block):
    shares = split(block, GRID_Z)
    width = shares[0].shape[1]
    high = grid.has(2)
    kept = [jnp.where(high, shares[2 + i], shares[i]) for i in range(2)]
    away = [jnp.where(high, shares[i], shares[2 + i]) for i in range(2)]
    came = unpacked(grid.partner(packed(away), FIRST), width)
    low = grid.share_low
    own = [jnp.where(low, kept[1], kept[0]), jnp.where(low, came[1], came[0])]
    away = [jnp.where(low, kept[0], kept[1]), jnp.where(low, came[0], came[1])]
    came = unpacked(grid.partner(packed(away), SECOND), width)
    near = [own[0], came[0], came[1], own[1]]
    return jnp.concatenate(placed(near, high, grid.has(1)), axis=1)


def by_rows(value):
    return with_layout_constraint(value, Layout(major_to_minor=tuple(range(value.ndim))))


def plane(field, dim, at):
    return lax.slice_in_dim(field, at, at + 1, axis=dim)


def with_ends(field, dim, low, high):
    last = field.shape[dim] - 1
    parts = [
        plane(field, dim, 0) if low is None else low,
        lax.slice_in_dim(field, 1, last, axis=dim),
        plane(field, dim, last) if high is None else high,
    ]
    return jnp.concatenate(parts, axis=dim)


def to_next_partition(value, width):
    kept = value[..., :-width]
    return jnp.concatenate([jnp.zeros_like(value[..., :width]), kept], axis=-1)


def to_previous_partition(value, width):
    kept = value[..., width:]
    return jnp.concatenate([kept, jnp.zeros_like(value[..., :width])], axis=-1)


def slots_matrix(cell_matrix, connectivity, potential):
    slots = jnp.arange(potential.shape[0], dtype=jnp.int32)
    total = jnp.where(slots[:, None] == slots[None, :], potential[:, None], 0.0)
    for c in range(cell_matrix.shape[0]):
        chosen = (connectivity[c][:, None] == slots[None, :]).astype(jnp.bfloat16)
        rows = lax.dot_general(
            chosen, cell_matrix[c], (((0,), (0,)), ((), ())), preferred_element_type=jnp.float32
        ).astype(jnp.bfloat16)
        total = total + jnp.dot(rows, chosen, preferred_element_type=jnp.float32)
    return total.astype(jnp.bfloat16)


def rounded(value):
    return lax.reduce_precision(value, 8, 7).astype(jnp.bfloat16)


def plus(first, second):
    return (first.astype(jnp.float32) + second.astype(jnp.float32)).astype(jnp.bfloat16)


def summed_along(grid, value, stride, count):
    factor = 2
    while count > 1:
        while count % factor:
            factor += 1
        at = grid.position // stride % factor
        terms = [value]
        for turn in range(1, factor):
            pairs = []
            for i in range(grid.devices):
                c = i // stride % factor
                pairs.append((i, i + ((c + turn) % factor - c) * stride))
            terms.append(lax.ppermute(value, AXIS, pairs))
        if factor == 2:
            value = plus(*terms)
        else:
            total = 0.0
            for k in range(factor):
                term = terms[0]
                for turn in range(1, factor):
                    term = jnp.where((at - turn) % factor == k, terms[turn], term)
                total = total + term.astype(jnp.float32)
            value = total.astype(jnp.bfloat16)
        count //= factor
        stride *= factor
    return value


def per_device(block, cell_matrix, connectivity, potential, locked):
    owned_rows, columns = block.shape
    slot_count = potential.shape[0]
    width = columns // GRID_Z
    edge = SIDE - 1
    grid = Grid()
    shape = (SIDE, SIDE, SIDE, columns)

    matrix = slots_matrix(cell_matrix, connectivity, potential)
    padded = jnp.pad(matrix, ((0, -slot_count % 16), (0, 0)))
    other = grid.partner(padded, FIRST)
    both = grid.partner(jnp.concatenate([padded, other], axis=0), SECOND)
    above = padded.shape[0]
    matrices = [padded, both[:above], both[above:], other]
    matrices = [m[:slot_count] for m in matrices]
    lane_owner = lax.broadcasted_iota(jnp.int32, (1, columns), 1) // width
    owner_near = lane_owner ^ grid.coords[2]

    mine = to_shares(grid, block)
    field = (
        jnp.zeros(shape, jnp.bfloat16)
        .at[1:, 1:, 1:]
        .set(mine.reshape(edge, edge, edge, columns))
    )
    field = with_ends(field, 2, to_next_partition(plane(field, 2, SIDE - 1), width), None)
    for dim in (1, 0):
        high = plane(field, dim, SIDE - 1)
        field = with_ends(field, dim, grid.exchanged(high, high, dim)[0], None)

    inside = jnp.ones(shape, jnp.bool_)
    first = (grid.coords[0] == 0, grid.coords[1] == 0, lane_owner.reshape(1, 1, 1, columns) == 0)
    for dim in range(3):
        at = lax.broadcasted_iota(jnp.int32, shape, dim)
        inside = inside & ~((at == 0) & first[dim])

    older = field
    current = field
    steps = len(chebyshev_coeffs)
    for step, coeffs in enumerate(chebyshev_coeffs):
        rows = current.reshape(slot_count, columns)
        partial = 0.0
        for r in range(GRID_Z):
            own = jnp.where(owner_near == r, rows, jnp.zeros_like(rows))
            partial = partial + jnp.dot(
                matrices[r], own, preferred_element_type=jnp.float32
            )
        partial = partial.reshape(shape)
        low, high = plane(partial, 2, 0), plane(partial, 2, SIDE - 1)
        partial = with_ends(
            partial,
            2,
            low + to_next_partition(high, width),
            high + to_previous_partition(low, width),
        )
        if step == steps - 1:
            break
        for dim in (1, 0):
            low, high = plane(partial, dim, 0), plane(partial, dim, SIDE - 1)
            low16, high16 = low.astype(jnp.bfloat16), high.astype(jnp.bfloat16)
            if (step, dim) == (0, 0):
                locked, low16, high16 = lax.optimization_barrier((locked, low16, high16))
                top = by_rows(locked[-edge * edge :])
                bottom = by_rows(grid.exchanged(top, top, 0, cross=0)[0])
                locked = jnp.concatenate([bottom, locked], axis=0)
            if (step, dim) == (1, 1):
                locked, low16, high16 = lax.optimization_barrier((locked, low16, high16))
                other_locked = grid.partner(locked, FIRST)
            to_low, to_high = grid.exchanged(low16, high16, dim)
            partial = with_ends(
                partial,
                dim,
                low + to_low.astype(jnp.float32),
                high + to_high.astype(jnp.float32),
            )
        following = coeffs[0] * (partial - centre * current.astype(jnp.float32)) - coeffs[
            1
        ] * older.astype(jnp.float32)
        following = rounded(jnp.where(inside, following, 0.0))
        older = current
        current = following

    low = plane(partial, 1, 0).astype(jnp.bfloat16)
    locked, other_locked, low = lax.optimization_barrier((locked, other_locked, low))
    both_locked = grid.partner(jnp.stack([locked, other_locked]), SECOND)
    all_locked = [locked, both_locked[0], both_locked[1], other_locked]
    to_high = grid.exchanged(low, low, 1)[1].astype(jnp.float32)
    partial = with_ends(partial, 1, None, plane(partial, 1, SIDE - 1) + to_high)
    partial = coeffs[0] * partial[:, 1:, 1:].reshape(SIDE, edge * edge, columns)

    def owned(field):
        return field[1:, 1:, 1:].reshape(edge, edge * edge, columns).astype(jnp.float32)

    rest = -coeffs[0] * centre * owned(current) - coeffs[1] * owned(older)
    sums = jnp.concatenate([partial[:1], partial[1:] + rest], axis=0)
    weights = sums.astype(jnp.bfloat16).reshape(SIDE * edge * edge, columns)
    share = 0.0
    for r in range(GRID_Z):
        share = share + lax.dot_general(
            all_locked[r],
            jnp.where(owner_near == r, weights, jnp.zeros_like(weights)),
            (((0,), (0,)), ((), ())),
            preferred_element_type=jnp.float32,
        )
    share = sum(split(share, GRID_Z))
    deep = share.shape[0] // GRID_Z
    share = jnp.concatenate(
        [share[i * deep : (i + 1) * deep] for i in range(GRID_Z)], axis=1
    ).astype(jnp.bfloat16)

    low = sums[0].astype(jnp.bfloat16)
    stride, count = grid.stride[0], grid.counts[0]
    even = grid.coords[0] % 2 == 0
    arrived = grid.partner(jnp.concatenate([share, low], axis=0), stride | 1)
    share = plus(share, arrived[:deep])
    to_high = jnp.where(even, arrived[deep:], jnp.zeros_like(low))
    if count > 2:
        to_high = to_high + grid.swapped(low, low, 0, 1)[1]
    sums = jnp.concatenate(
        [sums[1:edge], sums[edge:] + to_high[None].astype(jnp.float32)], axis=0
    )
    filtered = rounded(sums.reshape(owned_rows, columns))

    share = plus(share, grid.swapped(share, share, 1, 0, True))
    share = plus(share, grid.swapped(share, share, 1, 1, True))
    share = summed_along(grid, share, stride * 2, count // 2)

    high, low = grid.has(2), grid.share_low
    near = placed(split(filtered, GRID_Z), high, grid.has(1))
    sent = jnp.concatenate([share, packed([near[3], near[2]])], axis=0)
    arrived = grid.partner(sent, FIRST)
    held = jnp.stack([share, arrived[:deep]])
    came = unpacked(arrived[deep:], width)
    own = [near[0], came[0]]
    away = [near[1], came[1]]
    sent = jnp.concatenate([held.reshape(-1, columns), packed(away)], axis=0)
    arrived = grid.partner(sent, SECOND)
    others = arrived[: 2 * deep].reshape(held.shape)
    came = unpacked(arrived[2 * deep :], width)
    filtered = jnp.concatenate(placed([own[0], came[0], own[1], came[1]], high, low), axis=1)
    held = jnp.concatenate([held[0], others[0], held[1], others[1]], axis=1)
    size = (GRID_Z * columns, GRID_Z * columns)
    to, at = lax.broadcasted_iota(jnp.int32, size, 1), lax.broadcasted_iota(jnp.int32, size, 0)
    base = jnp.where(high, 2, 0) + jnp.where(low, 1, 0)
    goal = (
        (at // width % GRID_Z) * columns + ((at // columns) ^ base) * width + at % width
    )
    spread = jnp.dot(held, (goal == to).astype(jnp.bfloat16), preferred_element_type=jnp.float32)
    intersection = jnp.concatenate(split(spread, GRID_Z), axis=0)
    return filtered, intersection


def solution(mesh):
    in_specs = (
        P(AXIS, None),
        P(AXIS, None, None),
        P(AXIS, None),
        P(AXIS),
        P(AXIS, None),
    )
    out_specs = (P(AXIS, None), P())
    return jax.shard_map(
        per_device, mesh=mesh, in_specs=in_specs, out_specs=out_specs, check_vma=False
    )
```

```python
import jax
import jax.numpy as jnp
from jax import lax
from jax.experimental.layout import Layout, with_layout_constraint
from jax.sharding import PartitionSpec as P

GRID_Y = 4
GRID_Z = 4
SIDE = 7
AXIS = "cells"

chebyshev_coeffs = ((-1.0 / 7.0, 0.0), (-7.0 / 41.0, 8.0 / 41.0), (-41.0 / 259.0, 28.0 / 259.0))
centre = 6.0


class Grid:
    def __init__(self):
        self.devices = lax.axis_size(AXIS)
        self.counts = (self.devices // (GRID_Y * GRID_Z), GRID_Y, GRID_Z)
        self.stride = (GRID_Y * GRID_Z, GRID_Z, 1)
        self.position = lax.axis_index(AXIS)
        self.coords = tuple(
            self.position // self.stride[d] % self.counts[d] for d in range(3)
        )

        flips = self.coords[0] + self.coords[1] + self.coords[2] // 2 + self.coords[2]
        self.share_low = flips % 2 == 1

    def coord_of(self, device, dim):
        return device // self.stride[dim] % self.counts[dim]

    def swapped(self, low, high, dim, odd, raw=False, cross=1):
        count = self.counts[dim]
        pairs = []
        for i in range(self.devices):
            c = self.coord_of(i, dim)
            up = c % 2 == odd
            to = (c + (1 if up else -1)) % count
            pairs.append((i, (i + (to - c) * self.stride[dim]) ^ cross))
        lower = self.coords[dim] % 2 == odd
        arrived = lax.ppermute(jnp.where(lower, high, low), AXIS, pairs)
        if raw:
            return arrived
        zero = jnp.zeros_like(arrived)
        to_low, to_high = jnp.where(lower, zero, arrived), jnp.where(lower, arrived, zero)
        if odd or count % 2:
            to_low = jnp.where(self.coords[dim] > 0, to_low, zero)
            to_high = jnp.where(self.coords[dim] < count - 1, to_high, zero)
        return to_low, to_high

    def exchanged(self, low, high, dim, cross=1):
        to_low, to_high = self.swapped(low, high, dim, 0, cross=cross)
        if self.counts[dim] > 2:
            more_low, more_high = self.swapped(low, high, dim, 1, cross=cross)
            to_low, to_high = to_low + more_low, to_high + more_high
        return to_low, to_high

    def partner(self, value, bits):
        return lax.ppermute(value, AXIS, [(i, i ^ bits) for i in range(self.devices)])

    def has(self, bit):
        return (self.position & bit) != 0


FIRST, SECOND = 3, 1


def placed(near, high, low):
    near = [
        jnp.where(low, near[i ^ 1], near[i]) for i in range(GRID_Z)
    ]
    return [jnp.where(high, near[i ^ 2], near[i]) for i in range(GRID_Z)]


def packed(blocks):
    half = blocks[0].shape[0] // 2
    return jnp.concatenate([b[h : h + half] for h in (0, half) for b in blocks], axis=1)


def unpacked(value, width):
    return [
        jnp.concatenate([value[:, e : e + width] for e in (i * width, (i + 2) * width)], axis=0)
        for i in range(2)
    ]


def split(value, parts):
    width = value.shape[1] // parts
    return [value[:, i * width : (i + 1) * width] for i in range(parts)]


def to_shares(grid, block, other):
    shares = split(block, GRID_Z)
    width = shares[0].shape[1]
    high = grid.has(2)
    kept = [jnp.where(high, shares[2 + i], shares[i]) for i in range(2)]
    away = [jnp.where(high, shares[i], shares[2 + i]) for i in range(2)]
    came = unpacked(grid.partner(packed(away), FIRST), width)
    low = grid.share_low
    own = [jnp.where(low, kept[1], kept[0]), jnp.where(low, came[1], came[0])]
    away = [jnp.where(low, kept[0], kept[1]), jnp.where(low, came[0], came[1])]
    away, other = lax.optimization_barrier((packed(away), other))
    came = unpacked(grid.partner(away, SECOND), width)
    other = by_rows(grid.partner(other, SECOND))
    near = [own[0], came[0], came[1], own[1]]
    return jnp.concatenate(placed(near, high, grid.has(1)), axis=1), other


def by_rows(value):
    return with_layout_constraint(value, Layout(major_to_minor=tuple(range(value.ndim))))


def plane(field, dim, at):
    return lax.slice_in_dim(field, at, at + 1, axis=dim)


def with_ends(field, dim, low, high):
    last = field.shape[dim] - 1
    parts = [
        plane(field, dim, 0) if low is None else low,
        lax.slice_in_dim(field, 1, last, axis=dim),
        plane(field, dim, last) if high is None else high,
    ]
    return jnp.concatenate(parts, axis=dim)


def to_next_partition(value, width):
    kept = value[..., :-width]
    return jnp.concatenate([jnp.zeros_like(value[..., :width]), kept], axis=-1)


def to_previous_partition(value, width):
    kept = value[..., width:]
    return jnp.concatenate([kept, jnp.zeros_like(value[..., :width])], axis=-1)


def slots_matrix(cell_matrix, connectivity, potential):
    slots = jnp.arange(potential.shape[0], dtype=jnp.int32)
    total = jnp.where(slots[:, None] == slots[None, :], potential[:, None], 0.0)
    for c in range(cell_matrix.shape[0]):
        chosen = (connectivity[c][:, None] == slots[None, :]).astype(jnp.bfloat16)
        rows = lax.dot_general(
            chosen, cell_matrix[c], (((0,), (0,)), ((), ())), preferred_element_type=jnp.float32
        ).astype(jnp.bfloat16)
        total = total + jnp.dot(rows, chosen, preferred_element_type=jnp.float32)
    return total.astype(jnp.bfloat16)


def rounded(value):
    return lax.reduce_precision(value, 8, 7).astype(jnp.bfloat16)


def plus(first, second):
    return (first.astype(jnp.float32) + second.astype(jnp.float32)).astype(jnp.bfloat16)


def summed_along(grid, value, stride, count):
    factor = 2
    while count > 1:
        while count % factor:
            factor += 1
        at = grid.position // stride % factor
        terms = [value]
        for turn in range(1, factor):
            pairs = []
            for i in range(grid.devices):
                c = i // stride % factor
                pairs.append((i, i + ((c + turn) % factor - c) * stride))
            terms.append(lax.ppermute(value, AXIS, pairs))
        if factor == 2:
            value = plus(*terms)
        else:
            total = 0.0
            for k in range(factor):
                term = terms[0]
                for turn in range(1, factor):
                    term = jnp.where((at - turn) % factor == k, terms[turn], term)
                total = total + term.astype(jnp.float32)
            value = total.astype(jnp.bfloat16)
        count //= factor
        stride *= factor
    return value


def per_device(block, cell_matrix, connectivity, potential, locked):
    owned_rows, columns = block.shape
    slot_count = potential.shape[0]
    width = columns // GRID_Z
    edge = SIDE - 1
    grid = Grid()
    shape = (SIDE, SIDE, SIDE, columns)

    field = block.reshape(edge, edge, edge, columns)
    high = plane(field, 1, edge - 1)
    cell_matrix, high = lax.optimization_barrier((cell_matrix, high))
    matrix = by_rows(slots_matrix(cell_matrix, connectivity, potential))
    other = by_rows(grid.partner(matrix, FIRST))
    field = jnp.concatenate([grid.exchanged(high, high, 1, cross=0)[0], field], axis=1)
    high = plane(field, 0, edge - 1)

    locked, high = lax.optimization_barrier((locked, high))
    top = by_rows(locked[-edge * edge :])
    bottom = by_rows(grid.exchanged(top, top, 0, cross=0)[0])
    locked = jnp.concatenate([bottom, locked], axis=0)
    other_locked = grid.partner(locked, FIRST)

    field = jnp.concatenate([grid.exchanged(high, high, 0, cross=0)[0], field], axis=0)
    rows = field.reshape(SIDE * SIDE * edge, columns)
    second = by_rows(grid.partner(matrix, SECOND))
    mine, both = to_shares(grid, jnp.pad(rows, ((0, -rows.shape[0] % 16), (0, 0))), other)
    mine, both = lax.optimization_barrier((mine, both))
    matrices = [matrix, second, both, other]
    field = mine[: rows.shape[0]].reshape(SIDE, SIDE, edge, columns)
    low = to_next_partition(plane(field, 2, edge - 1), width)
    field = jnp.concatenate([low, field], axis=2)

    lane_owner = lax.broadcasted_iota(jnp.int32, (1, columns), 1) // width
    owner_near = lane_owner ^ grid.coords[2]

    inside = jnp.ones(shape, jnp.bool_)
    first = (grid.coords[0] == 0, grid.coords[1] == 0, lane_owner.reshape(1, 1, 1, columns) == 0)
    for dim in range(3):
        at = lax.broadcasted_iota(jnp.int32, shape, dim)
        inside = inside & ~((at == 0) & first[dim])

    older = field
    current = field
    steps = len(chebyshev_coeffs)
    for step, coeffs in enumerate(chebyshev_coeffs):
        rows = current.reshape(slot_count, columns)
        partial = 0.0
        for r in range(GRID_Z):
            own = jnp.where(owner_near == r, rows, jnp.zeros_like(rows))
            partial = partial + jnp.dot(
                matrices[r], own, preferred_element_type=jnp.float32
            )
        partial = partial.reshape(shape)
        low, high = plane(partial, 2, 0), plane(partial, 2, SIDE - 1)
        partial = with_ends(
            partial,
            2,
            low + to_next_partition(high, width),
            high + to_previous_partition(low, width),
        )
        if step == steps - 1:
            break
        for dim in (1, 0):
            low, high = plane(partial, dim, 0), plane(partial, dim, SIDE - 1)
            low16, high16 = low.astype(jnp.bfloat16), high.astype(jnp.bfloat16)
            if (step, dim) == (1, 1):
                low16, other_locked = lax.optimization_barrier((low16, other_locked))
            to_low, to_high = grid.exchanged(low16, high16, dim)
            partial = with_ends(
                partial,
                dim,
                low + to_low.astype(jnp.float32),
                high + to_high.astype(jnp.float32),
            )
        following = coeffs[0] * (partial - centre * current.astype(jnp.float32)) - coeffs[
            1
        ] * older.astype(jnp.float32)
        following = rounded(jnp.where(inside, following, 0.0))
        older = current
        current = following
        if step == 1:
            both_locked = grid.partner(jnp.stack([locked, other_locked]), SECOND)
            current, both_locked = lax.optimization_barrier((current, both_locked))
            all_locked = [locked, both_locked[0], both_locked[1], other_locked]

    low = plane(partial, 1, 0).astype(jnp.bfloat16)
    to_high = grid.exchanged(low, low, 1)[1].astype(jnp.float32)
    partial = with_ends(partial, 1, None, plane(partial, 1, SIDE - 1) + to_high)
    partial = coeffs[0] * partial[:, 1:, 1:].reshape(SIDE, edge * edge, columns)

    def owned(field):
        return field[1:, 1:, 1:].reshape(edge, edge * edge, columns).astype(jnp.float32)

    rest = -coeffs[0] * centre * owned(current) - coeffs[1] * owned(older)
    sums = jnp.concatenate([partial[:1], partial[1:] + rest], axis=0)
    weights = sums.astype(jnp.bfloat16).reshape(SIDE * edge * edge, columns)
    share = 0.0
    for r in range(GRID_Z):
        share = share + lax.dot_general(
            all_locked[r],
            jnp.where(owner_near == r, weights, jnp.zeros_like(weights)),
            (((0,), (0,)), ((), ())),
            preferred_element_type=jnp.float32,
        )
    share = sum(split(share, GRID_Z))
    deep = share.shape[0] // GRID_Z
    share = jnp.concatenate(
        [share[i * deep : (i + 1) * deep] for i in range(GRID_Z)], axis=1
    ).astype(jnp.bfloat16)

    low = sums[0].astype(jnp.bfloat16)
    stride, count = grid.stride[0], grid.counts[0]
    even = grid.coords[0] % 2 == 0
    arrived = grid.partner(jnp.concatenate([share, low], axis=0), stride | 1)
    share = plus(share, arrived[:deep])
    to_high = jnp.where(even, arrived[deep:], jnp.zeros_like(low))
    if count > 2:
        to_high = to_high + grid.swapped(low, low, 0, 1)[1]
    sums = jnp.concatenate(
        [sums[1:edge], sums[edge:] + to_high[None].astype(jnp.float32)], axis=0
    )
    filtered = rounded(sums.reshape(owned_rows, columns))

    share = plus(share, grid.swapped(share, share, 1, 0, True))
    share = plus(share, grid.swapped(share, share, 1, 1, True))
    share = summed_along(grid, share, stride * 2, count // 2)

    high, low = grid.has(2), grid.share_low
    near = placed(split(filtered, GRID_Z), high, grid.has(1))
    sent = jnp.concatenate([share, packed([near[3], near[2]])], axis=0)
    arrived = grid.partner(sent, FIRST)
    held = jnp.stack([share, arrived[:deep]])
    came = unpacked(arrived[deep:], width)
    own = [near[0], came[0]]
    away = [near[1], came[1]]
    sent = jnp.concatenate([held.reshape(-1, columns), packed(away)], axis=0)
    arrived = grid.partner(sent, SECOND)
    others = arrived[: 2 * deep].reshape(held.shape)
    came = unpacked(arrived[2 * deep :], width)
    filtered = jnp.concatenate(placed([own[0], came[0], own[1], came[1]], high, low), axis=1)
    held = jnp.concatenate([held[0], others[0], held[1], others[1]], axis=1)
    size = (GRID_Z * columns, GRID_Z * columns)
    to, at = lax.broadcasted_iota(jnp.int32, size, 1), lax.broadcasted_iota(jnp.int32, size, 0)
    base = jnp.where(high, 2, 0) + jnp.where(low, 1, 0)
    goal = (
        (at // width % GRID_Z) * columns + ((at // columns) ^ base) * width + at % width
    )
    spread = jnp.dot(held, (goal == to).astype(jnp.bfloat16), preferred_element_type=jnp.float32)
    intersection = jnp.concatenate(split(spread, GRID_Z), axis=0)
    return filtered, intersection


def solution(mesh):
    in_specs = (
        P(AXIS, None),
        P(AXIS, None, None),
        P(AXIS, None),
        P(AXIS),
        P(AXIS, None),
    )
    out_specs = (P(AXIS, None), P())
    return jax.shard_map(
        per_device, mesh=mesh, in_specs=in_specs, out_specs=out_specs, check_vma=False
    )
```

```python
import jax
import jax.numpy as jnp
from jax import lax
from jax.experimental.layout import Layout, with_layout_constraint
from jax.sharding import PartitionSpec as P

GRID_Y = 4
GRID_Z = 4
SIDE = 7
AXIS = "cells"

chebyshev_coeffs = ((-1.0 / 7.0, 0.0), (-7.0 / 41.0, 8.0 / 41.0), (-41.0 / 259.0, 28.0 / 259.0))
centre = 6.0


class Grid:
    def __init__(self):
        self.devices = lax.axis_size(AXIS)
        self.counts = (self.devices // (GRID_Y * GRID_Z), GRID_Y, GRID_Z)
        self.stride = (GRID_Y * GRID_Z, GRID_Z, 1)
        self.position = lax.axis_index(AXIS)
        self.coords = tuple(
            self.position // self.stride[d] % self.counts[d] for d in range(3)
        )

        flips = self.coords[0] + self.coords[1] + self.coords[2] // 2 + self.coords[2]
        self.share_low = flips % 2 == 1

    def coord_of(self, device, dim):
        return device // self.stride[dim] % self.counts[dim]

    def swapped(self, low, high, dim, odd, raw=False, cross=1):
        count = self.counts[dim]
        pairs = []
        for i in range(self.devices):
            c = self.coord_of(i, dim)
            up = c % 2 == odd
            to = (c + (1 if up else -1)) % count
            pairs.append((i, (i + (to - c) * self.stride[dim]) ^ cross))
        lower = self.coords[dim] % 2 == odd
        arrived = lax.ppermute(jnp.where(lower, high, low), AXIS, pairs)
        if raw:
            return arrived
        zero = jnp.zeros_like(arrived)
        to_low, to_high = jnp.where(lower, zero, arrived), jnp.where(lower, arrived, zero)
        if odd or count % 2:
            to_low = jnp.where(self.coords[dim] > 0, to_low, zero)
            to_high = jnp.where(self.coords[dim] < count - 1, to_high, zero)
        return to_low, to_high

    def exchanged(self, low, high, dim, cross=1):
        to_low, to_high = self.swapped(low, high, dim, 0, cross=cross)
        if self.counts[dim] > 2:
            more_low, more_high = self.swapped(low, high, dim, 1, cross=cross)
            to_low, to_high = to_low + more_low, to_high + more_high
        return to_low, to_high

    def partner(self, value, bits):
        return lax.ppermute(value, AXIS, [(i, i ^ bits) for i in range(self.devices)])

    def has(self, bit):
        return (self.position & bit) != 0


FIRST, SECOND = 3, 1


def placed(near, high, low):
    near = [
        jnp.where(low, near[i ^ 1], near[i]) for i in range(GRID_Z)
    ]
    return [jnp.where(high, near[i ^ 2], near[i]) for i in range(GRID_Z)]


def packed(blocks):
    half = blocks[0].shape[0] // 2
    return jnp.concatenate([b[h : h + half] for h in (0, half) for b in blocks], axis=1)


def unpacked(value, width):
    return [
        jnp.concatenate([value[:, e : e + width] for e in (i * width, (i + 2) * width)], axis=0)
        for i in range(2)
    ]


def split(value, parts):
    width = value.shape[1] // parts
    return [value[:, i * width : (i + 1) * width] for i in range(parts)]


def to_shares(grid, block, other):
    shares = split(block, GRID_Z)
    width = shares[0].shape[1]
    high = grid.has(2)
    kept = [jnp.where(high, shares[2 + i], shares[i]) for i in range(2)]
    away = [jnp.where(high, shares[i], shares[2 + i]) for i in range(2)]
    came = unpacked(grid.partner(packed(away), FIRST), width)
    low = grid.share_low
    own = [jnp.where(low, kept[1], kept[0]), jnp.where(low, came[1], came[0])]
    away = [jnp.where(low, kept[0], kept[1]), jnp.where(low, came[0], came[1])]
    away, other = lax.optimization_barrier((packed(away), other))
    came = unpacked(grid.partner(away, SECOND), width)
    other = by_rows(grid.partner(other, SECOND))
    near = [own[0], came[0], came[1], own[1]]
    return jnp.concatenate(placed(near, high, grid.has(1)), axis=1), other


def by_rows(value):
    return with_layout_constraint(value, Layout(major_to_minor=tuple(range(value.ndim))))


def plane(field, dim, at):
    return lax.slice_in_dim(field, at, at + 1, axis=dim)


def with_ends(field, dim, low, high):
    last = field.shape[dim] - 1
    parts = [
        plane(field, dim, 0) if low is None else low,
        lax.slice_in_dim(field, 1, last, axis=dim),
        plane(field, dim, last) if high is None else high,
    ]
    return jnp.concatenate(parts, axis=dim)


def to_next_partition(value, width):
    kept = value[..., :-width]
    return jnp.concatenate([jnp.zeros_like(value[..., :width]), kept], axis=-1)


def to_previous_partition(value, width):
    kept = value[..., width:]
    return jnp.concatenate([kept, jnp.zeros_like(value[..., :width])], axis=-1)


def slots_matrix(cell_matrix, connectivity, potential):
    slots = jnp.arange(potential.shape[0], dtype=jnp.int32)
    total = jnp.where(slots[:, None] == slots[None, :], potential[:, None], 0.0)
    for c in range(cell_matrix.shape[0]):
        chosen = (connectivity[c][:, None] == slots[None, :]).astype(jnp.bfloat16)
        rows = lax.dot_general(
            chosen, cell_matrix[c], (((0,), (0,)), ((), ())), preferred_element_type=jnp.float32
        ).astype(jnp.bfloat16)
        total = total + jnp.dot(rows, chosen, preferred_element_type=jnp.float32)
    return total.astype(jnp.bfloat16)


def rounded(value):
    return lax.reduce_precision(value, 8, 7).astype(jnp.bfloat16)


def plus(first, second):
    return (first.astype(jnp.float32) + second.astype(jnp.float32)).astype(jnp.bfloat16)


def summed_along(grid, value, stride, count):
    factor = 2
    while count > 1:
        while count % factor:
            factor += 1
        at = grid.position // stride % factor
        terms = [value]
        for turn in range(1, factor):
            pairs = []
            for i in range(grid.devices):
                c = i // stride % factor
                pairs.append((i, i + ((c + turn) % factor - c) * stride))
            terms.append(lax.ppermute(value, AXIS, pairs))
        if factor == 2:
            value = plus(*terms)
        else:
            total = 0.0
            for k in range(factor):
                term = terms[0]
                for turn in range(1, factor):
                    term = jnp.where((at - turn) % factor == k, terms[turn], term)
                total = total + term.astype(jnp.float32)
            value = total.astype(jnp.bfloat16)
        count //= factor
        stride *= factor
    return value


def per_device(block, cell_matrix, connectivity, potential, locked):
    owned_rows, columns = block.shape
    slot_count = potential.shape[0]
    width = columns // GRID_Z
    edge = SIDE - 1
    grid = Grid()
    shape = (SIDE, SIDE, SIDE, columns)

    field = block.reshape(edge, edge, edge, columns)
    high = plane(field, 1, edge - 1)
    cell_matrix, high = lax.optimization_barrier((cell_matrix, high))
    matrix = by_rows(slots_matrix(cell_matrix, connectivity, potential))
    other = by_rows(grid.partner(matrix, FIRST))
    field = jnp.concatenate([grid.exchanged(high, high, 1, cross=0)[0], field], axis=1)
    high = plane(field, 0, edge - 1)

    locked, high = lax.optimization_barrier((locked, high))
    top = by_rows(locked[-edge * edge :])
    bottom = by_rows(grid.exchanged(top, top, 0, cross=0)[0])
    locked = jnp.concatenate([bottom, locked], axis=0)
    other_locked = grid.partner(locked, FIRST)

    field = jnp.concatenate([grid.exchanged(high, high, 0, cross=0)[0], field], axis=0)
    rows = field.reshape(SIDE * SIDE * edge, columns)
    second = by_rows(grid.partner(matrix, SECOND))
    mine, both = to_shares(grid, jnp.pad(rows, ((0, -rows.shape[0] % 16), (0, 0))), other)
    mine, both = lax.optimization_barrier((mine, both))
    matrices = [matrix, second, both, other]
    field = mine[: rows.shape[0]].reshape(SIDE, SIDE, edge, columns)
    low = to_next_partition(plane(field, 2, edge - 1), width)
    field = jnp.concatenate([low, field], axis=2)

    lane_owner = lax.broadcasted_iota(jnp.int32, (1, columns), 1) // width
    owner_near = lane_owner ^ grid.coords[2]

    inside = jnp.ones(shape, jnp.bool_)
    first = (grid.coords[0] == 0, grid.coords[1] == 0, lane_owner.reshape(1, 1, 1, columns) == 0)
    for dim in range(3):
        at = lax.broadcasted_iota(jnp.int32, shape, dim)
        inside = inside & ~((at == 0) & first[dim])

    older = field
    current = field
    steps = len(chebyshev_coeffs)
    for step, coeffs in enumerate(chebyshev_coeffs):
        rows = current.reshape(slot_count, columns)
        partial = 0.0
        for r in range(GRID_Z):
            own = jnp.where(owner_near == r, rows, jnp.zeros_like(rows))
            partial = partial + jnp.dot(
                matrices[r], own, preferred_element_type=jnp.float32
            )
        partial = partial.reshape(shape)
        low, high = plane(partial, 2, 0), plane(partial, 2, SIDE - 1)
        partial = with_ends(
            partial,
            2,
            low + to_next_partition(high, width),
            high + to_previous_partition(low, width),
        )
        if step == steps - 1:
            break
        for dim in (1, 0):
            low, high = plane(partial, dim, 0), plane(partial, dim, SIDE - 1)
            low16, high16 = low.astype(jnp.bfloat16), high.astype(jnp.bfloat16)
            to_low, to_high = grid.exchanged(low16, high16, dim)
            partial = with_ends(
                partial,
                dim,
                low + to_low.astype(jnp.float32),
                high + to_high.astype(jnp.float32),
            )
        following = coeffs[0] * (partial - centre * current.astype(jnp.float32)) - coeffs[
            1
        ] * older.astype(jnp.float32)
        following = rounded(jnp.where(inside, following, 0.0))
        older = current
        current = following
        if step == 1:
            both_locked = grid.partner(jnp.stack([locked, other_locked]), SECOND)
            current, both_locked = lax.optimization_barrier((current, both_locked))
            all_locked = [locked, both_locked[0], both_locked[1], other_locked]

    low = plane(partial, 1, 0).astype(jnp.bfloat16)
    to_high = grid.exchanged(low, low, 1)[1].astype(jnp.float32)
    partial = with_ends(partial, 1, None, plane(partial, 1, SIDE - 1) + to_high)
    partial = coeffs[0] * partial[:, 1:, 1:].reshape(SIDE, edge * edge, columns)

    def owned(field):
        return field[1:, 1:, 1:].reshape(edge, edge * edge, columns).astype(jnp.float32)

    rest = -coeffs[0] * centre * owned(current) - coeffs[1] * owned(older)
    sums = jnp.concatenate([partial[:1], partial[1:] + rest], axis=0)
    weights = sums.astype(jnp.bfloat16).reshape(SIDE * edge * edge, columns)
    share = 0.0
    for r in range(GRID_Z):
        share = share + lax.dot_general(
            all_locked[r],
            jnp.where(owner_near == r, weights, jnp.zeros_like(weights)),
            (((0,), (0,)), ((), ())),
            preferred_element_type=jnp.float32,
        )
    share = sum(split(share, GRID_Z))
    deep = share.shape[0] // GRID_Z
    share = jnp.concatenate(
        [share[i * deep : (i + 1) * deep] for i in range(GRID_Z)], axis=1
    ).astype(jnp.bfloat16)

    low = sums[0].astype(jnp.bfloat16)
    stride, count = grid.stride[0], grid.counts[0]
    even = grid.coords[0] % 2 == 0
    arrived = grid.partner(jnp.concatenate([share, low], axis=0), stride | 1)
    share = plus(share, arrived[:deep])
    to_high = jnp.where(even, arrived[deep:], jnp.zeros_like(low))
    if count > 2:
        to_high = to_high + grid.swapped(low, low, 0, 1)[1]
    sums = jnp.concatenate(
        [sums[1:edge], sums[edge:] + to_high[None].astype(jnp.float32)], axis=0
    )
    filtered = rounded(sums.reshape(owned_rows, columns))

    share = plus(share, grid.swapped(share, share, 1, 0, True))
    share = plus(share, grid.swapped(share, share, 1, 1, True))
    share = summed_along(grid, share, stride * 2, count // 2)

    high, low = grid.has(2), grid.share_low
    near = placed(split(filtered, GRID_Z), high, grid.has(1))
    sent = jnp.concatenate([share, packed([near[3], near[2]])], axis=0)
    arrived = grid.partner(sent, FIRST)
    held = jnp.stack([share, arrived[:deep]])
    came = unpacked(arrived[deep:], width)
    own = [near[0], came[0]]
    away = [near[1], came[1]]
    sent = jnp.concatenate([held.reshape(-1, columns), packed(away)], axis=0)
    arrived = grid.partner(sent, SECOND)
    others = arrived[: 2 * deep].reshape(held.shape)
    came = unpacked(arrived[2 * deep :], width)
    filtered = jnp.concatenate(placed([own[0], came[0], own[1], came[1]], high, low), axis=1)
    held = jnp.concatenate([held[0], others[0], held[1], others[1]], axis=1)
    size = (GRID_Z * columns, GRID_Z * columns)
    to, at = lax.broadcasted_iota(jnp.int32, size, 1), lax.broadcasted_iota(jnp.int32, size, 0)
    base = jnp.where(high, 2, 0) + jnp.where(low, 1, 0)
    goal = (
        (at // width % GRID_Z) * columns + ((at // columns) ^ base) * width + at % width
    )
    spread = jnp.dot(held, (goal == to).astype(jnp.bfloat16), preferred_element_type=jnp.float32)
    intersection = jnp.concatenate(split(spread, GRID_Z), axis=0)
    return filtered, intersection


def solution(mesh):
    in_specs = (
        P(AXIS, None),
        P(AXIS, None, None),
        P(AXIS, None),
        P(AXIS),
        P(AXIS, None),
    )
    out_specs = (P(AXIS, None), P())
    return jax.shard_map(
        per_device, mesh=mesh, in_specs=in_specs, out_specs=out_specs, check_vma=False
    )
```

```python
import jax
import jax.numpy as jnp
from jax import lax
from jax.experimental.layout import Layout, with_layout_constraint
from jax.sharding import PartitionSpec as P

GRID_Y = 4
GRID_Z = 4
SIDE = 7
AXIS = "cells"

chebyshev_coeffs = ((-1.0 / 7.0, 0.0), (-7.0 / 41.0, 8.0 / 41.0), (-41.0 / 259.0, 28.0 / 259.0))
centre = 6.0


class Grid:
    def __init__(self):
        self.devices = lax.axis_size(AXIS)
        self.counts = (self.devices // (GRID_Y * GRID_Z), GRID_Y, GRID_Z)
        self.stride = (GRID_Y * GRID_Z, GRID_Z, 1)
        self.position = lax.axis_index(AXIS)
        self.coords = tuple(
            self.position // self.stride[d] % self.counts[d] for d in range(3)
        )

        flips = self.coords[0] + self.coords[1] + self.coords[2] // 2 + self.coords[2]
        self.share_low = flips % 2 == 1

    def coord_of(self, device, dim):
        return device // self.stride[dim] % self.counts[dim]

    def swapped(self, low, high, dim, odd, raw=False, cross=1):
        count = self.counts[dim]
        pairs = []
        for i in range(self.devices):
            c = self.coord_of(i, dim)
            up = c % 2 == odd
            to = (c + (1 if up else -1)) % count
            pairs.append((i, (i + (to - c) * self.stride[dim]) ^ cross))
        lower = self.coords[dim] % 2 == odd
        arrived = lax.ppermute(jnp.where(lower, high, low), AXIS, pairs)
        if raw:
            return arrived
        zero = jnp.zeros_like(arrived)
        to_low, to_high = jnp.where(lower, zero, arrived), jnp.where(lower, arrived, zero)
        if odd or count % 2:
            to_low = jnp.where(self.coords[dim] > 0, to_low, zero)
            to_high = jnp.where(self.coords[dim] < count - 1, to_high, zero)
        return to_low, to_high

    def exchanged(self, low, high, dim, cross=1):
        to_low, to_high = self.swapped(low, high, dim, 0, cross=cross)
        if self.counts[dim] > 2:
            more_low, more_high = self.swapped(low, high, dim, 1, cross=cross)
            to_low, to_high = to_low + more_low, to_high + more_high
        return to_low, to_high

    def partner(self, value, bits):
        return lax.ppermute(value, AXIS, [(i, i ^ bits) for i in range(self.devices)])

    def has(self, bit):
        return (self.position & bit) != 0


FIRST, SECOND = 3, 1


def placed(near, high, low):
    near = [
        jnp.where(low, near[i ^ 1], near[i]) for i in range(GRID_Z)
    ]
    return [jnp.where(high, near[i ^ 2], near[i]) for i in range(GRID_Z)]


def packed(blocks):
    half = blocks[0].shape[0] // 2
    return jnp.concatenate([b[h : h + half] for h in (0, half) for b in blocks], axis=1)


def unpacked(value, width):
    return [
        jnp.concatenate([value[:, e : e + width] for e in (i * width, (i + 2) * width)], axis=0)
        for i in range(2)
    ]


def split(value, parts):
    width = value.shape[1] // parts
    return [value[:, i * width : (i + 1) * width] for i in range(parts)]


def to_shares(grid, block, other):
    shares = split(block, GRID_Z)
    width = shares[0].shape[1]
    high = grid.has(2)
    kept = [jnp.where(high, shares[2 + i], shares[i]) for i in range(2)]
    away = [jnp.where(high, shares[i], shares[2 + i]) for i in range(2)]
    came = unpacked(grid.partner(packed(away), FIRST), width)
    low = grid.share_low
    own = [jnp.where(low, kept[1], kept[0]), jnp.where(low, came[1], came[0])]
    away = [jnp.where(low, kept[0], kept[1]), jnp.where(low, came[0], came[1])]
    away, other = lax.optimization_barrier((packed(away), other))
    came = unpacked(grid.partner(away, SECOND), width)
    other = by_rows(grid.partner(other, SECOND))
    near = [own[0], came[0], came[1], own[1]]
    return jnp.concatenate(placed(near, high, grid.has(1)), axis=1), other


def by_rows(value):
    return with_layout_constraint(value, Layout(major_to_minor=tuple(range(value.ndim))))


def plane(field, dim, at):
    return lax.slice_in_dim(field, at, at + 1, axis=dim)


def with_ends(field, dim, low, high):
    last = field.shape[dim] - 1
    parts = [
        plane(field, dim, 0) if low is None else low,
        lax.slice_in_dim(field, 1, last, axis=dim),
        plane(field, dim, last) if high is None else high,
    ]
    return jnp.concatenate(parts, axis=dim)


def to_next_partition(value, width):
    kept = value[..., :-width]
    return jnp.concatenate([jnp.zeros_like(value[..., :width]), kept], axis=-1)


def to_previous_partition(value, width):
    kept = value[..., width:]
    return jnp.concatenate([kept, jnp.zeros_like(value[..., :width])], axis=-1)


def slots_matrix(cell_matrix, connectivity, potential):
    slots = jnp.arange(potential.shape[0], dtype=jnp.int32)
    total = jnp.where(slots[:, None] == slots[None, :], potential[:, None], 0.0)
    for c in range(cell_matrix.shape[0]):
        chosen = (connectivity[c][:, None] == slots[None, :]).astype(jnp.bfloat16)
        rows = lax.dot_general(
            chosen, cell_matrix[c], (((0,), (0,)), ((), ())), preferred_element_type=jnp.float32
        ).astype(jnp.bfloat16)
        total = total + jnp.dot(rows, chosen, preferred_element_type=jnp.float32)
    return total.astype(jnp.bfloat16)


def rounded(value):
    return lax.reduce_precision(value, 8, 7).astype(jnp.bfloat16)


def plus(first, second):
    return (first.astype(jnp.float32) + second.astype(jnp.float32)).astype(jnp.bfloat16)


def summed_along(grid, value, stride, count):
    factor = 2
    while count > 1:
        while count % factor:
            factor += 1
        at = grid.position // stride % factor
        terms = [value]
        for turn in range(1, factor):
            pairs = []
            for i in range(grid.devices):
                c = i // stride % factor
                pairs.append((i, i + ((c + turn) % factor - c) * stride))
            terms.append(lax.ppermute(value, AXIS, pairs))
        if factor == 2:
            value = plus(*terms)
        else:
            total = 0.0
            for k in range(factor):
                term = terms[0]
                for turn in range(1, factor):
                    term = jnp.where((at - turn) % factor == k, terms[turn], term)
                total = total + term.astype(jnp.float32)
            value = total.astype(jnp.bfloat16)
        count //= factor
        stride *= factor
    return value


def per_device(block, cell_matrix, connectivity, potential, locked):
    owned_rows, columns = block.shape
    slot_count = potential.shape[0]
    width = columns // GRID_Z
    edge = SIDE - 1
    grid = Grid()
    shape = (SIDE, SIDE, SIDE, columns)

    field = block.reshape(edge, edge, edge, columns)
    high = plane(field, 1, edge - 1)
    cell_matrix, high = lax.optimization_barrier((cell_matrix, high))
    matrix = by_rows(slots_matrix(cell_matrix, connectivity, potential))
    other = by_rows(grid.partner(matrix, FIRST))
    field = jnp.concatenate([grid.exchanged(high, high, 1, cross=0)[0], field], axis=1)

    high = field[edge - 1].reshape(SIDE * edge, columns)
    tiles = -(-locked.shape[1] // columns)
    top = jnp.pad(locked[-edge * edge :], ((0, 0), (0, -locked.shape[1] % columns)))
    top = jnp.concatenate(split(top, tiles), axis=0)
    sent = jnp.concatenate([top, high], axis=0)
    arrived = grid.exchanged(sent, sent, 0, cross=0)[0]
    bottom = jnp.split(arrived[: top.shape[0]], tiles, axis=0)
    bottom = jnp.concatenate(bottom, axis=1)[:, : locked.shape[1]]
    locked = jnp.concatenate([bottom, locked], axis=0)
    field = jnp.concatenate(
        [arrived[top.shape[0] :].reshape(1, SIDE, edge, columns), field], axis=0
    )

    rows = field.reshape(SIDE * SIDE * edge, columns)
    second = by_rows(grid.partner(matrix, SECOND))
    mine, both = to_shares(grid, jnp.pad(rows, ((0, -rows.shape[0] % 16), (0, 0))), other)
    mine, both = lax.optimization_barrier((mine, both))
    matrices = [matrix, second, both, other]

    locked, mine = lax.optimization_barrier((locked, mine))
    parts = [locked[:128], locked[128:]]
    other_parts = [grid.partner(part, FIRST) for part in parts]
    field = mine[: rows.shape[0]].reshape(SIDE, SIDE, edge, columns)
    low = to_next_partition(plane(field, 2, edge - 1), width)
    field = jnp.concatenate([low, field], axis=2)

    lane_owner = lax.broadcasted_iota(jnp.int32, (1, columns), 1) // width
    owner_near = lane_owner ^ grid.coords[2]

    inside = jnp.ones(shape, jnp.bool_)
    first = (grid.coords[0] == 0, grid.coords[1] == 0, lane_owner.reshape(1, 1, 1, columns) == 0)
    for dim in range(3):
        at = lax.broadcasted_iota(jnp.int32, shape, dim)
        inside = inside & ~((at == 0) & first[dim])

    older = field
    current = field
    steps = len(chebyshev_coeffs)
    for step, coeffs in enumerate(chebyshev_coeffs):
        rows = current.reshape(slot_count, columns)
        partial = 0.0
        for r in range(GRID_Z):
            own = jnp.where(owner_near == r, rows, jnp.zeros_like(rows))
            partial = partial + jnp.dot(
                matrices[r], own, preferred_element_type=jnp.float32
            )
        partial = partial.reshape(shape)
        low, high = plane(partial, 2, 0), plane(partial, 2, SIDE - 1)
        partial = with_ends(
            partial,
            2,
            low + to_next_partition(high, width),
            high + to_previous_partition(low, width),
        )
        if step == steps - 1:
            break
        for dim in (1, 0):
            low, high = plane(partial, dim, 0), plane(partial, dim, SIDE - 1)
            low16, high16 = low.astype(jnp.bfloat16), high.astype(jnp.bfloat16)
            if step == 1:
                low16, other_parts[1 - dim] = lax.optimization_barrier(
                    (low16, other_parts[1 - dim])
                )
            to_low, to_high = grid.exchanged(low16, high16, dim)
            partial = with_ends(
                partial,
                dim,
                low + to_low.astype(jnp.float32),
                high + to_high.astype(jnp.float32),
            )
        following = coeffs[0] * (partial - centre * current.astype(jnp.float32)) - coeffs[
            1
        ] * older.astype(jnp.float32)
        following = rounded(jnp.where(inside, following, 0.0))
        older = current
        current = following
    other_locked = jnp.concatenate(other_parts, axis=0)
    both_locked = grid.partner(jnp.stack([locked, other_locked]), SECOND)
    low = plane(partial, 1, 0).astype(jnp.bfloat16)
    low, both_locked = lax.optimization_barrier((low, both_locked))
    all_locked = [locked, both_locked[0], both_locked[1], other_locked]
    to_high = grid.exchanged(low, low, 1)[1].astype(jnp.float32)
    partial = with_ends(partial, 1, None, plane(partial, 1, SIDE - 1) + to_high)
    partial = coeffs[0] * partial[:, 1:, 1:].reshape(SIDE, edge * edge, columns)

    def owned(field):
        return field[1:, 1:, 1:].reshape(edge, edge * edge, columns).astype(jnp.float32)

    rest = -coeffs[0] * centre * owned(current) - coeffs[1] * owned(older)
    sums = jnp.concatenate([partial[:1], partial[1:] + rest], axis=0)
    weights = sums.astype(jnp.bfloat16).reshape(SIDE * edge * edge, columns)
    share = 0.0
    for r in range(GRID_Z):
        share = share + lax.dot_general(
            all_locked[r],
            jnp.where(owner_near == r, weights, jnp.zeros_like(weights)),
            (((0,), (0,)), ((), ())),
            preferred_element_type=jnp.float32,
        )
    share = sum(split(share, GRID_Z))
    deep = share.shape[0] // GRID_Z
    share = jnp.concatenate(
        [share[i * deep : (i + 1) * deep] for i in range(GRID_Z)], axis=1
    ).astype(jnp.bfloat16)

    low = sums[0].astype(jnp.bfloat16)
    stride, count = grid.stride[0], grid.counts[0]
    even = grid.coords[0] % 2 == 0
    arrived = grid.partner(jnp.concatenate([share, low], axis=0), stride | 1)
    share = plus(share, arrived[:deep])
    to_high = jnp.where(even, arrived[deep:], jnp.zeros_like(low))
    if count > 2:
        to_high = to_high + grid.swapped(low, low, 0, 1)[1]
    sums = jnp.concatenate(
        [sums[1:edge], sums[edge:] + to_high[None].astype(jnp.float32)], axis=0
    )
    filtered = rounded(sums.reshape(owned_rows, columns))

    share = plus(share, grid.swapped(share, share, 1, 0, True))
    share = plus(share, grid.swapped(share, share, 1, 1, True))
    share = summed_along(grid, share, stride * 2, count // 2)

    high, low = grid.has(2), grid.share_low
    near = placed(split(filtered, GRID_Z), high, grid.has(1))
    sent = jnp.concatenate([share, packed([near[3], near[2]])], axis=0)
    arrived = grid.partner(sent, FIRST)
    held = jnp.stack([share, arrived[:deep]])
    came = unpacked(arrived[deep:], width)
    own = [near[0], came[0]]
    away = [near[1], came[1]]
    sent = jnp.concatenate([held.reshape(-1, columns), packed(away)], axis=0)
    arrived = grid.partner(sent, SECOND)
    others = arrived[: 2 * deep].reshape(held.shape)
    came = unpacked(arrived[2 * deep :], width)
    filtered = jnp.concatenate(placed([own[0], came[0], own[1], came[1]], high, low), axis=1)
    held = jnp.concatenate([held[0], others[0], held[1], others[1]], axis=1)
    size = (GRID_Z * columns, GRID_Z * columns)
    to, at = lax.broadcasted_iota(jnp.int32, size, 1), lax.broadcasted_iota(jnp.int32, size, 0)
    base = jnp.where(high, 2, 0) + jnp.where(low, 1, 0)
    goal = (
        (at // width % GRID_Z) * columns + ((at // columns) ^ base) * width + at % width
    )
    spread = jnp.dot(held, (goal == to).astype(jnp.bfloat16), preferred_element_type=jnp.float32)
    intersection = jnp.concatenate(split(spread, GRID_Z), axis=0)
    return filtered, intersection


def solution(mesh):
    in_specs = (
        P(AXIS, None),
        P(AXIS, None, None),
        P(AXIS, None),
        P(AXIS),
        P(AXIS, None),
    )
    out_specs = (P(AXIS, None), P())
    return jax.shard_map(
        per_device, mesh=mesh, in_specs=in_specs, out_specs=out_specs, check_vma=False
    )
```

```python
import jax
import jax.numpy as jnp
from jax import lax
from jax.experimental.layout import Layout, with_layout_constraint
from jax.sharding import PartitionSpec as P

GRID_Y = 4
GRID_Z = 4
SIDE = 7
AXIS = "cells"

chebyshev_coeffs = ((-1.0 / 7.0, 0.0), (-7.0 / 41.0, 8.0 / 41.0), (-41.0 / 259.0, 28.0 / 259.0))
centre = 6.0


class Grid:
    def __init__(self):
        self.devices = lax.axis_size(AXIS)
        self.counts = (self.devices // (GRID_Y * GRID_Z), GRID_Y, GRID_Z)
        self.stride = (GRID_Y * GRID_Z, GRID_Z, 1)
        self.position = lax.axis_index(AXIS)
        self.coords = tuple(
            self.position // self.stride[d] % self.counts[d] for d in range(3)
        )

        flips = self.coords[0] + self.coords[1] + self.coords[2] // 2 + self.coords[2]
        self.share_low = flips % 2 == 1

    def coord_of(self, device, dim):
        return device // self.stride[dim] % self.counts[dim]

    def swapped(self, low, high, dim, odd, raw=False, cross=1):
        count = self.counts[dim]
        pairs = []
        for i in range(self.devices):
            c = self.coord_of(i, dim)
            up = c % 2 == odd
            to = (c + (1 if up else -1)) % count
            pairs.append((i, (i + (to - c) * self.stride[dim]) ^ cross))
        lower = self.coords[dim] % 2 == odd
        arrived = lax.ppermute(jnp.where(lower, high, low), AXIS, pairs)
        if raw:
            return arrived
        zero = jnp.zeros_like(arrived)
        to_low, to_high = jnp.where(lower, zero, arrived), jnp.where(lower, arrived, zero)
        if odd or count % 2:
            to_low = jnp.where(self.coords[dim] > 0, to_low, zero)
            to_high = jnp.where(self.coords[dim] < count - 1, to_high, zero)
        return to_low, to_high

    def exchanged(self, low, high, dim, cross=1):
        to_low, to_high = self.swapped(low, high, dim, 0, cross=cross)
        if self.counts[dim] > 2:
            more_low, more_high = self.swapped(low, high, dim, 1, cross=cross)
            to_low, to_high = to_low + more_low, to_high + more_high
        return to_low, to_high

    def partner(self, value, bits):
        return lax.ppermute(value, AXIS, [(i, i ^ bits) for i in range(self.devices)])

    def has(self, bit):
        return (self.position & bit) != 0


FIRST, SECOND = 3, 1


def placed(near, high, low):
    near = [
        jnp.where(low, near[i ^ 1], near[i]) for i in range(GRID_Z)
    ]
    return [jnp.where(high, near[i ^ 2], near[i]) for i in range(GRID_Z)]


def packed(blocks):
    half = blocks[0].shape[0] // 2
    return jnp.concatenate([b[h : h + half] for h in (0, half) for b in blocks], axis=1)


def unpacked(value, width):
    return [
        jnp.concatenate([value[:, e : e + width] for e in (i * width, (i + 2) * width)], axis=0)
        for i in range(2)
    ]


def split(value, parts):
    width = value.shape[1] // parts
    return [value[:, i * width : (i + 1) * width] for i in range(parts)]


def to_shares(grid, block, other):
    shares = split(block, GRID_Z)
    width = shares[0].shape[1]
    high = grid.has(2)
    kept = [jnp.where(high, shares[2 + i], shares[i]) for i in range(2)]
    away = [jnp.where(high, shares[i], shares[2 + i]) for i in range(2)]
    came = unpacked(grid.partner(packed(away), FIRST), width)
    low = grid.share_low
    own = [jnp.where(low, kept[1], kept[0]), jnp.where(low, came[1], came[0])]
    away = [jnp.where(low, kept[0], kept[1]), jnp.where(low, came[0], came[1])]
    away, other = lax.optimization_barrier((packed(away), other))
    came = unpacked(grid.partner(away, SECOND), width)
    other = by_rows(grid.partner(other, SECOND))
    near = [own[0], came[0], came[1], own[1]]
    return jnp.concatenate(placed(near, high, grid.has(1)), axis=1), other


def by_rows(value):
    return with_layout_constraint(value, Layout(major_to_minor=tuple(range(value.ndim))))


def plane(field, dim, at):
    return lax.slice_in_dim(field, at, at + 1, axis=dim)


def with_ends(field, dim, low, high):
    last = field.shape[dim] - 1
    parts = [
        plane(field, dim, 0) if low is None else low,
        lax.slice_in_dim(field, 1, last, axis=dim),
        plane(field, dim, last) if high is None else high,
    ]
    return jnp.concatenate(parts, axis=dim)


def to_next_partition(value, width):
    kept = value[..., :-width]
    return jnp.concatenate([jnp.zeros_like(value[..., :width]), kept], axis=-1)


def to_previous_partition(value, width):
    kept = value[..., width:]
    return jnp.concatenate([kept, jnp.zeros_like(value[..., :width])], axis=-1)


def slots_matrix(cell_matrix, connectivity, potential):
    slots = jnp.arange(potential.shape[0], dtype=jnp.int32)
    total = jnp.where(slots[:, None] == slots[None, :], potential[:, None], 0.0)
    for c in range(cell_matrix.shape[0]):
        chosen = (connectivity[c][:, None] == slots[None, :]).astype(jnp.bfloat16)
        rows = lax.dot_general(
            chosen, cell_matrix[c], (((0,), (0,)), ((), ())), preferred_element_type=jnp.float32
        ).astype(jnp.bfloat16)
        total = total + jnp.dot(rows, chosen, preferred_element_type=jnp.float32)
    return total.astype(jnp.bfloat16)


def rounded(value):
    return lax.reduce_precision(value, 8, 7).astype(jnp.bfloat16)


def plus(first, second):
    return (first.astype(jnp.float32) + second.astype(jnp.float32)).astype(jnp.bfloat16)


def summed_along(grid, value, stride, count):
    factor = 2
    while count > 1:
        while count % factor:
            factor += 1
        at = grid.position // stride % factor
        terms = [value]
        for turn in range(1, factor):
            pairs = []
            for i in range(grid.devices):
                c = i // stride % factor
                pairs.append((i, i + ((c + turn) % factor - c) * stride))
            terms.append(lax.ppermute(value, AXIS, pairs))
        if factor == 2:
            value = plus(*terms)
        else:
            total = 0.0
            for k in range(factor):
                term = terms[0]
                for turn in range(1, factor):
                    term = jnp.where((at - turn) % factor == k, terms[turn], term)
                total = total + term.astype(jnp.float32)
            value = total.astype(jnp.bfloat16)
        count //= factor
        stride *= factor
    return value


def per_device(block, cell_matrix, connectivity, potential, locked):
    owned_rows, columns = block.shape
    slot_count = potential.shape[0]
    width = columns // GRID_Z
    edge = SIDE - 1
    grid = Grid()
    shape = (SIDE, SIDE, SIDE, columns)

    field = block.reshape(edge, edge, edge, columns)
    high = plane(field, 1, edge - 1)
    cell_matrix, high = lax.optimization_barrier((cell_matrix, high))
    matrix = by_rows(slots_matrix(cell_matrix, connectivity, potential))
    other = by_rows(grid.partner(matrix, FIRST))
    field = jnp.concatenate([grid.exchanged(high, high, 1, cross=0)[0], field], axis=1)

    high = field[edge - 1].reshape(SIDE * edge, columns)
    tiles = -(-locked.shape[1] // columns)
    top = jnp.pad(locked[-edge * edge :], ((0, 0), (0, -locked.shape[1] % columns)))
    top = jnp.concatenate(split(top, tiles), axis=0)
    sent = jnp.concatenate([top, high], axis=0)
    arrived = grid.exchanged(sent, sent, 0, cross=0)[0]
    bottom = jnp.split(arrived[: top.shape[0]], tiles, axis=0)
    bottom = jnp.concatenate(bottom, axis=1)[:, : locked.shape[1]]
    locked = jnp.concatenate([bottom, locked], axis=0)
    field = jnp.concatenate(
        [arrived[top.shape[0] :].reshape(1, SIDE, edge, columns), field], axis=0
    )

    rows = field.reshape(SIDE * SIDE * edge, columns)
    second = by_rows(grid.partner(matrix, SECOND))
    mine, both = to_shares(grid, jnp.pad(rows, ((0, -rows.shape[0] % 16), (0, 0))), other)
    mine, both = lax.optimization_barrier((mine, both))
    matrices = [matrix, second, both, other]

    locked, mine = lax.optimization_barrier((locked, mine))
    parts = [locked[:128], locked[128:]]
    other_parts = [grid.partner(part, FIRST) for part in parts]
    field = mine[: rows.shape[0]].reshape(SIDE, SIDE, edge, columns)
    low = to_next_partition(plane(field, 2, edge - 1), width)
    field = jnp.concatenate([low, field], axis=2)

    lane_owner = lax.broadcasted_iota(jnp.int32, (1, columns), 1) // width
    owner_near = lane_owner ^ grid.coords[2]

    older = field
    current = field
    steps = len(chebyshev_coeffs)
    for step, coeffs in enumerate(chebyshev_coeffs):
        rows = current.reshape(slot_count, columns)
        partial = 0.0
        for r in range(GRID_Z):
            own = jnp.where(owner_near == r, rows, jnp.zeros_like(rows))
            partial = partial + jnp.dot(
                matrices[r], own, preferred_element_type=jnp.float32
            )
        partial = partial.reshape(shape)
        low, high = plane(partial, 2, 0), plane(partial, 2, SIDE - 1)
        partial = with_ends(
            partial,
            2,
            jnp.where(lane_owner > 0, low + to_next_partition(high, width), 0.0),
            high + to_previous_partition(low, width),
        )
        if step == steps - 1:
            break
        for dim in (1, 0):
            low, high = plane(partial, dim, 0), plane(partial, dim, SIDE - 1)
            low16, high16 = low.astype(jnp.bfloat16), high.astype(jnp.bfloat16)
            if step == 1:
                low16, other_parts[1 - dim] = lax.optimization_barrier(
                    (low16, other_parts[1 - dim])
                )
            to_low, to_high = grid.exchanged(low16, high16, dim)
            partial = with_ends(
                partial,
                dim,
                jnp.where(grid.coords[dim] > 0, low + to_low.astype(jnp.float32), 0.0),
                high + to_high.astype(jnp.float32),
            )
        following = coeffs[0] * (partial - centre * current.astype(jnp.float32)) - coeffs[
            1
        ] * older.astype(jnp.float32)
        following = rounded(following)
        older = current
        current = following
    other_locked = jnp.concatenate(other_parts, axis=0)
    both_locked = grid.partner(jnp.stack([locked, other_locked]), SECOND)
    low = plane(partial, 1, 0).astype(jnp.bfloat16)
    low, both_locked = lax.optimization_barrier((low, both_locked))
    all_locked = [locked, both_locked[0], both_locked[1], other_locked]
    to_high = grid.exchanged(low, low, 1)[1].astype(jnp.float32)
    partial = with_ends(partial, 1, None, plane(partial, 1, SIDE - 1) + to_high)
    partial = coeffs[0] * partial[:, 1:, 1:].reshape(SIDE, edge * edge, columns)

    def owned(field):
        return field[1:, 1:, 1:].reshape(edge, edge * edge, columns).astype(jnp.float32)

    rest = -coeffs[0] * centre * owned(current) - coeffs[1] * owned(older)
    sums = jnp.concatenate([partial[:1], partial[1:] + rest], axis=0)
    weights = sums.astype(jnp.bfloat16).reshape(SIDE * edge * edge, columns)
    share = 0.0
    for r in range(GRID_Z):
        share = share + lax.dot_general(
            all_locked[r],
            jnp.where(owner_near == r, weights, jnp.zeros_like(weights)),
            (((0,), (0,)), ((), ())),
            preferred_element_type=jnp.float32,
        )
    share = sum(split(share, GRID_Z))
    deep = share.shape[0] // GRID_Z
    share = jnp.concatenate(
        [share[i * deep : (i + 1) * deep] for i in range(GRID_Z)], axis=1
    ).astype(jnp.bfloat16)

    low = sums[0].astype(jnp.bfloat16)
    stride, count = grid.stride[0], grid.counts[0]
    even = grid.coords[0] % 2 == 0
    arrived = grid.partner(jnp.concatenate([share, low], axis=0), stride | 1)
    share = plus(share, arrived[:deep])
    to_high = jnp.where(even, arrived[deep:], jnp.zeros_like(low))
    if count > 2:
        to_high = to_high + grid.swapped(low, low, 0, 1)[1]
    sums = jnp.concatenate(
        [sums[1:edge], sums[edge:] + to_high[None].astype(jnp.float32)], axis=0
    )
    filtered = rounded(sums.reshape(owned_rows, columns))

    share = plus(share, grid.swapped(share, share, 1, 0, True))
    share = plus(share, grid.swapped(share, share, 1, 1, True))
    share = summed_along(grid, share, stride * 2, count // 2)

    high, low = grid.has(2), grid.share_low
    near = placed(split(filtered, GRID_Z), high, grid.has(1))
    sent = jnp.concatenate([share, packed([near[3], near[2]])], axis=0)
    arrived = grid.partner(sent, FIRST)
    held = jnp.stack([share, arrived[:deep]])
    came = unpacked(arrived[deep:], width)
    own = [near[0], came[0]]
    away = [near[1], came[1]]
    sent = jnp.concatenate([held.reshape(-1, columns), packed(away)], axis=0)
    arrived = grid.partner(sent, SECOND)
    others = arrived[: 2 * deep].reshape(held.shape)
    came = unpacked(arrived[2 * deep :], width)
    filtered = jnp.concatenate(placed([own[0], came[0], own[1], came[1]], high, low), axis=1)
    held = placed([held[0], others[0], held[1], others[1]], high, low)
    intersection = jnp.concatenate(
        [
            jnp.concatenate([h[:, q * width : (q + 1) * width] for h in held], axis=1)
            for q in range(GRID_Z)
        ],
        axis=0,
    ).astype(jnp.float32)
    return filtered, intersection


def solution(mesh):
    in_specs = (
        P(AXIS, None),
        P(AXIS, None, None),
        P(AXIS, None),
        P(AXIS),
        P(AXIS, None),
    )
    out_specs = (P(AXIS, None), P())
    return jax.shard_map(
        per_device, mesh=mesh, in_specs=in_specs, out_specs=out_specs, check_vma=False
    )
```

```python
import jax
import jax.numpy as jnp
from jax import lax
from jax.experimental.layout import Layout, with_layout_constraint
from jax.sharding import PartitionSpec as P

GRID_Y = 4
GRID_Z = 4
SIDE = 7
AXIS = "cells"

chebyshev_coeffs = ((-1.0 / 7.0, 0.0), (-7.0 / 41.0, 8.0 / 41.0), (-41.0 / 259.0, 28.0 / 259.0))
centre = 6.0


class Grid:
    def __init__(self):
        self.devices = lax.axis_size(AXIS)
        self.counts = (self.devices // (GRID_Y * GRID_Z), GRID_Y, GRID_Z)
        self.stride = (GRID_Y * GRID_Z, GRID_Z, 1)
        self.position = lax.axis_index(AXIS)
        self.coords = tuple(
            self.position // self.stride[d] % self.counts[d] for d in range(3)
        )

        flips = self.coords[0] + self.coords[1] + self.coords[2] // 2 + self.coords[2]
        self.share_low = flips % 2 == 1

    def coord_of(self, device, dim):
        return device // self.stride[dim] % self.counts[dim]

    def swapped(self, low, high, dim, odd, raw=False, cross=1):
        count = self.counts[dim]
        pairs = []
        for i in range(self.devices):
            c = self.coord_of(i, dim)
            up = c % 2 == odd
            to = (c + (1 if up else -1)) % count
            pairs.append((i, (i + (to - c) * self.stride[dim]) ^ cross))
        lower = self.coords[dim] % 2 == odd
        arrived = lax.ppermute(jnp.where(lower, high, low), AXIS, pairs)
        if raw:
            return arrived
        zero = jnp.zeros_like(arrived)
        to_low, to_high = jnp.where(lower, zero, arrived), jnp.where(lower, arrived, zero)
        if odd or count % 2:
            to_low = jnp.where(self.coords[dim] > 0, to_low, zero)
            to_high = jnp.where(self.coords[dim] < count - 1, to_high, zero)
        return to_low, to_high

    def exchanged(self, low, high, dim, cross=1):
        to_low, to_high = self.swapped(low, high, dim, 0, cross=cross)
        if self.counts[dim] > 2:
            more_low, more_high = self.swapped(low, high, dim, 1, cross=cross)
            to_low, to_high = to_low + more_low, to_high + more_high
        return to_low, to_high

    def partner(self, value, bits):
        return lax.ppermute(value, AXIS, [(i, i ^ bits) for i in range(self.devices)])

    def has(self, bit):
        return (self.position & bit) != 0


FIRST, SECOND = 3, 1


def placed(near, high, low):
    near = [
        jnp.where(low, near[i ^ 1], near[i]) for i in range(GRID_Z)
    ]
    return [jnp.where(high, near[i ^ 2], near[i]) for i in range(GRID_Z)]


def packed(blocks):
    half = blocks[0].shape[0] // 2
    return jnp.concatenate([b[h : h + half] for h in (0, half) for b in blocks], axis=1)


def unpacked(value, width):
    return [
        jnp.concatenate([value[:, e : e + width] for e in (i * width, (i + 2) * width)], axis=0)
        for i in range(2)
    ]


def split(value, parts):
    width = value.shape[1] // parts
    return [value[:, i * width : (i + 1) * width] for i in range(parts)]


def to_shares(grid, block, other):
    shares = split(block, GRID_Z)
    width = shares[0].shape[1]
    high = grid.has(2)
    kept = [jnp.where(high, shares[2 + i], shares[i]) for i in range(2)]
    away = [jnp.where(high, shares[i], shares[2 + i]) for i in range(2)]
    came = unpacked(grid.partner(packed(away), FIRST), width)
    low = grid.share_low
    own = [jnp.where(low, kept[1], kept[0]), jnp.where(low, came[1], came[0])]
    away = [jnp.where(low, kept[0], kept[1]), jnp.where(low, came[0], came[1])]
    away, other = lax.optimization_barrier((packed(away), other))
    came = unpacked(grid.partner(away, SECOND), width)
    other = by_rows(grid.partner(other, SECOND))
    near = [own[0], came[0], came[1], own[1]]
    return jnp.concatenate(placed(near, high, grid.has(1)), axis=1), other


def by_rows(value):
    return with_layout_constraint(value, Layout(major_to_minor=tuple(range(value.ndim))))


def plane(field, dim, at):
    return lax.slice_in_dim(field, at, at + 1, axis=dim)


def with_ends(field, dim, low, high):
    last = field.shape[dim] - 1
    parts = [
        plane(field, dim, 0) if low is None else low,
        lax.slice_in_dim(field, 1, last, axis=dim),
        plane(field, dim, last) if high is None else high,
    ]
    return jnp.concatenate(parts, axis=dim)


def to_next_partition(value, width):
    kept = value[..., :-width]
    return jnp.concatenate([jnp.zeros_like(value[..., :width]), kept], axis=-1)


def to_previous_partition(value, width):
    kept = value[..., width:]
    return jnp.concatenate([kept, jnp.zeros_like(value[..., :width])], axis=-1)


def slots_matrix(cell_matrix, connectivity, potential):
    slots = jnp.arange(potential.shape[0], dtype=jnp.int32)
    total = jnp.where(slots[:, None] == slots[None, :], potential[:, None], 0.0)
    for c in range(cell_matrix.shape[0]):
        chosen = (connectivity[c][:, None] == slots[None, :]).astype(jnp.bfloat16)
        rows = lax.dot_general(
            chosen, cell_matrix[c], (((0,), (0,)), ((), ())), preferred_element_type=jnp.float32
        ).astype(jnp.bfloat16)
        total = total + jnp.dot(rows, chosen, preferred_element_type=jnp.float32)
    return total.astype(jnp.bfloat16)


def rounded(value):
    return lax.reduce_precision(value, 8, 7).astype(jnp.bfloat16)


def plus(first, second):
    return (first.astype(jnp.float32) + second.astype(jnp.float32)).astype(jnp.bfloat16)


def summed_along(grid, value, stride, count):
    factor = 2
    while count > 1:
        while count % factor:
            factor += 1
        at = grid.position // stride % factor
        terms = [value]
        for turn in range(1, factor):
            pairs = []
            for i in range(grid.devices):
                c = i // stride % factor
                pairs.append((i, i + ((c + turn) % factor - c) * stride))
            terms.append(lax.ppermute(value, AXIS, pairs))
        if factor == 2:
            value = plus(*terms)
        else:
            total = 0.0
            for k in range(factor):
                term = terms[0]
                for turn in range(1, factor):
                    term = jnp.where((at - turn) % factor == k, terms[turn], term)
                total = total + term.astype(jnp.float32)
            value = total.astype(jnp.bfloat16)
        count //= factor
        stride *= factor
    return value


def per_device(block, cell_matrix, connectivity, potential, locked):
    owned_rows, columns = block.shape
    slot_count = potential.shape[0]
    width = columns // GRID_Z
    edge = SIDE - 1
    grid = Grid()
    shape = (SIDE, SIDE, SIDE, columns)

    field = block.reshape(edge, edge, edge, columns)
    high = plane(field, 1, edge - 1)
    cell_matrix, high = lax.optimization_barrier((cell_matrix, high))
    matrix = by_rows(slots_matrix(cell_matrix, connectivity, potential))
    other = by_rows(grid.partner(matrix, FIRST))
    field = jnp.concatenate([grid.exchanged(high, high, 1, cross=0)[0], field], axis=1)

    high = field[edge - 1].reshape(SIDE * edge, columns)
    tiles = -(-locked.shape[1] // columns)
    top = jnp.pad(locked[-edge * edge :], ((0, 0), (0, -locked.shape[1] % columns)))
    top = jnp.concatenate(split(top, tiles), axis=0)
    sent = jnp.concatenate([top, high], axis=0)
    arrived = grid.exchanged(sent, sent, 0, cross=0)[0]
    bottom = jnp.split(arrived[: top.shape[0]], tiles, axis=0)
    bottom = jnp.concatenate(bottom, axis=1)[:, : locked.shape[1]]
    locked = jnp.concatenate([bottom, locked], axis=0)
    field = jnp.concatenate(
        [arrived[top.shape[0] :].reshape(1, SIDE, edge, columns), field], axis=0
    )

    rows = field.reshape(SIDE * SIDE * edge, columns)
    second = by_rows(grid.partner(matrix, SECOND))
    mine, both = to_shares(grid, jnp.pad(rows, ((0, -rows.shape[0] % 16), (0, 0))), other)
    mine, both = lax.optimization_barrier((mine, both))
    matrices = [matrix, second, both, other]

    locked, mine = lax.optimization_barrier((locked, mine))
    parts = [locked[:128], locked[128:]]
    other_parts = [grid.partner(part, FIRST) for part in parts]
    field = mine[: rows.shape[0]].reshape(SIDE, SIDE, edge, columns)
    low = to_next_partition(plane(field, 2, edge - 1), width)
    field = jnp.concatenate([low, field], axis=2)

    lane_owner = lax.broadcasted_iota(jnp.int32, (1, columns), 1) // width
    owner_near = lane_owner ^ grid.coords[2]

    current = field
    older = lax.optimization_barrier(field)
    steps = len(chebyshev_coeffs)
    for step, coeffs in enumerate(chebyshev_coeffs):
        rows = current.reshape(slot_count, columns)
        partial = 0.0
        for r in range(GRID_Z):
            own = jnp.where(owner_near == r, rows, jnp.zeros_like(rows))
            partial = partial + jnp.dot(
                matrices[r], own, preferred_element_type=jnp.float32
            )
        partial = partial.reshape(shape)
        low, high = plane(partial, 2, 0), plane(partial, 2, SIDE - 1)
        partial = with_ends(
            partial,
            2,
            jnp.where(lane_owner > 0, low + to_next_partition(high, width), 0.0),
            high + to_previous_partition(low, width),
        )
        if step == steps - 1:
            break
        for dim in (1, 0):
            low, high = plane(partial, dim, 0), plane(partial, dim, SIDE - 1)
            low16, high16 = low.astype(jnp.bfloat16), high.astype(jnp.bfloat16)
            if step == 1:
                low16, other_parts[1 - dim] = lax.optimization_barrier(
                    (low16, other_parts[1 - dim])
                )
            to_low, to_high = grid.exchanged(low16, high16, dim)
            partial = with_ends(
                partial,
                dim,
                jnp.where(grid.coords[dim] > 0, low + to_low.astype(jnp.float32), 0.0),
                high + to_high.astype(jnp.float32),
            )
        following = coeffs[0] * (partial - centre * current.astype(jnp.float32)) - coeffs[
            1
        ] * older.astype(jnp.float32)
        following = rounded(following)
        older = lax.optimization_barrier(current)
        current = following
    other_locked = jnp.concatenate(other_parts, axis=0)
    both_locked = grid.partner(jnp.stack([locked, other_locked]), SECOND)
    low = plane(partial, 1, 0).astype(jnp.bfloat16)
    all_locked = [locked, both_locked[0], both_locked[1], other_locked]
    to_high = grid.exchanged(low, low, 1)[1].astype(jnp.float32)
    partial = with_ends(partial, 1, None, plane(partial, 1, SIDE - 1) + to_high)
    partial = coeffs[0] * partial[:, 1:, 1:].reshape(SIDE, edge * edge, columns)

    def owned(field):
        return field[1:, 1:, 1:].reshape(edge, edge * edge, columns).astype(jnp.float32)

    rest = -coeffs[0] * centre * owned(current) - coeffs[1] * owned(older)
    sums = jnp.concatenate([partial[:1], partial[1:] + rest], axis=0)
    weights = sums.astype(jnp.bfloat16).reshape(SIDE * edge * edge, columns)
    share = 0.0
    for r in range(GRID_Z):
        share = share + lax.dot_general(
            all_locked[r],
            jnp.where(owner_near == r, weights, jnp.zeros_like(weights)),
            (((0,), (0,)), ((), ())),
            preferred_element_type=jnp.float32,
        )
    share = sum(split(share, GRID_Z))
    deep = share.shape[0] // GRID_Z
    share = jnp.concatenate(
        [share[i * deep : (i + 1) * deep] for i in range(GRID_Z)], axis=1
    ).astype(jnp.bfloat16)

    low = sums[0].astype(jnp.bfloat16)
    stride, count = grid.stride[0], grid.counts[0]
    even = grid.coords[0] % 2 == 0
    arrived = grid.partner(jnp.concatenate([share, low], axis=0), stride | 1)
    share = plus(share, arrived[:deep])
    to_high = jnp.where(even, arrived[deep:], jnp.zeros_like(low))
    if count > 2:
        to_high = to_high + grid.swapped(low, low, 0, 1)[1]
    sums = jnp.concatenate(
        [sums[1:edge], sums[edge:] + to_high[None].astype(jnp.float32)], axis=0
    )
    filtered = rounded(sums.reshape(owned_rows, columns))

    share = plus(share, grid.swapped(share, share, 1, 0, True))
    share = plus(share, grid.swapped(share, share, 1, 1, True))
    share = summed_along(grid, share, stride * 2, count // 2)

    high, low = grid.has(2), grid.share_low
    near = placed(split(filtered, GRID_Z), high, grid.has(1))
    sent = jnp.concatenate([share, packed([near[3], near[2]])], axis=0)
    arrived = grid.partner(sent, FIRST)
    held = jnp.stack([share, arrived[:deep]])
    came = unpacked(arrived[deep:], width)
    own = [near[0], came[0]]
    away = [near[1], came[1]]
    sent = jnp.concatenate([held.reshape(-1, columns), packed(away)], axis=0)
    arrived = grid.partner(sent, SECOND)
    others = arrived[: 2 * deep].reshape(held.shape)
    came = unpacked(arrived[2 * deep :], width)
    filtered = jnp.concatenate(placed([own[0], came[0], own[1], came[1]], high, low), axis=1)
    held = placed([held[0], others[0], held[1], others[1]], high, low)
    intersection = jnp.concatenate(
        [
            jnp.concatenate([h[:, q * width : (q + 1) * width] for h in held], axis=1)
            for q in range(GRID_Z)
        ],
        axis=0,
    ).astype(jnp.float32)
    return filtered, intersection


def solution(mesh):
    in_specs = (
        P(AXIS, None),
        P(AXIS, None, None),
        P(AXIS, None),
        P(AXIS),
        P(AXIS, None),
    )
    out_specs = (P(AXIS, None), P())
    return jax.shard_map(
        per_device, mesh=mesh, in_specs=in_specs, out_specs=out_specs, check_vma=False
    )
```

```python
import jax
import jax.numpy as jnp
from jax import lax
from jax.experimental.layout import Layout, with_layout_constraint
from jax.sharding import PartitionSpec as P

GRID_Y = 4
GRID_Z = 4
SIDE = 7
AXIS = "cells"

chebyshev_coeffs = ((-1.0 / 7.0, 0.0), (-7.0 / 41.0, 8.0 / 41.0), (-41.0 / 259.0, 28.0 / 259.0))
centre = 6.0


class Grid:
    def __init__(self):
        self.devices = lax.axis_size(AXIS)
        self.counts = (self.devices // (GRID_Y * GRID_Z), GRID_Y, GRID_Z)
        self.stride = (GRID_Y * GRID_Z, GRID_Z, 1)
        self.position = lax.axis_index(AXIS)
        self.coords = tuple(
            self.position // self.stride[d] % self.counts[d] for d in range(3)
        )

        flips = self.coords[0] + self.coords[1] + self.coords[2] // 2 + self.coords[2]
        self.share_low = flips % 2 == 1

    def coord_of(self, device, dim):
        return device // self.stride[dim] % self.counts[dim]

    def swapped(self, low, high, dim, odd, raw=False, cross=1):
        count = self.counts[dim]
        pairs = []
        for i in range(self.devices):
            c = self.coord_of(i, dim)
            up = c % 2 == odd
            to = (c + (1 if up else -1)) % count
            pairs.append((i, (i + (to - c) * self.stride[dim]) ^ cross))
        lower = self.coords[dim] % 2 == odd
        arrived = lax.ppermute(jnp.where(lower, high, low), AXIS, pairs)
        if raw:
            return arrived
        zero = jnp.zeros_like(arrived)
        to_low, to_high = jnp.where(lower, zero, arrived), jnp.where(lower, arrived, zero)
        if odd or count % 2:
            to_low = jnp.where(self.coords[dim] > 0, to_low, zero)
            to_high = jnp.where(self.coords[dim] < count - 1, to_high, zero)
        return to_low, to_high

    def exchanged(self, low, high, dim, cross=1):
        to_low, to_high = self.swapped(low, high, dim, 0, cross=cross)
        if self.counts[dim] > 2:
            more_low, more_high = self.swapped(low, high, dim, 1, cross=cross)
            to_low, to_high = to_low + more_low, to_high + more_high
        return to_low, to_high

    def partner(self, value, bits):
        return lax.ppermute(value, AXIS, [(i, i ^ bits) for i in range(self.devices)])

    def has(self, bit):
        return (self.position & bit) != 0


FIRST, SECOND = 3, 1


def placed(near, high, low):
    near = [
        jnp.where(low, near[i ^ 1], near[i]) for i in range(GRID_Z)
    ]
    return [jnp.where(high, near[i ^ 2], near[i]) for i in range(GRID_Z)]


def packed(blocks):
    half = blocks[0].shape[0] // 2
    return jnp.concatenate([b[h : h + half] for h in (0, half) for b in blocks], axis=1)


def unpacked(value, width):
    return [
        jnp.concatenate([value[:, e : e + width] for e in (i * width, (i + 2) * width)], axis=0)
        for i in range(2)
    ]


def split(value, parts):
    width = value.shape[1] // parts
    return [value[:, i * width : (i + 1) * width] for i in range(parts)]


def to_shares(grid, block, other):
    shares = split(block, GRID_Z)
    width = shares[0].shape[1]
    high = grid.has(2)
    kept = [jnp.where(high, shares[2 + i], shares[i]) for i in range(2)]
    away = [jnp.where(high, shares[i], shares[2 + i]) for i in range(2)]
    came = unpacked(grid.partner(packed(away), FIRST), width)
    low = grid.share_low
    own = [jnp.where(low, kept[1], kept[0]), jnp.where(low, came[1], came[0])]
    away = [jnp.where(low, kept[0], kept[1]), jnp.where(low, came[0], came[1])]
    away, other = lax.optimization_barrier((packed(away), other))
    came = unpacked(grid.partner(away, SECOND), width)
    other = by_rows(grid.partner(other, SECOND))
    near = [own[0], came[0], came[1], own[1]]
    return jnp.concatenate(placed(near, high, grid.has(1)), axis=1), other


def by_rows(value):
    return with_layout_constraint(value, Layout(major_to_minor=tuple(range(value.ndim))))


def plane(field, dim, at):
    return lax.slice_in_dim(field, at, at + 1, axis=dim)


def with_ends(field, dim, low, high):
    last = field.shape[dim] - 1
    parts = [
        plane(field, dim, 0) if low is None else low,
        lax.slice_in_dim(field, 1, last, axis=dim),
        plane(field, dim, last) if high is None else high,
    ]
    return jnp.concatenate(parts, axis=dim)


def to_next_partition(value, width):
    kept = value[..., :-width]
    return jnp.concatenate([jnp.zeros_like(value[..., :width]), kept], axis=-1)


def to_previous_partition(value, width):
    kept = value[..., width:]
    return jnp.concatenate([kept, jnp.zeros_like(value[..., :width])], axis=-1)


def slots_matrix(cell_matrix, connectivity, potential):
    slots = jnp.arange(potential.shape[0], dtype=jnp.int32)
    total = jnp.where(slots[:, None] == slots[None, :], potential[:, None], 0.0)
    for c in range(cell_matrix.shape[0]):
        chosen = (connectivity[c][:, None] == slots[None, :]).astype(jnp.bfloat16)
        rows = lax.dot_general(
            chosen, cell_matrix[c], (((0,), (0,)), ((), ())), preferred_element_type=jnp.float32
        ).astype(jnp.bfloat16)
        total = total + jnp.dot(rows, chosen, preferred_element_type=jnp.float32)
    return total.astype(jnp.bfloat16)


def rounded(value):
    return lax.reduce_precision(value, 8, 7).astype(jnp.bfloat16)


def plus(first, second):
    return (first.astype(jnp.float32) + second.astype(jnp.float32)).astype(jnp.bfloat16)


def summed_along(grid, value, stride, count):
    factor = 2
    while count > 1:
        while count % factor:
            factor += 1
        at = grid.position // stride % factor
        terms = [value]
        for turn in range(1, factor):
            pairs = []
            for i in range(grid.devices):
                c = i // stride % factor
                pairs.append((i, i + ((c + turn) % factor - c) * stride))
            terms.append(lax.ppermute(value, AXIS, pairs))
        if factor == 2:
            value = plus(*terms)
        else:
            total = 0.0
            for k in range(factor):
                term = terms[0]
                for turn in range(1, factor):
                    term = jnp.where((at - turn) % factor == k, terms[turn], term)
                total = total + term.astype(jnp.float32)
            value = total.astype(jnp.bfloat16)
        count //= factor
        stride *= factor
    return value


def per_device(block, cell_matrix, connectivity, potential, locked):
    owned_rows, columns = block.shape
    slot_count = potential.shape[0]
    width = columns // GRID_Z
    edge = SIDE - 1
    grid = Grid()
    shape = (SIDE, SIDE, SIDE, columns)

    field = block.reshape(edge, edge, edge, columns)
    high = plane(field, 1, edge - 1)
    cell_matrix, high = lax.optimization_barrier((cell_matrix, high))
    matrix = by_rows(slots_matrix(cell_matrix, connectivity, potential))
    other = by_rows(grid.partner(matrix, FIRST))
    field = jnp.concatenate([grid.exchanged(high, high, 1, cross=0)[0], field], axis=1)

    high = field[edge - 1].reshape(SIDE * edge, columns)
    tiles = -(-locked.shape[1] // columns)
    top = jnp.pad(locked[-edge * edge :], ((0, 0), (0, -locked.shape[1] % columns)))
    top = jnp.concatenate(split(top, tiles), axis=0)
    sent = jnp.concatenate([top, high], axis=0)
    sent, matrix = lax.optimization_barrier((sent, matrix))
    arrived = grid.exchanged(sent, sent, 0, cross=0)[0]
    bottom = jnp.split(arrived[: top.shape[0]], tiles, axis=0)
    bottom = jnp.concatenate(bottom, axis=1)[:, : locked.shape[1]]
    locked = jnp.concatenate([bottom, locked], axis=0)
    field = jnp.concatenate(
        [arrived[top.shape[0] :].reshape(1, SIDE, edge, columns), field], axis=0
    )

    rows = field.reshape(SIDE * SIDE * edge, columns)
    second = by_rows(grid.partner(matrix, SECOND))
    mine, both = to_shares(grid, jnp.pad(rows, ((0, -rows.shape[0] % 16), (0, 0))), other)
    mine, both = lax.optimization_barrier((mine, both))
    matrices = [matrix, second, both, other]

    locked, mine = lax.optimization_barrier((locked, mine))
    parts = [locked[:128], locked[128:]]
    other_parts = [grid.partner(part, FIRST) for part in parts]
    field = mine[: rows.shape[0]].reshape(SIDE, SIDE, edge, columns)
    low = to_next_partition(plane(field, 2, edge - 1), width)
    field = jnp.concatenate([low, field], axis=2)

    lane_owner = lax.broadcasted_iota(jnp.int32, (1, columns), 1) // width
    owner_near = lane_owner ^ grid.coords[2]

    current = field
    older = lax.optimization_barrier(field)
    steps = len(chebyshev_coeffs)
    for step, coeffs in enumerate(chebyshev_coeffs):
        rows = current.reshape(slot_count, columns)
        partial = 0.0
        for r in range(GRID_Z):
            own = jnp.where(owner_near == r, rows, jnp.zeros_like(rows))
            partial = partial + jnp.dot(
                matrices[r], own, preferred_element_type=jnp.float32
            )
        partial = partial.reshape(shape)
        low, high = plane(partial, 2, 0), plane(partial, 2, SIDE - 1)
        partial = with_ends(
            partial,
            2,
            jnp.where(lane_owner > 0, low + to_next_partition(high, width), 0.0),
            high + to_previous_partition(low, width),
        )
        if step == steps - 1:
            break
        for dim in (1, 0):
            low, high = plane(partial, dim, 0), plane(partial, dim, SIDE - 1)
            low16, high16 = low.astype(jnp.bfloat16), high.astype(jnp.bfloat16)
            if step == 1:
                low16, other_parts[1 - dim] = lax.optimization_barrier(
                    (low16, other_parts[1 - dim])
                )
            to_low, to_high = grid.exchanged(low16, high16, dim)
            partial = with_ends(
                partial,
                dim,
                jnp.where(grid.coords[dim] > 0, low + to_low.astype(jnp.float32), 0.0),
                high + to_high.astype(jnp.float32),
            )
        following = coeffs[0] * (partial - centre * current.astype(jnp.float32)) - coeffs[
            1
        ] * older.astype(jnp.float32)
        following = rounded(following)
        older = lax.optimization_barrier(current)
        current = following
    other_locked = jnp.concatenate(other_parts, axis=0)
    both_locked = [grid.partner(l, SECOND) for l in (locked, other_locked)]
    low = plane(partial, 1, 0).astype(jnp.bfloat16)
    all_locked = [locked, both_locked[0], both_locked[1], other_locked]
    to_high = grid.exchanged(low, low, 1)[1].astype(jnp.float32)
    partial = with_ends(partial, 1, None, plane(partial, 1, SIDE - 1) + to_high)
    partial = coeffs[0] * partial[:, 1:, 1:].reshape(SIDE, edge * edge, columns)

    def owned(field):
        return field[1:, 1:, 1:].reshape(edge, edge * edge, columns).astype(jnp.float32)

    rest = -coeffs[0] * centre * owned(current) - coeffs[1] * owned(older)
    sums = jnp.concatenate([partial[:1], partial[1:] + rest], axis=0)
    weights = sums.astype(jnp.bfloat16).reshape(SIDE * edge * edge, columns)
    share = 0.0
    for r in range(GRID_Z):
        share = share + lax.dot_general(
            all_locked[r],
            jnp.where(owner_near == r, weights, jnp.zeros_like(weights)),
            (((0,), (0,)), ((), ())),
            preferred_element_type=jnp.float32,
        )
    share = sum(split(share, GRID_Z))
    deep = share.shape[0] // GRID_Z
    share = jnp.concatenate(
        [share[i * deep : (i + 1) * deep] for i in range(GRID_Z)], axis=1
    ).astype(jnp.bfloat16)

    low = sums[0].astype(jnp.bfloat16)
    stride, count = grid.stride[0], grid.counts[0]
    even = grid.coords[0] % 2 == 0
    arrived = grid.partner(jnp.concatenate([share, low], axis=0), stride | 1)
    share = plus(share, arrived[:deep])
    to_high = jnp.where(even, arrived[deep:], jnp.zeros_like(low))
    if count > 2:
        to_high = to_high + grid.swapped(low, low, 0, 1)[1]
    sums = jnp.concatenate(
        [sums[1:edge], sums[edge:] + to_high[None].astype(jnp.float32)], axis=0
    )
    filtered = rounded(sums.reshape(owned_rows, columns))

    share = plus(share, grid.swapped(share, share, 1, 0, True))
    share = plus(share, grid.swapped(share, share, 1, 1, True))
    share = summed_along(grid, share, stride * 2, count // 2)

    high, low = grid.has(2), grid.share_low
    near = placed(split(filtered, GRID_Z), high, grid.has(1))
    sent = jnp.concatenate([share, packed([near[3], near[2]])], axis=0)
    arrived = grid.partner(sent, FIRST)
    held = jnp.stack([share, arrived[:deep]])
    came = unpacked(arrived[deep:], width)
    own = [near[0], came[0]]
    away = [near[1], came[1]]
    sent = jnp.concatenate([held.reshape(-1, columns), packed(away)], axis=0)
    arrived = grid.partner(sent, SECOND)
    others = arrived[: 2 * deep].reshape(held.shape)
    came = unpacked(arrived[2 * deep :], width)
    filtered = jnp.concatenate(placed([own[0], came[0], own[1], came[1]], high, low), axis=1)
    held = placed([held[0], others[0], held[1], others[1]], high, low)
    intersection = jnp.concatenate(
        [
            jnp.concatenate([h[:, q * width : (q + 1) * width] for h in held], axis=1)
            for q in range(GRID_Z)
        ],
        axis=0,
    ).astype(jnp.float32)
    return filtered, intersection


def solution(mesh):
    in_specs = (
        P(AXIS, None),
        P(AXIS, None, None),
        P(AXIS, None),
        P(AXIS),
        P(AXIS, None),
    )
    out_specs = (P(AXIS, None), P())
    return jax.shard_map(
        per_device, mesh=mesh, in_specs=in_specs, out_specs=out_specs, check_vma=False
    )
```

```python
import jax
import jax.numpy as jnp
from jax import lax
from jax.experimental.layout import Layout, with_layout_constraint
from jax.sharding import PartitionSpec as P

GRID_Y = 4
GRID_Z = 4
SIDE = 7
AXIS = "cells"

chebyshev_coeffs = ((-1.0 / 7.0, 0.0), (-7.0 / 41.0, 8.0 / 41.0), (-41.0 / 259.0, 28.0 / 259.0))
centre = 6.0


class Grid:
    def __init__(self):
        self.devices = lax.axis_size(AXIS)
        self.counts = (self.devices // (GRID_Y * GRID_Z), GRID_Y, GRID_Z)
        self.stride = (GRID_Y * GRID_Z, GRID_Z, 1)
        self.position = lax.axis_index(AXIS)
        self.coords = tuple(
            self.position // self.stride[d] % self.counts[d] for d in range(3)
        )

        flips = self.coords[0] + self.coords[1] + self.coords[2] // 2 + self.coords[2]
        self.share_low = flips % 2 == 1

    def coord_of(self, device, dim):
        return device // self.stride[dim] % self.counts[dim]

    def swapped(self, low, high, dim, odd, raw=False, cross=1):
        count = self.counts[dim]
        pairs = []
        for i in range(self.devices):
            c = self.coord_of(i, dim)
            up = c % 2 == odd
            to = (c + (1 if up else -1)) % count
            pairs.append((i, (i + (to - c) * self.stride[dim]) ^ cross))
        lower = self.coords[dim] % 2 == odd
        arrived = lax.ppermute(jnp.where(lower, high, low), AXIS, pairs)
        if raw:
            return arrived
        zero = jnp.zeros_like(arrived)
        to_low, to_high = jnp.where(lower, zero, arrived), jnp.where(lower, arrived, zero)
        if odd or count % 2:
            to_low = jnp.where(self.coords[dim] > 0, to_low, zero)
            to_high = jnp.where(self.coords[dim] < count - 1, to_high, zero)
        return to_low, to_high

    def exchanged(self, low, high, dim, cross=1):
        to_low, to_high = self.swapped(low, high, dim, 0, cross=cross)
        if self.counts[dim] > 2:
            more_low, more_high = self.swapped(low, high, dim, 1, cross=cross)
            to_low, to_high = to_low + more_low, to_high + more_high
        return to_low, to_high

    def partner(self, value, bits):
        return lax.ppermute(value, AXIS, [(i, i ^ bits) for i in range(self.devices)])

    def has(self, bit):
        return (self.position & bit) != 0


FIRST, SECOND = 3, 1


def placed(near, high, low):
    near = [
        jnp.where(low, near[i ^ 1], near[i]) for i in range(GRID_Z)
    ]
    return [jnp.where(high, near[i ^ 2], near[i]) for i in range(GRID_Z)]


def packed(blocks):
    half = blocks[0].shape[0] // 2
    return jnp.concatenate([b[h : h + half] for h in (0, half) for b in blocks], axis=1)


def unpacked(value, width):
    return [
        jnp.concatenate([value[:, e : e + width] for e in (i * width, (i + 2) * width)], axis=0)
        for i in range(2)
    ]


def split(value, parts):
    width = value.shape[1] // parts
    return [value[:, i * width : (i + 1) * width] for i in range(parts)]


def to_shares(grid, block, other):
    shares = split(block, GRID_Z)
    width = shares[0].shape[1]
    high = grid.has(2)
    kept = [jnp.where(high, shares[2 + i], shares[i]) for i in range(2)]
    away = [jnp.where(high, shares[i], shares[2 + i]) for i in range(2)]
    came = unpacked(grid.partner(packed(away), FIRST), width)
    low = grid.share_low
    own = [jnp.where(low, kept[1], kept[0]), jnp.where(low, came[1], came[0])]
    away = [jnp.where(low, kept[0], kept[1]), jnp.where(low, came[0], came[1])]
    away, other = lax.optimization_barrier((packed(away), other))
    came = unpacked(grid.partner(away, SECOND), width)
    other = by_rows(grid.partner(other, SECOND))
    near = [own[0], came[0], came[1], own[1]]
    return jnp.concatenate(placed(near, high, grid.has(1)), axis=1), other


def by_rows(value):
    return with_layout_constraint(value, Layout(major_to_minor=tuple(range(value.ndim))))


def plane(field, dim, at):
    return lax.slice_in_dim(field, at, at + 1, axis=dim)


def with_ends(field, dim, low, high):
    last = field.shape[dim] - 1
    parts = [
        plane(field, dim, 0) if low is None else low,
        lax.slice_in_dim(field, 1, last, axis=dim),
        plane(field, dim, last) if high is None else high,
    ]
    return jnp.concatenate(parts, axis=dim)


def to_next_partition(value, width):
    kept = value[..., :-width]
    return jnp.concatenate([jnp.zeros_like(value[..., :width]), kept], axis=-1)


def to_previous_partition(value, width):
    kept = value[..., width:]
    return jnp.concatenate([kept, jnp.zeros_like(value[..., :width])], axis=-1)


def slots_matrix(cell_matrix, connectivity, potential):
    slots = jnp.arange(potential.shape[0], dtype=jnp.int32)
    total = jnp.where(slots[:, None] == slots[None, :], potential[:, None], 0.0)
    for c in range(cell_matrix.shape[0]):
        chosen = (connectivity[c][:, None] == slots[None, :]).astype(jnp.bfloat16)
        rows = lax.dot_general(
            chosen, cell_matrix[c], (((0,), (0,)), ((), ())), preferred_element_type=jnp.float32
        ).astype(jnp.bfloat16)
        total = total + jnp.dot(rows, chosen, preferred_element_type=jnp.float32)
    return total.astype(jnp.bfloat16)


def rounded(value):
    return lax.reduce_precision(value, 8, 7).astype(jnp.bfloat16)


def plus(first, second):
    return (first.astype(jnp.float32) + second.astype(jnp.float32)).astype(jnp.bfloat16)


def summed_along(grid, value, stride, count):
    factor = 2
    while count > 1:
        while count % factor:
            factor += 1
        at = grid.position // stride % factor
        terms = [value]
        for turn in range(1, factor):
            pairs = []
            for i in range(grid.devices):
                c = i // stride % factor
                pairs.append((i, i + ((c + turn) % factor - c) * stride))
            terms.append(lax.ppermute(value, AXIS, pairs))
        if factor == 2:
            value = plus(*terms)
        else:
            total = 0.0
            for k in range(factor):
                term = terms[0]
                for turn in range(1, factor):
                    term = jnp.where((at - turn) % factor == k, terms[turn], term)
                total = total + term.astype(jnp.float32)
            value = total.astype(jnp.bfloat16)
        count //= factor
        stride *= factor
    return value


def per_device(block, cell_matrix, connectivity, potential, locked):
    owned_rows, columns = block.shape
    slot_count = potential.shape[0]
    width = columns // GRID_Z
    edge = SIDE - 1
    grid = Grid()
    shape = (SIDE, SIDE, SIDE, columns)

    field = block.reshape(edge, edge, edge, columns)
    high = plane(field, 1, edge - 1)
    cell_matrix, high = lax.optimization_barrier((cell_matrix, high))
    matrix = by_rows(slots_matrix(cell_matrix, connectivity, potential))
    other = by_rows(grid.partner(matrix, FIRST))
    field = jnp.concatenate([grid.exchanged(high, high, 1, cross=0)[0], field], axis=1)

    high = field[edge - 1].reshape(SIDE * edge, columns)
    tiles = -(-locked.shape[1] // columns)
    top = jnp.pad(locked[-edge * edge :], ((0, 0), (0, -locked.shape[1] % columns)))
    top = jnp.concatenate(split(top, tiles), axis=0)
    sent = jnp.concatenate([top, high], axis=0)
    sent, matrix = lax.optimization_barrier((sent, matrix))
    arrived = grid.exchanged(sent, sent, 0, cross=0)[0]
    bottom = jnp.split(arrived[: top.shape[0]], tiles, axis=0)
    bottom = jnp.concatenate(bottom, axis=1)[:, : locked.shape[1]]
    other_locked = grid.partner(locked, FIRST)
    other_bottom = grid.partner(bottom, FIRST)
    field = jnp.concatenate(
        [arrived[top.shape[0] :].reshape(1, SIDE, edge, columns), field], axis=0
    )

    rows = field.reshape(SIDE * SIDE * edge, columns)
    second = by_rows(grid.partner(matrix, SECOND))
    mine, both = to_shares(grid, jnp.pad(rows, ((0, -rows.shape[0] % 16), (0, 0))), other)
    mine, both, other_locked = lax.optimization_barrier((mine, both, other_locked))
    matrices = [matrix, second, both, other]
    field = mine[: rows.shape[0]].reshape(SIDE, SIDE, edge, columns)
    low = to_next_partition(plane(field, 2, edge - 1), width)
    field = jnp.concatenate([low, field], axis=2)

    lane_owner = lax.broadcasted_iota(jnp.int32, (1, columns), 1) // width
    owner_near = lane_owner ^ grid.coords[2]

    current = field
    older = lax.optimization_barrier(field)
    steps = len(chebyshev_coeffs)
    for step, coeffs in enumerate(chebyshev_coeffs):
        rows = current.reshape(slot_count, columns)
        partial = 0.0
        for r in range(GRID_Z):
            own = jnp.where(owner_near == r, rows, jnp.zeros_like(rows))
            partial = partial + jnp.dot(
                matrices[r], own, preferred_element_type=jnp.float32
            )
        partial = partial.reshape(shape)
        low, high = plane(partial, 2, 0), plane(partial, 2, SIDE - 1)
        partial = with_ends(
            partial,
            2,
            jnp.where(lane_owner > 0, low + to_next_partition(high, width), 0.0),
            high + to_previous_partition(low, width),
        )
        if step == steps - 1:
            break
        for dim in (1, 0):
            low, high = plane(partial, dim, 0), plane(partial, dim, SIDE - 1)
            low16, high16 = low.astype(jnp.bfloat16), high.astype(jnp.bfloat16)
            if (step, dim) == (1, 1):
                low16, other_bottom = lax.optimization_barrier((low16, other_bottom))
            to_low, to_high = grid.exchanged(low16, high16, dim)
            partial = with_ends(
                partial,
                dim,
                jnp.where(grid.coords[dim] > 0, low + to_low.astype(jnp.float32), 0.0),
                high + to_high.astype(jnp.float32),
            )
        following = coeffs[0] * (partial - centre * current.astype(jnp.float32)) - coeffs[
            1
        ] * older.astype(jnp.float32)
        following = rounded(following)
        older = lax.optimization_barrier(current)
        current = following
    locked = jnp.concatenate([bottom, locked], axis=0)
    other_locked = jnp.concatenate([other_bottom, other_locked], axis=0)
    both_locked = [grid.partner(l, SECOND) for l in (locked, other_locked)]
    low = plane(partial, 1, 0).astype(jnp.bfloat16)
    all_locked = [locked, both_locked[0], both_locked[1], other_locked]
    to_high = grid.exchanged(low, low, 1)[1].astype(jnp.float32)
    partial = with_ends(partial, 1, None, plane(partial, 1, SIDE - 1) + to_high)
    partial = coeffs[0] * partial[:, 1:, 1:].reshape(SIDE, edge * edge, columns)

    def owned(field):
        return field[1:, 1:, 1:].reshape(edge, edge * edge, columns).astype(jnp.float32)

    rest = -coeffs[0] * centre * owned(current) - coeffs[1] * owned(older)
    sums = jnp.concatenate([partial[:1], partial[1:] + rest], axis=0)
    weights = sums.astype(jnp.bfloat16).reshape(SIDE * edge * edge, columns)
    share = 0.0
    for r in range(GRID_Z):
        share = share + lax.dot_general(
            all_locked[r],
            jnp.where(owner_near == r, weights, jnp.zeros_like(weights)),
            (((0,), (0,)), ((), ())),
            preferred_element_type=jnp.float32,
        )
    share = sum(split(share, GRID_Z))
    deep = share.shape[0] // GRID_Z
    share = jnp.concatenate(
        [share[i * deep : (i + 1) * deep] for i in range(GRID_Z)], axis=1
    ).astype(jnp.bfloat16)

    low = sums[0].astype(jnp.bfloat16)
    stride, count = grid.stride[0], grid.counts[0]
    even = grid.coords[0] % 2 == 0
    arrived = grid.partner(jnp.concatenate([share, low], axis=0), stride | 1)
    share = plus(share, arrived[:deep])
    to_high = jnp.where(even, arrived[deep:], jnp.zeros_like(low))
    if count > 2:
        to_high = to_high + grid.swapped(low, low, 0, 1)[1]
    sums = jnp.concatenate(
        [sums[1:edge], sums[edge:] + to_high[None].astype(jnp.float32)], axis=0
    )
    filtered = rounded(sums.reshape(owned_rows, columns))

    share = plus(share, grid.swapped(share, share, 1, 0, True))
    share = plus(share, grid.swapped(share, share, 1, 1, True))
    share = summed_along(grid, share, stride * 2, count // 2)

    high, low = grid.has(2), grid.share_low
    near = placed(split(filtered, GRID_Z), high, grid.has(1))
    sent = jnp.concatenate([share, packed([near[3], near[2]])], axis=0)
    arrived = grid.partner(sent, FIRST)
    held = jnp.stack([share, arrived[:deep]])
    came = unpacked(arrived[deep:], width)
    own = [near[0], came[0]]
    away = [near[1], came[1]]
    sent = jnp.concatenate([held.reshape(-1, columns), packed(away)], axis=0)
    arrived = grid.partner(sent, SECOND)
    others = arrived[: 2 * deep].reshape(held.shape)
    came = unpacked(arrived[2 * deep :], width)
    filtered = jnp.concatenate(placed([own[0], came[0], own[1], came[1]], high, low), axis=1)
    held = placed([held[0], others[0], held[1], others[1]], high, low)
    intersection = jnp.concatenate(
        [
            jnp.concatenate([h[:, q * width : (q + 1) * width] for h in held], axis=1)
            for q in range(GRID_Z)
        ],
        axis=0,
    ).astype(jnp.float32)
    return filtered, intersection


def solution(mesh):
    in_specs = (
        P(AXIS, None),
        P(AXIS, None, None),
        P(AXIS, None),
        P(AXIS),
        P(AXIS, None),
    )
    out_specs = (P(AXIS, None), P())
    return jax.shard_map(
        per_device, mesh=mesh, in_specs=in_specs, out_specs=out_specs, check_vma=False
    )
```

```python
import jax
import jax.numpy as jnp
from jax import lax
from jax.experimental.layout import Layout, with_layout_constraint
from jax.sharding import PartitionSpec as P

GRID_Y = 4
GRID_Z = 4
SIDE = 7
AXIS = "cells"

chebyshev_coeffs = ((-1.0 / 7.0, 0.0), (-7.0 / 41.0, 8.0 / 41.0), (-41.0 / 259.0, 28.0 / 259.0))
centre = 6.0


class Grid:
    def __init__(self):
        self.devices = lax.axis_size(AXIS)
        self.counts = (self.devices // (GRID_Y * GRID_Z), GRID_Y, GRID_Z)
        self.stride = (GRID_Y * GRID_Z, GRID_Z, 1)
        self.position = lax.axis_index(AXIS)
        self.coords = tuple(
            self.position // self.stride[d] % self.counts[d] for d in range(3)
        )

        flips = self.coords[0] + self.coords[1] + self.coords[2] // 2 + self.coords[2]
        self.share_low = flips % 2 == 1

    def coord_of(self, device, dim):
        return device // self.stride[dim] % self.counts[dim]

    def swapped(self, low, high, dim, odd, raw=False, cross=1):
        count = self.counts[dim]
        pairs = []
        for i in range(self.devices):
            c = self.coord_of(i, dim)
            up = c % 2 == odd
            to = (c + (1 if up else -1)) % count
            pairs.append((i, (i + (to - c) * self.stride[dim]) ^ cross))
        lower = self.coords[dim] % 2 == odd
        arrived = lax.ppermute(jnp.where(lower, high, low), AXIS, pairs)
        if raw:
            return arrived
        zero = jnp.zeros_like(arrived)
        to_low, to_high = jnp.where(lower, zero, arrived), jnp.where(lower, arrived, zero)
        if odd or count % 2:
            to_low = jnp.where(self.coords[dim] > 0, to_low, zero)
            to_high = jnp.where(self.coords[dim] < count - 1, to_high, zero)
        return to_low, to_high

    def exchanged(self, low, high, dim, cross=1):
        to_low, to_high = self.swapped(low, high, dim, 0, cross=cross)
        if self.counts[dim] > 2:
            more_low, more_high = self.swapped(low, high, dim, 1, cross=cross)
            to_low, to_high = to_low + more_low, to_high + more_high
        return to_low, to_high

    def partner(self, value, bits):
        return lax.ppermute(value, AXIS, [(i, i ^ bits) for i in range(self.devices)])

    def has(self, bit):
        return (self.position & bit) != 0


FIRST, SECOND = 3, 1


def placed(near, high, low):
    near = [
        jnp.where(low, near[i ^ 1], near[i]) for i in range(GRID_Z)
    ]
    return [jnp.where(high, near[i ^ 2], near[i]) for i in range(GRID_Z)]


def packed(blocks):
    half = blocks[0].shape[0] // 2
    return jnp.concatenate([b[h : h + half] for h in (0, half) for b in blocks], axis=1)


def unpacked(value, width):
    return [
        jnp.concatenate([value[:, e : e + width] for e in (i * width, (i + 2) * width)], axis=0)
        for i in range(2)
    ]


def split(value, parts):
    width = value.shape[1] // parts
    return [value[:, i * width : (i + 1) * width] for i in range(parts)]


def to_shares(grid, block, other):
    shares = split(block, GRID_Z)
    width = shares[0].shape[1]
    high = grid.has(2)
    kept = [jnp.where(high, shares[2 + i], shares[i]) for i in range(2)]
    away = [jnp.where(high, shares[i], shares[2 + i]) for i in range(2)]
    came = unpacked(grid.partner(packed(away), FIRST), width)
    low = grid.share_low
    own = [jnp.where(low, kept[1], kept[0]), jnp.where(low, came[1], came[0])]
    away = [jnp.where(low, kept[0], kept[1]), jnp.where(low, came[0], came[1])]
    away, other = lax.optimization_barrier((packed(away), other))
    came = unpacked(grid.partner(away, SECOND), width)
    other = by_rows(grid.partner(other, SECOND))
    near = [own[0], came[0], came[1], own[1]]
    return jnp.concatenate(placed(near, high, grid.has(1)), axis=1), other


def by_rows(value):
    return with_layout_constraint(value, Layout(major_to_minor=tuple(range(value.ndim))))


def plane(field, dim, at):
    return lax.slice_in_dim(field, at, at + 1, axis=dim)


def with_ends(field, dim, low, high):
    last = field.shape[dim] - 1
    parts = [
        plane(field, dim, 0) if low is None else low,
        lax.slice_in_dim(field, 1, last, axis=dim),
        plane(field, dim, last) if high is None else high,
    ]
    return jnp.concatenate(parts, axis=dim)


def to_next_partition(value, width):
    kept = value[..., :-width]
    return jnp.concatenate([jnp.zeros_like(value[..., :width]), kept], axis=-1)


def to_previous_partition(value, width):
    kept = value[..., width:]
    return jnp.concatenate([kept, jnp.zeros_like(value[..., :width])], axis=-1)


def slots_matrix(cell_matrix, connectivity, potential):
    slots = jnp.arange(potential.shape[0], dtype=jnp.int32)
    total = jnp.where(slots[:, None] == slots[None, :], potential[:, None], 0.0)
    for c in range(cell_matrix.shape[0]):
        chosen = (connectivity[c][:, None] == slots[None, :]).astype(jnp.bfloat16)
        rows = lax.dot_general(
            chosen, cell_matrix[c], (((0,), (0,)), ((), ())), preferred_element_type=jnp.float32
        ).astype(jnp.bfloat16)
        total = total + jnp.dot(rows, chosen, preferred_element_type=jnp.float32)
    return total.astype(jnp.bfloat16)


def rounded(value):
    return lax.reduce_precision(value, 8, 7).astype(jnp.bfloat16)


def plus(first, second):
    return (first.astype(jnp.float32) + second.astype(jnp.float32)).astype(jnp.bfloat16)


def summed_along(grid, value, stride, count):
    factor = 2
    while count > 1:
        while count % factor:
            factor += 1
        at = grid.position // stride % factor
        terms = [value]
        for turn in range(1, factor):
            pairs = []
            for i in range(grid.devices):
                c = i // stride % factor
                pairs.append((i, i + ((c + turn) % factor - c) * stride))
            terms.append(lax.ppermute(value, AXIS, pairs))
        if factor == 2:
            value = plus(*terms)
        else:
            total = 0.0
            for k in range(factor):
                term = terms[0]
                for turn in range(1, factor):
                    term = jnp.where((at - turn) % factor == k, terms[turn], term)
                total = total + term.astype(jnp.float32)
            value = total.astype(jnp.bfloat16)
        count //= factor
        stride *= factor
    return value


def per_device(block, cell_matrix, connectivity, potential, locked):
    owned_rows, columns = block.shape
    slot_count = potential.shape[0]
    width = columns // GRID_Z
    edge = SIDE - 1
    grid = Grid()
    shape = (SIDE, SIDE, SIDE, columns)

    field = block.reshape(edge, edge, edge, columns)
    high = plane(field, 1, edge - 1)
    cell_matrix, high = lax.optimization_barrier((cell_matrix, high))
    matrix = by_rows(slots_matrix(cell_matrix, connectivity, potential))
    other = by_rows(grid.partner(matrix, FIRST))
    field = jnp.concatenate([grid.exchanged(high, high, 1, cross=0)[0], field], axis=1)

    high = field[edge - 1].reshape(SIDE * edge, columns)
    tiles = -(-locked.shape[1] // columns)
    top = jnp.pad(locked[-edge * edge :], ((0, 0), (0, -locked.shape[1] % columns)))
    top = jnp.concatenate(split(top, tiles), axis=0)
    sent = jnp.concatenate([top, high], axis=0)
    sent, matrix = lax.optimization_barrier((sent, matrix))
    arrived = grid.exchanged(sent, sent, 0, cross=0)[0]
    bottom = jnp.split(arrived[: top.shape[0]], tiles, axis=0)
    bottom = jnp.concatenate(bottom, axis=1)[:, : locked.shape[1]]
    cut = max(0, 128 - bottom.shape[0])
    other_late = grid.partner(jnp.concatenate([bottom, locked[:cut]], axis=0), FIRST)
    other_early = grid.partner(locked[cut:], FIRST)
    field = jnp.concatenate(
        [arrived[top.shape[0] :].reshape(1, SIDE, edge, columns), field], axis=0
    )

    rows = field.reshape(SIDE * SIDE * edge, columns)
    second = by_rows(grid.partner(matrix, SECOND))
    mine, both = to_shares(grid, jnp.pad(rows, ((0, -rows.shape[0] % 16), (0, 0))), other)
    mine, both, other_early = lax.optimization_barrier((mine, both, other_early))
    matrices = [matrix, second, both, other]
    field = mine[: rows.shape[0]].reshape(SIDE, SIDE, edge, columns)
    low = to_next_partition(plane(field, 2, edge - 1), width)
    field = jnp.concatenate([low, field], axis=2)

    lane_owner = lax.broadcasted_iota(jnp.int32, (1, columns), 1) // width
    owner_near = lane_owner ^ grid.coords[2]

    current = field
    older = lax.optimization_barrier(field)
    steps = len(chebyshev_coeffs)
    for step, coeffs in enumerate(chebyshev_coeffs):
        rows = current.reshape(slot_count, columns)
        partial = 0.0
        for r in range(GRID_Z):
            own = jnp.where(owner_near == r, rows, jnp.zeros_like(rows))
            partial = partial + jnp.dot(
                matrices[r], own, preferred_element_type=jnp.float32
            )
        partial = partial.reshape(shape)
        low, high = plane(partial, 2, 0), plane(partial, 2, SIDE - 1)
        partial = with_ends(
            partial,
            2,
            jnp.where(lane_owner > 0, low + to_next_partition(high, width), 0.0),
            high + to_previous_partition(low, width),
        )
        if step == steps - 1:
            break
        for dim in (1, 0):
            low, high = plane(partial, dim, 0), plane(partial, dim, SIDE - 1)
            low16, high16 = low.astype(jnp.bfloat16), high.astype(jnp.bfloat16)
            to_low, to_high = grid.exchanged(low16, high16, dim)
            partial = with_ends(
                partial,
                dim,
                jnp.where(grid.coords[dim] > 0, low + to_low.astype(jnp.float32), 0.0),
                high + to_high.astype(jnp.float32),
            )
        following = coeffs[0] * (partial - centre * current.astype(jnp.float32)) - coeffs[
            1
        ] * older.astype(jnp.float32)
        following = rounded(following)
        older = lax.optimization_barrier(current)
        current = following
    locked = jnp.concatenate([bottom, locked], axis=0)
    other_locked = jnp.concatenate([other_late, other_early], axis=0)
    both_locked = [grid.partner(l, SECOND) for l in (locked, other_locked)]
    low = plane(partial, 1, 0).astype(jnp.bfloat16)
    all_locked = [locked, both_locked[0], both_locked[1], other_locked]
    to_high = grid.exchanged(low, low, 1)[1].astype(jnp.float32)
    partial = with_ends(partial, 1, None, plane(partial, 1, SIDE - 1) + to_high)
    partial = coeffs[0] * partial[:, 1:, 1:].reshape(SIDE, edge * edge, columns)

    def owned(field):
        return field[1:, 1:, 1:].reshape(edge, edge * edge, columns).astype(jnp.float32)

    rest = -coeffs[0] * centre * owned(current) - coeffs[1] * owned(older)
    sums = jnp.concatenate([partial[:1], partial[1:] + rest], axis=0)
    weights = sums.astype(jnp.bfloat16).reshape(SIDE * edge * edge, columns)
    share = 0.0
    for r in range(GRID_Z):
        share = share + lax.dot_general(
            all_locked[r],
            jnp.where(owner_near == r, weights, jnp.zeros_like(weights)),
            (((0,), (0,)), ((), ())),
            preferred_element_type=jnp.float32,
        )
    share = sum(split(share, GRID_Z))
    deep = share.shape[0] // GRID_Z
    share = jnp.concatenate(
        [share[i * deep : (i + 1) * deep] for i in range(GRID_Z)], axis=1
    ).astype(jnp.bfloat16)

    low = sums[0].astype(jnp.bfloat16)
    stride, count = grid.stride[0], grid.counts[0]
    even = grid.coords[0] % 2 == 0
    arrived = grid.partner(jnp.concatenate([share, low], axis=0), stride | 1)
    share = plus(share, arrived[:deep])
    to_high = jnp.where(even, arrived[deep:], jnp.zeros_like(low))
    if count > 2:
        to_high = to_high + grid.swapped(low, low, 0, 1)[1]
    sums = jnp.concatenate(
        [sums[1:edge], sums[edge:] + to_high[None].astype(jnp.float32)], axis=0
    )
    filtered = rounded(sums.reshape(owned_rows, columns))

    share = plus(share, grid.swapped(share, share, 1, 0, True))
    share = plus(share, grid.swapped(share, share, 1, 1, True))
    share = summed_along(grid, share, stride * 2, count // 2)

    high, low = grid.has(2), grid.share_low
    near = placed(split(filtered, GRID_Z), high, grid.has(1))
    sent = jnp.concatenate([share, packed([near[3], near[2]])], axis=0)
    arrived = grid.partner(sent, FIRST)
    held = jnp.stack([share, arrived[:deep]])
    came = unpacked(arrived[deep:], width)
    own = [near[0], came[0]]
    away = [near[1], came[1]]
    sent = jnp.concatenate([held.reshape(-1, columns), packed(away)], axis=0)
    arrived = grid.partner(sent, SECOND)
    others = arrived[: 2 * deep].reshape(held.shape)
    came = unpacked(arrived[2 * deep :], width)
    filtered = jnp.concatenate(placed([own[0], came[0], own[1], came[1]], high, low), axis=1)
    held = placed([held[0], others[0], held[1], others[1]], high, low)
    intersection = jnp.concatenate(
        [
            jnp.concatenate([h[:, q * width : (q + 1) * width] for h in held], axis=1)
            for q in range(GRID_Z)
        ],
        axis=0,
    ).astype(jnp.float32)
    return filtered, intersection


def solution(mesh):
    in_specs = (
        P(AXIS, None),
        P(AXIS, None, None),
        P(AXIS, None),
        P(AXIS),
        P(AXIS, None),
    )
    out_specs = (P(AXIS, None), P())
    return jax.shard_map(
        per_device, mesh=mesh, in_specs=in_specs, out_specs=out_specs, check_vma=False
    )
```

```python
import jax
import jax.numpy as jnp
from jax import lax
from jax.experimental.layout import Layout, with_layout_constraint
from jax.sharding import PartitionSpec as P

GRID_Y = 4
GRID_Z = 4
SIDE = 7
AXIS = "cells"

chebyshev_coeffs = ((-1.0 / 7.0, 0.0), (-7.0 / 41.0, 8.0 / 41.0), (-41.0 / 259.0, 28.0 / 259.0))
centre = 6.0


class Grid:
    def __init__(self):
        self.devices = lax.axis_size(AXIS)
        self.counts = (self.devices // (GRID_Y * GRID_Z), GRID_Y, GRID_Z)
        self.stride = (GRID_Y * GRID_Z, GRID_Z, 1)
        self.position = lax.axis_index(AXIS)
        self.coords = tuple(
            self.position // self.stride[d] % self.counts[d] for d in range(3)
        )

        flips = self.coords[0] + self.coords[1] + self.coords[2] // 2 + self.coords[2]
        self.share_low = flips % 2 == 1

    def coord_of(self, device, dim):
        return device // self.stride[dim] % self.counts[dim]

    def swapped(self, low, high, dim, odd, raw=False, cross=1):
        count = self.counts[dim]
        pairs = []
        for i in range(self.devices):
            c = self.coord_of(i, dim)
            up = c % 2 == odd
            to = (c + (1 if up else -1)) % count
            pairs.append((i, (i + (to - c) * self.stride[dim]) ^ cross))
        lower = self.coords[dim] % 2 == odd
        arrived = lax.ppermute(jnp.where(lower, high, low), AXIS, pairs)
        if raw:
            return arrived
        zero = jnp.zeros_like(arrived)
        to_low, to_high = jnp.where(lower, zero, arrived), jnp.where(lower, arrived, zero)
        if odd or count % 2:
            to_low = jnp.where(self.coords[dim] > 0, to_low, zero)
            to_high = jnp.where(self.coords[dim] < count - 1, to_high, zero)
        return to_low, to_high

    def exchanged(self, low, high, dim, cross=1):
        to_low, to_high = self.swapped(low, high, dim, 0, cross=cross)
        if self.counts[dim] > 2:
            more_low, more_high = self.swapped(low, high, dim, 1, cross=cross)
            to_low, to_high = to_low + more_low, to_high + more_high
        return to_low, to_high

    def partner(self, value, bits):
        return lax.ppermute(value, AXIS, [(i, i ^ bits) for i in range(self.devices)])

    def has(self, bit):
        return (self.position & bit) != 0


FIRST, SECOND = 3, 1


def placed(near, high, low):
    near = [
        jnp.where(low, near[i ^ 1], near[i]) for i in range(GRID_Z)
    ]
    return [jnp.where(high, near[i ^ 2], near[i]) for i in range(GRID_Z)]


def packed(blocks):
    half = blocks[0].shape[0] // 2
    return jnp.concatenate([b[h : h + half] for h in (0, half) for b in blocks], axis=1)


def unpacked(value, width):
    return [
        jnp.concatenate([value[:, e : e + width] for e in (i * width, (i + 2) * width)], axis=0)
        for i in range(2)
    ]


def split(value, parts):
    width = value.shape[1] // parts
    return [value[:, i * width : (i + 1) * width] for i in range(parts)]


def to_shares(grid, block, other):
    shares = split(block, GRID_Z)
    width = shares[0].shape[1]
    high = grid.has(2)
    kept = [jnp.where(high, shares[2 + i], shares[i]) for i in range(2)]
    away = [jnp.where(high, shares[i], shares[2 + i]) for i in range(2)]
    came = unpacked(grid.partner(packed(away), FIRST), width)
    low = grid.share_low
    own = [jnp.where(low, kept[1], kept[0]), jnp.where(low, came[1], came[0])]
    away = [jnp.where(low, kept[0], kept[1]), jnp.where(low, came[0], came[1])]
    away, other = lax.optimization_barrier((packed(away), other))
    came = unpacked(grid.partner(away, SECOND), width)
    other = by_rows(grid.partner(other, SECOND))
    near = [own[0], came[0], came[1], own[1]]
    return jnp.concatenate(placed(near, high, grid.has(1)), axis=1), other


def by_rows(value):
    return with_layout_constraint(value, Layout(major_to_minor=tuple(range(value.ndim))))


def plane(field, dim, at):
    return lax.slice_in_dim(field, at, at + 1, axis=dim)


def with_ends(field, dim, low, high):
    last = field.shape[dim] - 1
    parts = [
        plane(field, dim, 0) if low is None else low,
        lax.slice_in_dim(field, 1, last, axis=dim),
        plane(field, dim, last) if high is None else high,
    ]
    return jnp.concatenate(parts, axis=dim)


def to_next_partition(value, width):
    kept = value[..., :-width]
    return jnp.concatenate([jnp.zeros_like(value[..., :width]), kept], axis=-1)


def to_previous_partition(value, width):
    kept = value[..., width:]
    return jnp.concatenate([kept, jnp.zeros_like(value[..., :width])], axis=-1)


def slots_matrix(cell_matrix, connectivity, potential):
    slots = jnp.arange(potential.shape[0], dtype=jnp.int32)
    total = jnp.where(slots[:, None] == slots[None, :], potential[:, None], 0.0)
    for c in range(cell_matrix.shape[0]):
        chosen = (connectivity[c][:, None] == slots[None, :]).astype(jnp.bfloat16)
        rows = lax.dot_general(
            chosen, cell_matrix[c], (((0,), (0,)), ((), ())), preferred_element_type=jnp.float32
        ).astype(jnp.bfloat16)
        total = total + jnp.dot(rows, chosen, preferred_element_type=jnp.float32)
    return total.astype(jnp.bfloat16)


def rounded(value):
    return lax.reduce_precision(value, 8, 7).astype(jnp.bfloat16)


def plus(first, second):
    return (first.astype(jnp.float32) + second.astype(jnp.float32)).astype(jnp.bfloat16)


def summed_along(grid, value, stride, count):
    factor = 2
    while count > 1:
        while count % factor:
            factor += 1
        at = grid.position // stride % factor
        terms = [value]
        for turn in range(1, factor):
            pairs = []
            for i in range(grid.devices):
                c = i // stride % factor
                pairs.append((i, i + ((c + turn) % factor - c) * stride))
            terms.append(lax.ppermute(value, AXIS, pairs))
        if factor == 2:
            value = plus(*terms)
        else:
            total = 0.0
            for k in range(factor):
                term = terms[0]
                for turn in range(1, factor):
                    term = jnp.where((at - turn) % factor == k, terms[turn], term)
                total = total + term.astype(jnp.float32)
            value = total.astype(jnp.bfloat16)
        count //= factor
        stride *= factor
    return value


def per_device(block, cell_matrix, connectivity, potential, locked):
    owned_rows, columns = block.shape
    slot_count = potential.shape[0]
    width = columns // GRID_Z
    edge = SIDE - 1
    grid = Grid()
    shape = (SIDE, SIDE, SIDE, columns)

    field = block.reshape(edge, edge, edge, columns)
    high = plane(field, 1, edge - 1)
    cell_matrix, high = lax.optimization_barrier((cell_matrix, high))
    matrix = by_rows(slots_matrix(cell_matrix, connectivity, potential))
    other = by_rows(grid.partner(matrix, FIRST))
    field = jnp.concatenate([grid.exchanged(high, high, 1, cross=0)[0], field], axis=1)

    high = plane(field, 0, edge - 1)
    high, matrix = lax.optimization_barrier((high, matrix))
    field = jnp.concatenate([grid.exchanged(high, high, 0, cross=0)[0], field], axis=0)
    top = by_rows(locked[-edge * edge :])
    bottom = by_rows(grid.exchanged(top, top, 0, cross=0)[0])

    cut = max(0, 128 - bottom.shape[0])
    other_late = grid.partner(jnp.concatenate([bottom, locked[:cut]], axis=0), FIRST)
    other_early = grid.partner(locked[cut:], FIRST)

    rows = field.reshape(SIDE * SIDE * edge, columns)
    second = by_rows(grid.partner(matrix, SECOND))
    mine, both = to_shares(grid, jnp.pad(rows, ((0, -rows.shape[0] % 16), (0, 0))), other)
    mine, both, other_early = lax.optimization_barrier((mine, both, other_early))
    matrices = [matrix, second, both, other]
    field = mine[: rows.shape[0]].reshape(SIDE, SIDE, edge, columns)
    low = to_next_partition(plane(field, 2, edge - 1), width)
    field = jnp.concatenate([low, field], axis=2)

    lane_owner = lax.broadcasted_iota(jnp.int32, (1, columns), 1) // width
    owner_near = lane_owner ^ grid.coords[2]

    current = field
    older = lax.optimization_barrier(field)
    steps = len(chebyshev_coeffs)
    for step, coeffs in enumerate(chebyshev_coeffs):
        rows = current.reshape(slot_count, columns)
        partial = 0.0
        for r in range(GRID_Z):
            own = jnp.where(owner_near == r, rows, jnp.zeros_like(rows))
            partial = partial + jnp.dot(
                matrices[r], own, preferred_element_type=jnp.float32
            )
        partial = partial.reshape(shape)
        low, high = plane(partial, 2, 0), plane(partial, 2, SIDE - 1)
        partial = with_ends(
            partial,
            2,
            jnp.where(lane_owner > 0, low + to_next_partition(high, width), 0.0),
            high + to_previous_partition(low, width),
        )
        if step == steps - 1:
            break
        for dim in (1, 0):
            low, high = plane(partial, dim, 0), plane(partial, dim, SIDE - 1)
            low16, high16 = low.astype(jnp.bfloat16), high.astype(jnp.bfloat16)
            to_low, to_high = grid.exchanged(low16, high16, dim)
            partial = with_ends(
                partial,
                dim,
                jnp.where(grid.coords[dim] > 0, low + to_low.astype(jnp.float32), 0.0),
                high + to_high.astype(jnp.float32),
            )
        following = coeffs[0] * (partial - centre * current.astype(jnp.float32)) - coeffs[
            1
        ] * older.astype(jnp.float32)
        following = rounded(following)
        older = lax.optimization_barrier(current)
        current = following
    locked = lax.optimization_barrier(jnp.concatenate([bottom, locked], axis=0))
    other_locked = jnp.concatenate([other_late, other_early], axis=0)
    both_locked = [grid.partner(l, SECOND) for l in (locked, other_locked)]
    low = plane(partial, 1, 0).astype(jnp.bfloat16)
    all_locked = [locked, both_locked[0], both_locked[1], other_locked]
    to_high = grid.exchanged(low, low, 1)[1].astype(jnp.float32)
    partial = with_ends(partial, 1, None, plane(partial, 1, SIDE - 1) + to_high)
    partial = coeffs[0] * partial[:, 1:, 1:].reshape(SIDE, edge * edge, columns)

    def owned(field):
        return field[1:, 1:, 1:].reshape(edge, edge * edge, columns).astype(jnp.float32)

    rest = -coeffs[0] * centre * owned(current) - coeffs[1] * owned(older)
    sums = jnp.concatenate([partial[:1], partial[1:] + rest], axis=0)
    weights = sums.astype(jnp.bfloat16).reshape(SIDE * edge * edge, columns)
    share = 0.0
    for r in range(GRID_Z):
        share = share + lax.dot_general(
            all_locked[r],
            jnp.where(owner_near == r, weights, jnp.zeros_like(weights)),
            (((0,), (0,)), ((), ())),
            preferred_element_type=jnp.float32,
        )
    share = sum(split(share, GRID_Z))
    deep = share.shape[0] // GRID_Z
    share = jnp.concatenate(
        [share[i * deep : (i + 1) * deep] for i in range(GRID_Z)], axis=1
    ).astype(jnp.bfloat16)

    low = sums[0].astype(jnp.bfloat16)
    stride, count = grid.stride[0], grid.counts[0]
    even = grid.coords[0] % 2 == 0
    arrived = grid.partner(jnp.concatenate([share, low], axis=0), stride | 1)
    share = plus(share, arrived[:deep])
    to_high = jnp.where(even, arrived[deep:], jnp.zeros_like(low))
    if count > 2:
        to_high = to_high + grid.swapped(low, low, 0, 1)[1]
    sums = jnp.concatenate(
        [sums[1:edge], sums[edge:] + to_high[None].astype(jnp.float32)], axis=0
    )
    filtered = rounded(sums.reshape(owned_rows, columns))

    share = plus(share, grid.swapped(share, share, 1, 0, True))
    share = plus(share, grid.swapped(share, share, 1, 1, True))
    share = summed_along(grid, share, stride * 2, count // 2)

    high, low = grid.has(2), grid.share_low
    near = placed(split(filtered, GRID_Z), high, grid.has(1))
    sent = jnp.concatenate([share, packed([near[3], near[2]])], axis=0)
    arrived = grid.partner(sent, FIRST)
    held = jnp.stack([share, arrived[:deep]])
    came = unpacked(arrived[deep:], width)
    own = [near[0], came[0]]
    away = [near[1], came[1]]
    sent = jnp.concatenate([held.reshape(-1, columns), packed(away)], axis=0)
    arrived = grid.partner(sent, SECOND)
    others = arrived[: 2 * deep].reshape(held.shape)
    came = unpacked(arrived[2 * deep :], width)
    filtered = jnp.concatenate(placed([own[0], came[0], own[1], came[1]], high, low), axis=1)
    held = placed([held[0], others[0], held[1], others[1]], high, low)
    intersection = jnp.concatenate(
        [
            jnp.concatenate([h[:, q * width : (q + 1) * width] for h in held], axis=1)
            for q in range(GRID_Z)
        ],
        axis=0,
    ).astype(jnp.float32)
    return filtered, intersection


def solution(mesh):
    in_specs = (
        P(AXIS, None),
        P(AXIS, None, None),
        P(AXIS, None),
        P(AXIS),
        P(AXIS, None),
    )
    out_specs = (P(AXIS, None), P())
    return jax.shard_map(
        per_device, mesh=mesh, in_specs=in_specs, out_specs=out_specs, check_vma=False
    )
```

```python
import jax
import jax.numpy as jnp
from jax import lax
from jax.experimental.layout import Layout, with_layout_constraint
from jax.sharding import PartitionSpec as P

GRID_Y = 4
GRID_Z = 4
SIDE = 7
AXIS = "cells"

chebyshev_coeffs = ((-1.0 / 7.0, 0.0), (-7.0 / 41.0, 8.0 / 41.0), (-41.0 / 259.0, 28.0 / 259.0))
centre = 6.0


class Grid:
    def __init__(self):
        self.devices = lax.axis_size(AXIS)
        self.counts = (self.devices // (GRID_Y * GRID_Z), GRID_Y, GRID_Z)
        self.stride = (GRID_Y * GRID_Z, GRID_Z, 1)
        self.position = lax.axis_index(AXIS)
        self.coords = tuple(
            self.position // self.stride[d] % self.counts[d] for d in range(3)
        )

        flips = self.coords[0] + self.coords[1] + self.coords[2] // 2 + self.coords[2]
        self.share_low = flips % 2 == 1

    def coord_of(self, device, dim):
        return device // self.stride[dim] % self.counts[dim]

    def swapped(self, low, high, dim, odd, raw=False, cross=1):
        count = self.counts[dim]
        pairs = []
        for i in range(self.devices):
            c = self.coord_of(i, dim)
            up = c % 2 == odd
            to = (c + (1 if up else -1)) % count
            pairs.append((i, (i + (to - c) * self.stride[dim]) ^ cross))
        lower = self.coords[dim] % 2 == odd
        arrived = lax.ppermute(jnp.where(lower, high, low), AXIS, pairs)
        if raw:
            return arrived
        zero = jnp.zeros_like(arrived)
        to_low, to_high = jnp.where(lower, zero, arrived), jnp.where(lower, arrived, zero)
        if odd or count % 2:
            to_low = jnp.where(self.coords[dim] > 0, to_low, zero)
            to_high = jnp.where(self.coords[dim] < count - 1, to_high, zero)
        return to_low, to_high

    def exchanged(self, low, high, dim, cross=1):
        to_low, to_high = self.swapped(low, high, dim, 0, cross=cross)
        if self.counts[dim] > 2:
            more_low, more_high = self.swapped(low, high, dim, 1, cross=cross)
            to_low, to_high = to_low + more_low, to_high + more_high
        return to_low, to_high

    def partner(self, value, bits):
        return lax.ppermute(value, AXIS, [(i, i ^ bits) for i in range(self.devices)])

    def has(self, bit):
        return (self.position & bit) != 0


FIRST, SECOND = 3, 1


def placed(near, high, low):
    near = [
        jnp.where(low, near[i ^ 1], near[i]) for i in range(GRID_Z)
    ]
    return [jnp.where(high, near[i ^ 2], near[i]) for i in range(GRID_Z)]


def packed(blocks):
    half = blocks[0].shape[0] // 2
    return jnp.concatenate([b[h : h + half] for h in (0, half) for b in blocks], axis=1)


def unpacked(value, width):
    return [
        jnp.concatenate([value[:, e : e + width] for e in (i * width, (i + 2) * width)], axis=0)
        for i in range(2)
    ]


def split(value, parts):
    width = value.shape[1] // parts
    return [value[:, i * width : (i + 1) * width] for i in range(parts)]


def to_shares(grid, block, other):
    shares = split(block, GRID_Z)
    width = shares[0].shape[1]
    high = grid.has(2)
    kept = [jnp.where(high, shares[2 + i], shares[i]) for i in range(2)]
    away = [jnp.where(high, shares[i], shares[2 + i]) for i in range(2)]
    came = unpacked(grid.partner(packed(away), FIRST), width)
    low = grid.share_low
    own = [jnp.where(low, kept[1], kept[0]), jnp.where(low, came[1], came[0])]
    away = [jnp.where(low, kept[0], kept[1]), jnp.where(low, came[0], came[1])]
    away, other = lax.optimization_barrier((packed(away), other))
    came = unpacked(grid.partner(away, SECOND), width)
    other = by_rows(grid.partner(other, SECOND))
    near = [own[0], came[0], came[1], own[1]]
    return jnp.concatenate(placed(near, high, grid.has(1)), axis=1), other


def by_rows(value):
    return with_layout_constraint(value, Layout(major_to_minor=tuple(range(value.ndim))))


def plane(field, dim, at):
    return lax.slice_in_dim(field, at, at + 1, axis=dim)


def with_ends(field, dim, low, high):
    last = field.shape[dim] - 1
    parts = [
        plane(field, dim, 0) if low is None else low,
        lax.slice_in_dim(field, 1, last, axis=dim),
        plane(field, dim, last) if high is None else high,
    ]
    return jnp.concatenate(parts, axis=dim)


def to_next_partition(value, width):
    kept = value[..., :-width]
    return jnp.concatenate([jnp.zeros_like(value[..., :width]), kept], axis=-1)


def to_previous_partition(value, width):
    kept = value[..., width:]
    return jnp.concatenate([kept, jnp.zeros_like(value[..., :width])], axis=-1)


def slots_matrix(cell_matrix, connectivity, potential):
    slots = jnp.arange(potential.shape[0], dtype=jnp.int32)
    total = jnp.where(slots[:, None] == slots[None, :], potential[:, None], 0.0)
    for c in range(cell_matrix.shape[0]):
        chosen = (connectivity[c][:, None] == slots[None, :]).astype(jnp.bfloat16)
        rows = lax.dot_general(
            chosen, cell_matrix[c], (((0,), (0,)), ((), ())), preferred_element_type=jnp.float32
        ).astype(jnp.bfloat16)
        total = total + jnp.dot(rows, chosen, preferred_element_type=jnp.float32)
    return total.astype(jnp.bfloat16)


def rounded(value):
    return lax.reduce_precision(value, 8, 7).astype(jnp.bfloat16)


def plus(first, second):
    return (first.astype(jnp.float32) + second.astype(jnp.float32)).astype(jnp.bfloat16)


def summed_along(grid, value, stride, count):
    factor = 2
    while count > 1:
        while count % factor:
            factor += 1
        at = grid.position // stride % factor
        terms = [value]
        for turn in range(1, factor):
            pairs = []
            for i in range(grid.devices):
                c = i // stride % factor
                pairs.append((i, i + ((c + turn) % factor - c) * stride))
            terms.append(lax.ppermute(value, AXIS, pairs))
        if factor == 2:
            value = plus(*terms)
        else:
            total = 0.0
            for k in range(factor):
                term = terms[0]
                for turn in range(1, factor):
                    term = jnp.where((at - turn) % factor == k, terms[turn], term)
                total = total + term.astype(jnp.float32)
            value = total.astype(jnp.bfloat16)
        count //= factor
        stride *= factor
    return value


def per_device(block, cell_matrix, connectivity, potential, locked):
    owned_rows, columns = block.shape
    slot_count = potential.shape[0]
    width = columns // GRID_Z
    edge = SIDE - 1
    grid = Grid()
    shape = (SIDE, SIDE, SIDE, columns)

    field = block.reshape(edge, edge, edge, columns)
    high = plane(field, 1, edge - 1)
    matrix = by_rows(slots_matrix(cell_matrix, connectivity, potential))
    matrix, high = lax.optimization_barrier((matrix, high))
    other = by_rows(grid.partner(matrix, FIRST))
    field = jnp.concatenate([grid.exchanged(high, high, 1, cross=0)[0], field], axis=1)

    high = field[edge - 1].reshape(SIDE * edge, columns)
    tiles = -(-locked.shape[1] // columns)
    top = jnp.pad(locked[-edge * edge :], ((0, 0), (0, -locked.shape[1] % columns)))
    top = jnp.concatenate(split(top, tiles), axis=0)
    sent = jnp.concatenate([top, high], axis=0)
    sent, matrix = lax.optimization_barrier((sent, matrix))
    arrived = grid.exchanged(sent, sent, 0, cross=0)[0]
    bottom = jnp.split(arrived[: top.shape[0]], tiles, axis=0)
    bottom = jnp.concatenate(bottom, axis=1)[:, : locked.shape[1]]
    cut = max(0, 128 - bottom.shape[0])
    other_late = grid.partner(jnp.concatenate([bottom, locked[:cut]], axis=0), FIRST)
    other_early = grid.partner(locked[cut:], FIRST)
    field = jnp.concatenate(
        [arrived[top.shape[0] :].reshape(1, SIDE, edge, columns), field], axis=0
    )

    rows = field.reshape(SIDE * SIDE * edge, columns)
    second = by_rows(grid.partner(matrix, SECOND))
    mine, both = to_shares(grid, jnp.pad(rows, ((0, -rows.shape[0] % 16), (0, 0))), other)
    mine, both, other_early = lax.optimization_barrier((mine, both, other_early))
    matrices = [matrix, second, both, other]
    field = mine[: rows.shape[0]].reshape(SIDE, SIDE, edge, columns)
    low = to_next_partition(plane(field, 2, edge - 1), width)
    field = jnp.concatenate([low, field], axis=2)

    lane_owner = lax.broadcasted_iota(jnp.int32, (1, columns), 1) // width
    owner_near = lane_owner ^ grid.coords[2]

    current = field
    older = lax.optimization_barrier(field)
    steps = len(chebyshev_coeffs)
    for step, coeffs in enumerate(chebyshev_coeffs):
        rows = current.reshape(slot_count, columns)
        partial = 0.0
        for r in range(GRID_Z):
            own = jnp.where(owner_near == r, rows, jnp.zeros_like(rows))
            partial = partial + jnp.dot(
                matrices[r], own, preferred_element_type=jnp.float32
            )
        partial = partial.reshape(shape)
        low, high = plane(partial, 2, 0), plane(partial, 2, SIDE - 1)
        partial = with_ends(
            partial,
            2,
            jnp.where(lane_owner > 0, low + to_next_partition(high, width), 0.0),
            high + to_previous_partition(low, width),
        )
        if step == steps - 1:
            break
        for dim in (1, 0):
            low, high = plane(partial, dim, 0), plane(partial, dim, SIDE - 1)
            low16, high16 = low.astype(jnp.bfloat16), high.astype(jnp.bfloat16)
            to_low, to_high = grid.exchanged(low16, high16, dim)
            partial = with_ends(
                partial,
                dim,
                jnp.where(grid.coords[dim] > 0, low + to_low.astype(jnp.float32), 0.0),
                high + to_high.astype(jnp.float32),
            )
        following = coeffs[0] * (partial - centre * current.astype(jnp.float32)) - coeffs[
            1
        ] * older.astype(jnp.float32)
        following = rounded(following)
        older = lax.optimization_barrier(current)
        current = following
    locked = lax.optimization_barrier(jnp.concatenate([bottom, locked], axis=0))
    other_locked = jnp.concatenate([other_late, other_early], axis=0)
    both_locked = [grid.partner(l, SECOND) for l in (locked, other_locked)]
    low = plane(partial, 1, 0).astype(jnp.bfloat16)
    all_locked = [locked, both_locked[0], both_locked[1], other_locked]
    to_high = grid.exchanged(low, low, 1)[1].astype(jnp.float32)
    partial = with_ends(partial, 1, None, plane(partial, 1, SIDE - 1) + to_high)
    partial = coeffs[0] * partial[:, 1:, 1:].reshape(SIDE, edge * edge, columns)

    def owned(field):
        return field[1:, 1:, 1:].reshape(edge, edge * edge, columns).astype(jnp.float32)

    rest = -coeffs[0] * centre * owned(current) - coeffs[1] * owned(older)
    sums = jnp.concatenate([partial[:1], partial[1:] + rest], axis=0)
    weights = sums.astype(jnp.bfloat16).reshape(SIDE * edge * edge, columns)
    share = 0.0
    for r in range(GRID_Z):
        share = share + lax.dot_general(
            all_locked[r],
            jnp.where(owner_near == r, weights, jnp.zeros_like(weights)),
            (((0,), (0,)), ((), ())),
            preferred_element_type=jnp.float32,
        )
    share = sum(split(share, GRID_Z))
    deep = share.shape[0] // GRID_Z
    share = jnp.concatenate(
        [share[i * deep : (i + 1) * deep] for i in range(GRID_Z)], axis=1
    ).astype(jnp.bfloat16)

    low = sums[0].astype(jnp.bfloat16)
    stride, count = grid.stride[0], grid.counts[0]
    even = grid.coords[0] % 2 == 0
    arrived = grid.partner(jnp.concatenate([share, low], axis=0), stride | 1)
    share = plus(share, arrived[:deep])
    to_high = jnp.where(even, arrived[deep:], jnp.zeros_like(low))
    if count > 2:
        to_high = to_high + grid.swapped(low, low, 0, 1)[1]
    sums = jnp.concatenate(
        [sums[1:edge], sums[edge:] + to_high[None].astype(jnp.float32)], axis=0
    )
    filtered = rounded(sums.reshape(owned_rows, columns))

    share = plus(share, grid.swapped(share, share, 1, 0, True))
    share = plus(share, grid.swapped(share, share, 1, 1, True))
    share = summed_along(grid, share, stride * 2, count // 2)

    high, low = grid.has(2), grid.share_low
    near = placed(split(filtered, GRID_Z), high, grid.has(1))
    sent = jnp.concatenate([share, packed([near[3], near[2]])], axis=0)
    arrived = grid.partner(sent, FIRST)
    held = jnp.stack([share, arrived[:deep]])
    came = unpacked(arrived[deep:], width)
    own = [near[0], came[0]]
    away = [near[1], came[1]]
    sent = jnp.concatenate([held.reshape(-1, columns), packed(away)], axis=0)
    arrived = grid.partner(sent, SECOND)
    others = arrived[: 2 * deep].reshape(held.shape)
    came = unpacked(arrived[2 * deep :], width)
    filtered = jnp.concatenate(placed([own[0], came[0], own[1], came[1]], high, low), axis=1)
    held = placed([held[0], others[0], held[1], others[1]], high, low)
    intersection = jnp.concatenate(
        [
            jnp.concatenate([h[:, q * width : (q + 1) * width] for h in held], axis=1)
            for q in range(GRID_Z)
        ],
        axis=0,
    ).astype(jnp.float32)
    return filtered, intersection


def solution(mesh):
    in_specs = (
        P(AXIS, None),
        P(AXIS, None, None),
        P(AXIS, None),
        P(AXIS),
        P(AXIS, None),
    )
    out_specs = (P(AXIS, None), P())
    return jax.shard_map(
        per_device, mesh=mesh, in_specs=in_specs, out_specs=out_specs, check_vma=False
    )
```

```python
import jax
import jax.numpy as jnp
from jax import lax
from jax.experimental.layout import Layout, with_layout_constraint
from jax.sharding import PartitionSpec as P

GRID_Y = 4
GRID_Z = 4
SIDE = 7
AXIS = "cells"

chebyshev_coeffs = ((-1.0 / 7.0, 0.0), (-7.0 / 41.0, 8.0 / 41.0), (-41.0 / 259.0, 28.0 / 259.0))
centre = 6.0


class Grid:
    def __init__(self):
        self.devices = lax.axis_size(AXIS)
        self.counts = (self.devices // (GRID_Y * GRID_Z), GRID_Y, GRID_Z)
        self.stride = (GRID_Y * GRID_Z, GRID_Z, 1)
        self.position = lax.axis_index(AXIS)
        self.coords = tuple(
            self.position // self.stride[d] % self.counts[d] for d in range(3)
        )

        flips = self.coords[0] + self.coords[1] + self.coords[2] // 2 + self.coords[2]
        self.share_low = flips % 2 == 1

    def coord_of(self, device, dim):
        return device // self.stride[dim] % self.counts[dim]

    def swapped(self, low, high, dim, odd, raw=False, cross=1):
        count = self.counts[dim]
        pairs = []
        for i in range(self.devices):
            c = self.coord_of(i, dim)
            up = c % 2 == odd
            to = (c + (1 if up else -1)) % count
            pairs.append((i, (i + (to - c) * self.stride[dim]) ^ cross))
        lower = self.coords[dim] % 2 == odd
        arrived = lax.ppermute(jnp.where(lower, high, low), AXIS, pairs)
        if raw:
            return arrived
        zero = jnp.zeros_like(arrived)
        to_low, to_high = jnp.where(lower, zero, arrived), jnp.where(lower, arrived, zero)
        if odd or count % 2:
            to_low = jnp.where(self.coords[dim] > 0, to_low, zero)
            to_high = jnp.where(self.coords[dim] < count - 1, to_high, zero)
        return to_low, to_high

    def exchanged(self, low, high, dim, cross=1):
        to_low, to_high = self.swapped(low, high, dim, 0, cross=cross)
        if self.counts[dim] > 2:
            more_low, more_high = self.swapped(low, high, dim, 1, cross=cross)
            to_low, to_high = to_low + more_low, to_high + more_high
        return to_low, to_high

    def partner(self, value, bits):
        return lax.ppermute(value, AXIS, [(i, i ^ bits) for i in range(self.devices)])

    def has(self, bit):
        return (self.position & bit) != 0


FIRST, SECOND = 3, 1


def placed(near, high, low):
    near = [
        jnp.where(low, near[i ^ 1], near[i]) for i in range(GRID_Z)
    ]
    return [jnp.where(high, near[i ^ 2], near[i]) for i in range(GRID_Z)]


def packed(blocks):
    half = blocks[0].shape[0] // 2
    return jnp.concatenate([b[h : h + half] for h in (0, half) for b in blocks], axis=1)


def unpacked(value, width):
    return [
        jnp.concatenate([value[:, e : e + width] for e in (i * width, (i + 2) * width)], axis=0)
        for i in range(2)
    ]


def split(value, parts):
    width = value.shape[1] // parts
    return [value[:, i * width : (i + 1) * width] for i in range(parts)]


def to_shares(grid, block, other):
    shares = split(block, GRID_Z)
    width = shares[0].shape[1]
    high = grid.has(2)
    kept = [jnp.where(high, shares[2 + i], shares[i]) for i in range(2)]
    away = [jnp.where(high, shares[i], shares[2 + i]) for i in range(2)]
    came = unpacked(grid.partner(packed(away), FIRST), width)
    low = grid.share_low
    own = [jnp.where(low, kept[1], kept[0]), jnp.where(low, came[1], came[0])]
    away = [jnp.where(low, kept[0], kept[1]), jnp.where(low, came[0], came[1])]
    away, other = lax.optimization_barrier((packed(away), other))
    came = unpacked(grid.partner(away, SECOND), width)
    other = by_rows(grid.partner(other, SECOND))
    near = [own[0], came[0], came[1], own[1]]
    return jnp.concatenate(placed(near, high, grid.has(1)), axis=1), other


def by_rows(value):
    return with_layout_constraint(value, Layout(major_to_minor=tuple(range(value.ndim))))


def plane(field, dim, at):
    return lax.slice_in_dim(field, at, at + 1, axis=dim)


def with_ends(field, dim, low, high):
    last = field.shape[dim] - 1
    parts = [
        plane(field, dim, 0) if low is None else low,
        lax.slice_in_dim(field, 1, last, axis=dim),
        plane(field, dim, last) if high is None else high,
    ]
    return jnp.concatenate(parts, axis=dim)


def to_next_partition(value, width):
    kept = value[..., :-width]
    return jnp.concatenate([jnp.zeros_like(value[..., :width]), kept], axis=-1)


def to_previous_partition(value, width):
    kept = value[..., width:]
    return jnp.concatenate([kept, jnp.zeros_like(value[..., :width])], axis=-1)


def slots_matrix(cell_matrix, connectivity, potential):
    slots = jnp.arange(potential.shape[0], dtype=jnp.int32)
    total = jnp.where(slots[:, None] == slots[None, :], potential[:, None], 0.0)
    for c in range(cell_matrix.shape[0]):
        chosen = (connectivity[c][:, None] == slots[None, :]).astype(jnp.bfloat16)
        rows = lax.dot_general(
            chosen, cell_matrix[c], (((0,), (0,)), ((), ())), preferred_element_type=jnp.float32
        ).astype(jnp.bfloat16)
        total = total + jnp.dot(rows, chosen, preferred_element_type=jnp.float32)
    return total.astype(jnp.bfloat16)


def rounded(value):
    return lax.reduce_precision(value, 8, 7).astype(jnp.bfloat16)


def plus(first, second):
    return (first.astype(jnp.float32) + second.astype(jnp.float32)).astype(jnp.bfloat16)


def summed_along(grid, value, stride, count):
    factor = 2
    while count > 1:
        while count % factor:
            factor += 1
        at = grid.position // stride % factor
        terms = [value]
        for turn in range(1, factor):
            pairs = []
            for i in range(grid.devices):
                c = i // stride % factor
                pairs.append((i, i + ((c + turn) % factor - c) * stride))
            terms.append(lax.ppermute(value, AXIS, pairs))
        if factor == 2:
            value = plus(*terms)
        else:
            total = 0.0
            for k in range(factor):
                term = terms[0]
                for turn in range(1, factor):
                    term = jnp.where((at - turn) % factor == k, terms[turn], term)
                total = total + term.astype(jnp.float32)
            value = total.astype(jnp.bfloat16)
        count //= factor
        stride *= factor
    return value


def per_device(block, cell_matrix, connectivity, potential, locked):
    owned_rows, columns = block.shape
    slot_count = potential.shape[0]
    width = columns // GRID_Z
    edge = SIDE - 1
    grid = Grid()
    shape = (SIDE, SIDE, SIDE, columns)

    field = block.reshape(edge, edge, edge, columns)
    high = plane(field, 1, edge - 1)
    cell_matrix, high = lax.optimization_barrier((cell_matrix, high))
    matrix = by_rows(slots_matrix(cell_matrix, connectivity, potential))
    other = by_rows(grid.partner(matrix, FIRST))
    field = jnp.concatenate([grid.exchanged(high, high, 1, cross=0)[0], field], axis=1)

    high = field[edge - 1].reshape(SIDE * edge, columns)
    tiles = -(-locked.shape[1] // columns)
    top = jnp.pad(locked[-edge * edge :], ((0, 0), (0, -locked.shape[1] % columns)))
    top = lax.optimization_barrier(jnp.concatenate(split(top, tiles), axis=0))
    sent = jnp.concatenate([top, high], axis=0)
    sent, matrix = lax.optimization_barrier((sent, matrix))
    arrived = grid.exchanged(sent, sent, 0, cross=0)[0]
    bottom = jnp.split(arrived[: top.shape[0]], tiles, axis=0)
    bottom = jnp.concatenate(bottom, axis=1)[:, : locked.shape[1]]
    cut = max(0, 128 - bottom.shape[0])
    other_late = grid.partner(jnp.concatenate([bottom, locked[:cut]], axis=0), FIRST)
    other_early = grid.partner(locked[cut:], FIRST)
    field = jnp.concatenate(
        [arrived[top.shape[0] :].reshape(1, SIDE, edge, columns), field], axis=0
    )

    rows = field.reshape(SIDE * SIDE * edge, columns)
    second = by_rows(grid.partner(matrix, SECOND))
    mine, both = to_shares(grid, jnp.pad(rows, ((0, -rows.shape[0] % 16), (0, 0))), other)
    mine, both, other_early = lax.optimization_barrier((mine, both, other_early))
    matrices = [matrix, second, both, other]
    field = mine[: rows.shape[0]].reshape(SIDE, SIDE, edge, columns)
    low = to_next_partition(plane(field, 2, edge - 1), width)
    field = jnp.concatenate([low, field], axis=2)

    lane_owner = lax.broadcasted_iota(jnp.int32, (1, columns), 1) // width
    owner_near = lane_owner ^ grid.coords[2]

    current = field
    older = lax.optimization_barrier(field)
    steps = len(chebyshev_coeffs)
    for step, coeffs in enumerate(chebyshev_coeffs):
        rows = current.reshape(slot_count, columns)
        partial = 0.0
        for r in range(GRID_Z):
            own = jnp.where(owner_near == r, rows, jnp.zeros_like(rows))
            partial = partial + jnp.dot(
                matrices[r], own, preferred_element_type=jnp.float32
            )
        partial = partial.reshape(shape)
        low, high = plane(partial, 2, 0), plane(partial, 2, SIDE - 1)
        partial = with_ends(
            partial,
            2,
            jnp.where(lane_owner > 0, low + to_next_partition(high, width), 0.0),
            high + to_previous_partition(low, width),
        )
        if step == steps - 1:
            break
        for dim in (1, 0):
            low, high = plane(partial, dim, 0), plane(partial, dim, SIDE - 1)
            low16, high16 = low.astype(jnp.bfloat16), high.astype(jnp.bfloat16)
            to_low, to_high = grid.exchanged(low16, high16, dim)
            partial = with_ends(
                partial,
                dim,
                jnp.where(grid.coords[dim] > 0, low + to_low.astype(jnp.float32), 0.0),
                high + to_high.astype(jnp.float32),
            )
        following = coeffs[0] * (partial - centre * current.astype(jnp.float32)) - coeffs[
            1
        ] * older.astype(jnp.float32)
        following = rounded(following)
        older = lax.optimization_barrier(current)
        current = following
    locked = lax.optimization_barrier(jnp.concatenate([bottom, locked], axis=0))
    other_locked = jnp.concatenate([other_late, other_early], axis=0)
    both_locked = [grid.partner(l, SECOND) for l in (locked, other_locked)]
    low = plane(partial, 1, 0).astype(jnp.bfloat16)
    all_locked = [locked, both_locked[0], both_locked[1], other_locked]
    to_high = grid.exchanged(low, low, 1)[1].astype(jnp.float32)
    partial = with_ends(partial, 1, None, plane(partial, 1, SIDE - 1) + to_high)
    partial = coeffs[0] * partial[:, 1:, 1:].reshape(SIDE, edge * edge, columns)

    def owned(field):
        return field[1:, 1:, 1:].reshape(edge, edge * edge, columns).astype(jnp.float32)

    rest = -coeffs[0] * centre * owned(current) - coeffs[1] * owned(older)
    sums = jnp.concatenate([partial[:1], partial[1:] + rest], axis=0)
    weights = sums.astype(jnp.bfloat16).reshape(SIDE * edge * edge, columns)
    share = 0.0
    for r in range(GRID_Z):
        share = share + lax.dot_general(
            all_locked[r],
            jnp.where(owner_near == r, weights, jnp.zeros_like(weights)),
            (((0,), (0,)), ((), ())),
            preferred_element_type=jnp.float32,
        )
    share = sum(split(share, GRID_Z))
    deep = share.shape[0] // GRID_Z
    share = jnp.concatenate(
        [share[i * deep : (i + 1) * deep] for i in range(GRID_Z)], axis=1
    ).astype(jnp.bfloat16)

    low = sums[0].astype(jnp.bfloat16)
    stride, count = grid.stride[0], grid.counts[0]
    even = grid.coords[0] % 2 == 0
    arrived = grid.partner(jnp.concatenate([share, low], axis=0), stride | 1)
    share = plus(share, arrived[:deep])
    to_high = jnp.where(even, arrived[deep:], jnp.zeros_like(low))
    if count > 2:
        to_high = to_high + grid.swapped(low, low, 0, 1)[1]
    sums = jnp.concatenate(
        [sums[1:edge], sums[edge:] + to_high[None].astype(jnp.float32)], axis=0
    )
    filtered = rounded(sums.reshape(owned_rows, columns))

    share = plus(share, grid.swapped(share, share, 1, 0, True))
    share = plus(share, grid.swapped(share, share, 1, 1, True))
    share = summed_along(grid, share, stride * 2, count // 2)

    high, low = grid.has(2), grid.share_low
    near = placed(split(filtered, GRID_Z), high, grid.has(1))
    sent = jnp.concatenate([share, packed([near[3], near[2]])], axis=0)
    arrived = grid.partner(sent, FIRST)
    held = jnp.stack([share, arrived[:deep]])
    came = unpacked(arrived[deep:], width)
    own = [near[0], came[0]]
    away = [near[1], came[1]]
    sent = jnp.concatenate([held.reshape(-1, columns), packed(away)], axis=0)
    arrived = grid.partner(sent, SECOND)
    others = arrived[: 2 * deep].reshape(held.shape)
    came = unpacked(arrived[2 * deep :], width)
    filtered = jnp.concatenate(placed([own[0], came[0], own[1], came[1]], high, low), axis=1)
    held = placed([held[0], others[0], held[1], others[1]], high, low)
    intersection = jnp.concatenate(
        [
            jnp.concatenate([h[:, q * width : (q + 1) * width] for h in held], axis=1)
            for q in range(GRID_Z)
        ],
        axis=0,
    ).astype(jnp.float32)
    return filtered, intersection


def solution(mesh):
    in_specs = (
        P(AXIS, None),
        P(AXIS, None, None),
        P(AXIS, None),
        P(AXIS),
        P(AXIS, None),
    )
    out_specs = (P(AXIS, None), P())
    return jax.shard_map(
        per_device, mesh=mesh, in_specs=in_specs, out_specs=out_specs, check_vma=False
    )
```

```python
import jax
import jax.numpy as jnp
from jax import lax
from jax.experimental.layout import Layout, with_layout_constraint
from jax.sharding import PartitionSpec as P

GRID_Y = 4
GRID_Z = 4
SIDE = 7
AXIS = "cells"

chebyshev_coeffs = ((-1.0 / 7.0, 0.0), (-7.0 / 41.0, 8.0 / 41.0), (-41.0 / 259.0, 28.0 / 259.0))
centre = 6.0


class Grid:
    def __init__(self):
        self.devices = lax.axis_size(AXIS)
        self.counts = (self.devices // (GRID_Y * GRID_Z), GRID_Y, GRID_Z)
        self.stride = (GRID_Y * GRID_Z, GRID_Z, 1)
        self.position = lax.axis_index(AXIS)
        self.coords = tuple(
            self.position // self.stride[d] % self.counts[d] for d in range(3)
        )

        flips = self.coords[0] + self.coords[1] + self.coords[2] // 2 + self.coords[2]
        self.share_low = flips % 2 == 1

    def coord_of(self, device, dim):
        return device // self.stride[dim] % self.counts[dim]

    def swapped(self, low, high, dim, odd, raw=False, cross=1):
        count = self.counts[dim]
        pairs = []
        for i in range(self.devices):
            c = self.coord_of(i, dim)
            up = c % 2 == odd
            to = (c + (1 if up else -1)) % count
            pairs.append((i, (i + (to - c) * self.stride[dim]) ^ cross))
        lower = self.coords[dim] % 2 == odd
        arrived = lax.ppermute(jnp.where(lower, high, low), AXIS, pairs)
        if raw:
            return arrived
        zero = jnp.zeros_like(arrived)
        to_low, to_high = jnp.where(lower, zero, arrived), jnp.where(lower, arrived, zero)
        if odd or count % 2:
            to_low = jnp.where(self.coords[dim] > 0, to_low, zero)
            to_high = jnp.where(self.coords[dim] < count - 1, to_high, zero)
        return to_low, to_high

    def exchanged(self, low, high, dim, cross=1):
        to_low, to_high = self.swapped(low, high, dim, 0, cross=cross)
        if self.counts[dim] > 2:
            more_low, more_high = self.swapped(low, high, dim, 1, cross=cross)
            to_low, to_high = to_low + more_low, to_high + more_high
        return to_low, to_high

    def partner(self, value, bits):
        return lax.ppermute(value, AXIS, [(i, i ^ bits) for i in range(self.devices)])

    def has(self, bit):
        return (self.position & bit) != 0


FIRST, SECOND = 3, 1


def placed(near, high, low):
    near = [
        jnp.where(low, near[i ^ 1], near[i]) for i in range(GRID_Z)
    ]
    return [jnp.where(high, near[i ^ 2], near[i]) for i in range(GRID_Z)]


def packed(blocks):
    half = blocks[0].shape[0] // 2
    return jnp.concatenate([b[h : h + half] for h in (0, half) for b in blocks], axis=1)


def unpacked(value, width):
    return [
        jnp.concatenate([value[:, e : e + width] for e in (i * width, (i + 2) * width)], axis=0)
        for i in range(2)
    ]


def split(value, parts):
    width = value.shape[1] // parts
    return [value[:, i * width : (i + 1) * width] for i in range(parts)]


def to_shares(grid, block, other):
    shares = split(block, GRID_Z)
    width = shares[0].shape[1]
    high = grid.has(2)
    kept = [jnp.where(high, shares[2 + i], shares[i]) for i in range(2)]
    away = [jnp.where(high, shares[i], shares[2 + i]) for i in range(2)]
    came = unpacked(grid.partner(packed(away), FIRST), width)
    low = grid.share_low
    own = [jnp.where(low, kept[1], kept[0]), jnp.where(low, came[1], came[0])]
    away = [jnp.where(low, kept[0], kept[1]), jnp.where(low, came[0], came[1])]
    away, other = lax.optimization_barrier((packed(away), other))
    came = unpacked(grid.partner(away, SECOND), width)
    other = by_rows(grid.partner(other, SECOND))
    near = [own[0], came[0], came[1], own[1]]
    return jnp.concatenate(placed(near, high, grid.has(1)), axis=1), other


def by_rows(value):
    return with_layout_constraint(value, Layout(major_to_minor=tuple(range(value.ndim))))


def plane(field, dim, at):
    return lax.slice_in_dim(field, at, at + 1, axis=dim)


def with_ends(field, dim, low, high):
    last = field.shape[dim] - 1
    parts = [
        plane(field, dim, 0) if low is None else low,
        lax.slice_in_dim(field, 1, last, axis=dim),
        plane(field, dim, last) if high is None else high,
    ]
    return jnp.concatenate(parts, axis=dim)


def to_next_partition(value, width):
    kept = value[..., :-width]
    return jnp.concatenate([jnp.zeros_like(value[..., :width]), kept], axis=-1)


def to_previous_partition(value, width):
    kept = value[..., width:]
    return jnp.concatenate([kept, jnp.zeros_like(value[..., :width])], axis=-1)


def slots_matrix(cell_matrix, connectivity, potential):
    slots = jnp.arange(potential.shape[0], dtype=jnp.int32)
    total = jnp.where(slots[:, None] == slots[None, :], potential[:, None], 0.0)
    for c in range(cell_matrix.shape[0]):
        chosen = (connectivity[c][:, None] == slots[None, :]).astype(jnp.bfloat16)
        rows = lax.dot_general(
            chosen, cell_matrix[c], (((0,), (0,)), ((), ())), preferred_element_type=jnp.float32
        ).astype(jnp.bfloat16)
        total = total + jnp.dot(rows, chosen, preferred_element_type=jnp.float32)
    return total.astype(jnp.bfloat16)


def rounded(value):
    return lax.reduce_precision(value, 8, 7).astype(jnp.bfloat16)


def plus(first, second):
    return (first.astype(jnp.float32) + second.astype(jnp.float32)).astype(jnp.bfloat16)


def summed_along(grid, value, stride, count):
    factor = 2
    while count > 1:
        while count % factor:
            factor += 1
        at = grid.position // stride % factor
        terms = [value]
        for turn in range(1, factor):
            pairs = []
            for i in range(grid.devices):
                c = i // stride % factor
                pairs.append((i, i + ((c + turn) % factor - c) * stride))
            terms.append(lax.ppermute(value, AXIS, pairs))
        if factor == 2:
            value = plus(*terms)
        else:
            total = 0.0
            for k in range(factor):
                term = terms[0]
                for turn in range(1, factor):
                    term = jnp.where((at - turn) % factor == k, terms[turn], term)
                total = total + term.astype(jnp.float32)
            value = total.astype(jnp.bfloat16)
        count //= factor
        stride *= factor
    return value


def per_device(block, cell_matrix, connectivity, potential, locked):
    owned_rows, columns = block.shape
    slot_count = potential.shape[0]
    width = columns // GRID_Z
    edge = SIDE - 1
    grid = Grid()
    shape = (SIDE, SIDE, SIDE, columns)

    field = block.reshape(edge, edge, edge, columns)
    high = plane(field, 1, edge - 1)
    cell_matrix, high = lax.optimization_barrier((cell_matrix, high))
    matrix = by_rows(slots_matrix(cell_matrix, connectivity, potential))
    other = by_rows(grid.partner(matrix, FIRST))
    field = jnp.concatenate([grid.exchanged(high, high, 1, cross=0)[0], field], axis=1)

    high = field[edge - 1].reshape(SIDE * edge, columns)
    tiles = -(-locked.shape[1] // columns)
    top = jnp.pad(locked[-edge * edge :], ((0, 0), (0, -locked.shape[1] % columns)))
    top = lax.optimization_barrier(jnp.concatenate(split(top, tiles), axis=0))
    sent = jnp.concatenate([top, high], axis=0)
    sent, matrix = lax.optimization_barrier((sent, matrix))
    arrived = grid.exchanged(sent, sent, 0, cross=0)[0]
    bottom = jnp.split(arrived[: top.shape[0]], tiles, axis=0)
    bottom = jnp.concatenate(bottom, axis=1)[:, : locked.shape[1]]
    cut = max(0, 128 - bottom.shape[0])
    other_late = grid.partner(jnp.concatenate([bottom, locked[:cut]], axis=0), FIRST)
    other_early = grid.partner(locked[cut:], FIRST)
    field = jnp.concatenate(
        [arrived[top.shape[0] :].reshape(1, SIDE, edge, columns), field], axis=0
    )

    rows = field.reshape(SIDE * SIDE * edge, columns)
    second = by_rows(grid.partner(matrix, SECOND))
    mine, both = to_shares(grid, jnp.pad(rows, ((0, -rows.shape[0] % 16), (0, 0))), other)
    mine, both, other_early = lax.optimization_barrier((mine, both, other_early))
    matrices = [matrix, second, both, other]
    field = mine[: rows.shape[0]].reshape(SIDE, SIDE, edge, columns)
    low = to_next_partition(plane(field, 2, edge - 1), width)
    field = jnp.concatenate([low, field], axis=2)

    lane_owner = lax.broadcasted_iota(jnp.int32, (1, columns), 1) // width
    owner_near = lane_owner ^ grid.coords[2]

    current = field
    older = lax.optimization_barrier(field)
    steps = len(chebyshev_coeffs)
    for step, coeffs in enumerate(chebyshev_coeffs):
        rows = current.reshape(slot_count, columns)
        partial = 0.0
        for r in range(GRID_Z):
            own = jnp.where(owner_near == r, rows, jnp.zeros_like(rows))
            partial = partial + jnp.dot(
                matrices[r], own, preferred_element_type=jnp.float32
            )
        partial = partial.reshape(shape)
        low, high = plane(partial, 2, 0), plane(partial, 2, SIDE - 1)
        partial = with_ends(
            partial,
            2,
            jnp.where(lane_owner > 0, low + to_next_partition(high, width), 0.0),
            high + to_previous_partition(low, width),
        )
        if step == steps - 1:
            break
        for dim in (1, 0):
            low, high = plane(partial, dim, 0), plane(partial, dim, SIDE - 1)
            low16, high16 = low.astype(jnp.bfloat16), high.astype(jnp.bfloat16)
            to_low, to_high = grid.exchanged(low16, high16, dim)
            partial = with_ends(
                partial,
                dim,
                jnp.where(grid.coords[dim] > 0, low + to_low.astype(jnp.float32), 0.0),
                high + to_high.astype(jnp.float32),
            )
        following = coeffs[0] * (partial - centre * current.astype(jnp.float32)) - coeffs[
            1
        ] * older.astype(jnp.float32)
        following = rounded(following)
        older = lax.optimization_barrier(current)
        current = following
    locked = lax.optimization_barrier(jnp.concatenate([bottom, locked], axis=0))
    other_locked = jnp.concatenate([other_late, other_early], axis=0)
    both_locked = [grid.partner(l, SECOND) for l in (locked, other_locked)]
    low = plane(partial, 1, 0).astype(jnp.bfloat16)
    all_locked = [locked, both_locked[0], both_locked[1], other_locked]
    to_high = grid.exchanged(low, low, 1)[1].astype(jnp.float32)
    partial = with_ends(partial, 1, None, plane(partial, 1, SIDE - 1) + to_high)
    partial = coeffs[0] * partial[:, 1:, 1:].reshape(SIDE, edge * edge, columns)

    def owned(field):
        return field[1:, 1:, 1:].reshape(edge, edge * edge, columns).astype(jnp.float32)

    rest = -coeffs[0] * centre * owned(current) - coeffs[1] * owned(older)
    sums = jnp.concatenate([partial[:1], partial[1:] + rest], axis=0)
    weights = sums.astype(jnp.bfloat16).reshape(SIDE * edge * edge, columns)
    share = 0.0
    for r in range(GRID_Z):
        share = share + lax.dot_general(
            all_locked[r],
            jnp.where(owner_near == r, weights, jnp.zeros_like(weights)),
            (((0,), (0,)), ((), ())),
            preferred_element_type=jnp.float32,
        )
    share = sum(split(share, GRID_Z))
    deep = share.shape[0] // GRID_Z
    share = jnp.concatenate(
        [share[i * deep : (i + 1) * deep] for i in range(GRID_Z)], axis=1
    ).astype(jnp.bfloat16)

    low = sums[0].astype(jnp.bfloat16)
    stride, count = grid.stride[0], grid.counts[0]
    even = grid.coords[0] % 2 == 0
    arrived = grid.partner(jnp.concatenate([share, low], axis=0), stride | 1)
    share = plus(share, arrived[:deep])
    to_high = jnp.where(even, arrived[deep:], jnp.zeros_like(low))
    if count > 2:
        to_high = to_high + grid.swapped(low, low, 0, 1)[1]
    sums = jnp.concatenate(
        [sums[1:edge], sums[edge:] + to_high[None].astype(jnp.float32)], axis=0
    )
    filtered = rounded(sums.reshape(owned_rows, columns))

    share = plus(share, grid.swapped(share, share, 1, 0, True))
    share = plus(share, grid.swapped(share, share, 1, 1, True))
    share = summed_along(grid, share, stride * 2, count // 2)

    high, low = grid.has(2), grid.share_low
    near = placed(split(filtered, GRID_Z), high, grid.has(1))
    sent = jnp.concatenate([share, packed([near[3], near[2]])], axis=0)
    arrived = grid.partner(sent, FIRST)
    held = [share, arrived[:deep]]
    came = unpacked(arrived[deep:], width)
    own = [near[0], came[0]]
    away = [near[1], came[1]]
    came = unpacked(grid.partner(packed(away), SECOND), width)
    others = [grid.partner(h, SECOND) for h in held]
    filtered = jnp.concatenate(placed([own[0], came[0], own[1], came[1]], high, low), axis=1)
    held = placed([held[0], others[0], held[1], others[1]], high, low)
    intersection = jnp.concatenate(
        [
            jnp.concatenate([h[:, q * width : (q + 1) * width] for h in held], axis=1)
            for q in range(GRID_Z)
        ],
        axis=0,
    ).astype(jnp.float32)
    return filtered, intersection


def solution(mesh):
    in_specs = (
        P(AXIS, None),
        P(AXIS, None, None),
        P(AXIS, None),
        P(AXIS),
        P(AXIS, None),
    )
    out_specs = (P(AXIS, None), P())
    return jax.shard_map(
        per_device, mesh=mesh, in_specs=in_specs, out_specs=out_specs, check_vma=False
    )
```

```python
import jax
import jax.numpy as jnp
from jax import lax
from jax.experimental.layout import Layout, with_layout_constraint
from jax.sharding import PartitionSpec as P

GRID_Y = 4
GRID_Z = 4
SIDE = 7
AXIS = "cells"

chebyshev_coeffs = ((-1.0 / 7.0, 0.0), (-7.0 / 41.0, 8.0 / 41.0), (-41.0 / 259.0, 28.0 / 259.0))
centre = 6.0


class Grid:
    def __init__(self):
        self.devices = lax.axis_size(AXIS)
        self.counts = (self.devices // (GRID_Y * GRID_Z), GRID_Y, GRID_Z)
        self.stride = (GRID_Y * GRID_Z, GRID_Z, 1)
        self.position = lax.axis_index(AXIS)
        self.coords = tuple(
            self.position // self.stride[d] % self.counts[d] for d in range(3)
        )

        flips = self.coords[0] + self.coords[1] + self.coords[2] // 2 + self.coords[2]
        self.share_low = flips % 2 == 1

    def coord_of(self, device, dim):
        return device // self.stride[dim] % self.counts[dim]

    def swapped(self, low, high, dim, odd, raw=False, cross=1):
        count = self.counts[dim]
        pairs = []
        for i in range(self.devices):
            c = self.coord_of(i, dim)
            up = c % 2 == odd
            to = (c + (1 if up else -1)) % count
            pairs.append((i, (i + (to - c) * self.stride[dim]) ^ cross))
        lower = self.coords[dim] % 2 == odd
        arrived = lax.ppermute(jnp.where(lower, high, low), AXIS, pairs)
        if raw:
            return arrived
        zero = jnp.zeros_like(arrived)
        to_low, to_high = jnp.where(lower, zero, arrived), jnp.where(lower, arrived, zero)
        if odd or count % 2:
            to_low = jnp.where(self.coords[dim] > 0, to_low, zero)
            to_high = jnp.where(self.coords[dim] < count - 1, to_high, zero)
        return to_low, to_high

    def exchanged(self, low, high, dim, cross=1):
        to_low, to_high = self.swapped(low, high, dim, 0, cross=cross)
        if self.counts[dim] > 2:
            more_low, more_high = self.swapped(low, high, dim, 1, cross=cross)
            to_low, to_high = to_low + more_low, to_high + more_high
        return to_low, to_high

    def partner(self, value, bits):
        return lax.ppermute(value, AXIS, [(i, i ^ bits) for i in range(self.devices)])

    def has(self, bit):
        return (self.position & bit) != 0


FIRST, SECOND = 3, 1


def placed(near, high, low):
    near = [
        jnp.where(low, near[i ^ 1], near[i]) for i in range(GRID_Z)
    ]
    return [jnp.where(high, near[i ^ 2], near[i]) for i in range(GRID_Z)]


def packed(blocks):
    half = blocks[0].shape[0] // 2
    return jnp.concatenate([b[h : h + half] for h in (0, half) for b in blocks], axis=1)


def unpacked(value, width):
    return [
        jnp.concatenate([value[:, e : e + width] for e in (i * width, (i + 2) * width)], axis=0)
        for i in range(2)
    ]


def split(value, parts):
    width = value.shape[1] // parts
    return [value[:, i * width : (i + 1) * width] for i in range(parts)]


def to_shares(grid, block, other):
    shares = split(block, GRID_Z)
    width = shares[0].shape[1]
    high = grid.has(2)
    kept = [jnp.where(high, shares[2 + i], shares[i]) for i in range(2)]
    away = [jnp.where(high, shares[i], shares[2 + i]) for i in range(2)]
    came = unpacked(grid.partner(packed(away), FIRST), width)
    low = grid.share_low
    own = [jnp.where(low, kept[1], kept[0]), jnp.where(low, came[1], came[0])]
    away = [jnp.where(low, kept[0], kept[1]), jnp.where(low, came[0], came[1])]
    away, other = lax.optimization_barrier((packed(away), other))
    came = unpacked(grid.partner(away, SECOND), width)
    other = by_rows(grid.partner(other, SECOND))
    near = [own[0], came[0], came[1], own[1]]
    return jnp.concatenate(placed(near, high, grid.has(1)), axis=1), other


def by_rows(value):
    return with_layout_constraint(value, Layout(major_to_minor=tuple(range(value.ndim))))


def plane(field, dim, at):
    return lax.slice_in_dim(field, at, at + 1, axis=dim)


def with_ends(field, dim, low, high):
    last = field.shape[dim] - 1
    parts = [
        plane(field, dim, 0) if low is None else low,
        lax.slice_in_dim(field, 1, last, axis=dim),
        plane(field, dim, last) if high is None else high,
    ]
    return jnp.concatenate(parts, axis=dim)


def to_next_partition(value, width):
    kept = value[..., :-width]
    return jnp.concatenate([jnp.zeros_like(value[..., :width]), kept], axis=-1)


def to_previous_partition(value, width):
    kept = value[..., width:]
    return jnp.concatenate([kept, jnp.zeros_like(value[..., :width])], axis=-1)


def slots_matrix(cell_matrix, connectivity, potential):
    slots = jnp.arange(potential.shape[0], dtype=jnp.int32)
    total = jnp.where(slots[:, None] == slots[None, :], potential[:, None], 0.0)
    for c in range(cell_matrix.shape[0]):
        chosen = (connectivity[c][:, None] == slots[None, :]).astype(jnp.bfloat16)
        rows = lax.dot_general(
            chosen, cell_matrix[c], (((0,), (0,)), ((), ())), preferred_element_type=jnp.float32
        ).astype(jnp.bfloat16)
        total = total + jnp.dot(rows, chosen, preferred_element_type=jnp.float32)
    return total.astype(jnp.bfloat16)


def rounded(value):
    return lax.reduce_precision(value, 8, 7).astype(jnp.bfloat16)


def plus(first, second):
    return (first.astype(jnp.float32) + second.astype(jnp.float32)).astype(jnp.bfloat16)


def summed_along(grid, value, stride, count):
    factor = 2
    while count > 1:
        while count % factor:
            factor += 1
        at = grid.position // stride % factor
        terms = [value]
        for turn in range(1, factor):
            pairs = []
            for i in range(grid.devices):
                c = i // stride % factor
                pairs.append((i, i + ((c + turn) % factor - c) * stride))
            terms.append(lax.ppermute(value, AXIS, pairs))
        if factor == 2:
            value = plus(*terms)
        else:
            total = 0.0
            for k in range(factor):
                term = terms[0]
                for turn in range(1, factor):
                    term = jnp.where((at - turn) % factor == k, terms[turn], term)
                total = total + term.astype(jnp.float32)
            value = total.astype(jnp.bfloat16)
        count //= factor
        stride *= factor
    return value


def per_device(block, cell_matrix, connectivity, potential, locked):
    owned_rows, columns = block.shape
    slot_count = potential.shape[0]
    width = columns // GRID_Z
    edge = SIDE - 1
    grid = Grid()
    shape = (SIDE, SIDE, SIDE, columns)

    field = block.reshape(edge, edge, edge, columns)
    high = plane(field, 1, edge - 1)
    cell_matrix, high = lax.optimization_barrier((cell_matrix, high))
    matrix = by_rows(slots_matrix(cell_matrix, connectivity, potential))
    other = by_rows(grid.partner(matrix, FIRST))
    field = jnp.concatenate([grid.exchanged(high, high, 1, cross=0)[0], field], axis=1)

    high = field[edge - 1].reshape(SIDE * edge, columns)
    tiles = -(-locked.shape[1] // columns)
    top = jnp.pad(locked[-edge * edge :], ((0, 0), (0, -locked.shape[1] % columns)))
    top = lax.optimization_barrier(jnp.concatenate(split(top, tiles), axis=0))
    sent = jnp.concatenate([top, high], axis=0)
    cut = max(0, 128 - edge * edge)
    sent, matrix, early = lax.optimization_barrier((sent, matrix, locked[cut:]))
    arrived = grid.exchanged(sent, sent, 0, cross=0)[0]
    bottom = jnp.split(arrived[: top.shape[0]], tiles, axis=0)
    bottom = jnp.concatenate(bottom, axis=1)[:, : locked.shape[1]]
    other_late = grid.partner(jnp.concatenate([bottom, locked[:cut]], axis=0), FIRST)
    other_early = grid.partner(early, FIRST)
    field = jnp.concatenate(
        [arrived[top.shape[0] :].reshape(1, SIDE, edge, columns), field], axis=0
    )

    rows = field.reshape(SIDE * SIDE * edge, columns)
    second = by_rows(grid.partner(matrix, SECOND))
    mine, both = to_shares(grid, jnp.pad(rows, ((0, -rows.shape[0] % 16), (0, 0))), other)
    mine, both, other_early = lax.optimization_barrier((mine, both, other_early))
    matrices = [matrix, second, both, other]
    field = mine[: rows.shape[0]].reshape(SIDE, SIDE, edge, columns)
    low = to_next_partition(plane(field, 2, edge - 1), width)
    field = jnp.concatenate([low, field], axis=2)

    lane_owner = lax.broadcasted_iota(jnp.int32, (1, columns), 1) // width
    owner_near = lane_owner ^ grid.coords[2]

    current = field
    older = lax.optimization_barrier(field)
    steps = len(chebyshev_coeffs)
    for step, coeffs in enumerate(chebyshev_coeffs):
        rows = current.reshape(slot_count, columns)
        partial = 0.0
        for r in range(GRID_Z):
            own = jnp.where(owner_near == r, rows, jnp.zeros_like(rows))
            partial = partial + jnp.dot(
                matrices[r], own, preferred_element_type=jnp.float32
            )
        partial = partial.reshape(shape)
        low, high = plane(partial, 2, 0), plane(partial, 2, SIDE - 1)
        partial = with_ends(
            partial,
            2,
            jnp.where(lane_owner > 0, low + to_next_partition(high, width), 0.0),
            high + to_previous_partition(low, width),
        )
        if step == steps - 1:
            break
        for dim in (1, 0):
            low, high = plane(partial, dim, 0), plane(partial, dim, SIDE - 1)
            low16, high16 = low.astype(jnp.bfloat16), high.astype(jnp.bfloat16)
            to_low, to_high = grid.exchanged(low16, high16, dim)
            partial = with_ends(
                partial,
                dim,
                jnp.where(grid.coords[dim] > 0, low + to_low.astype(jnp.float32), 0.0),
                high + to_high.astype(jnp.float32),
            )
        following = coeffs[0] * (partial - centre * current.astype(jnp.float32)) - coeffs[
            1
        ] * older.astype(jnp.float32)
        following = rounded(following)
        older = lax.optimization_barrier(current)
        current = following
    locked = lax.optimization_barrier(jnp.concatenate([bottom, locked], axis=0))
    other_locked = jnp.concatenate([other_late, other_early], axis=0)
    both_locked = [grid.partner(l, SECOND) for l in (locked, other_locked)]
    low = plane(partial, 1, 0).astype(jnp.bfloat16)
    all_locked = [locked, both_locked[0], both_locked[1], other_locked]
    to_high = grid.exchanged(low, low, 1)[1].astype(jnp.float32)
    partial = with_ends(partial, 1, None, plane(partial, 1, SIDE - 1) + to_high)
    partial = coeffs[0] * partial[:, 1:, 1:].reshape(SIDE, edge * edge, columns)

    def owned(field):
        return field[1:, 1:, 1:].reshape(edge, edge * edge, columns).astype(jnp.float32)

    rest = -coeffs[0] * centre * owned(current) - coeffs[1] * owned(older)
    sums = jnp.concatenate([partial[:1], partial[1:] + rest], axis=0)
    weights = sums.astype(jnp.bfloat16).reshape(SIDE * edge * edge, columns)
    share = 0.0
    for r in range(GRID_Z):
        share = share + lax.dot_general(
            all_locked[r],
            jnp.where(owner_near == r, weights, jnp.zeros_like(weights)),
            (((0,), (0,)), ((), ())),
            preferred_element_type=jnp.float32,
        )
    share = sum(split(share, GRID_Z))
    deep = share.shape[0] // GRID_Z
    share = jnp.concatenate(
        [share[i * deep : (i + 1) * deep] for i in range(GRID_Z)], axis=1
    ).astype(jnp.bfloat16)

    low = sums[0].astype(jnp.bfloat16)
    stride, count = grid.stride[0], grid.counts[0]
    even = grid.coords[0] % 2 == 0
    arrived = grid.partner(jnp.concatenate([share, low], axis=0), stride | 1)
    share = plus(share, arrived[:deep])
    to_high = jnp.where(even, arrived[deep:], jnp.zeros_like(low))
    if count > 2:
        to_high = to_high + grid.swapped(low, low, 0, 1)[1]
    sums = jnp.concatenate(
        [sums[1:edge], sums[edge:] + to_high[None].astype(jnp.float32)], axis=0
    )
    filtered = rounded(sums.reshape(owned_rows, columns))

    share = plus(share, grid.swapped(share, share, 1, 0, True))
    share = plus(share, grid.swapped(share, share, 1, 1, True))
    share = summed_along(grid, share, stride * 2, count // 2)

    high, low = grid.has(2), grid.share_low
    near = placed(split(filtered, GRID_Z), high, grid.has(1))
    sent = jnp.concatenate([share, packed([near[3], near[2]])], axis=0)
    arrived = grid.partner(sent, FIRST)
    held = [share, arrived[:deep]]
    came = unpacked(arrived[deep:], width)
    own = [near[0], came[0]]
    away = [near[1], came[1]]
    came = unpacked(grid.partner(packed(away), SECOND), width)
    others = [grid.partner(h, SECOND) for h in held]
    filtered = jnp.concatenate(placed([own[0], came[0], own[1], came[1]], high, low), axis=1)
    held = placed([held[0], others[0], held[1], others[1]], high, low)
    intersection = jnp.concatenate(
        [
            jnp.concatenate([h[:, q * width : (q + 1) * width] for h in held], axis=1)
            for q in range(GRID_Z)
        ],
        axis=0,
    ).astype(jnp.float32)
    return filtered, intersection


def solution(mesh):
    in_specs = (
        P(AXIS, None),
        P(AXIS, None, None),
        P(AXIS, None),
        P(AXIS),
        P(AXIS, None),
    )
    out_specs = (P(AXIS, None), P())
    return jax.shard_map(
        per_device, mesh=mesh, in_specs=in_specs, out_specs=out_specs, check_vma=False
    )
```

```python
import jax
import jax.numpy as jnp
from jax import lax
from jax.experimental.layout import Layout, with_layout_constraint
from jax.sharding import PartitionSpec as P

GRID_Y = 4
GRID_Z = 4
SIDE = 7
AXIS = "cells"

chebyshev_coeffs = ((-1.0 / 7.0, 0.0), (-7.0 / 41.0, 8.0 / 41.0), (-41.0 / 259.0, 28.0 / 259.0))
centre = 6.0


class Grid:
    def __init__(self):
        self.devices = lax.axis_size(AXIS)
        self.counts = (self.devices // (GRID_Y * GRID_Z), GRID_Y, GRID_Z)
        self.stride = (GRID_Y * GRID_Z, GRID_Z, 1)
        self.position = lax.axis_index(AXIS)
        self.coords = tuple(
            self.position // self.stride[d] % self.counts[d] for d in range(3)
        )

        flips = self.coords[0] + self.coords[1] + self.coords[2] // 2 + self.coords[2]
        self.share_low = flips % 2 == 1

    def coord_of(self, device, dim):
        return device // self.stride[dim] % self.counts[dim]

    def swapped(self, low, high, dim, odd, raw=False, cross=1):
        count = self.counts[dim]
        pairs = []
        for i in range(self.devices):
            c = self.coord_of(i, dim)
            up = c % 2 == odd
            to = (c + (1 if up else -1)) % count
            pairs.append((i, (i + (to - c) * self.stride[dim]) ^ cross))
        lower = self.coords[dim] % 2 == odd
        arrived = lax.ppermute(jnp.where(lower, high, low), AXIS, pairs)
        if raw:
            return arrived
        zero = jnp.zeros_like(arrived)
        to_low, to_high = jnp.where(lower, zero, arrived), jnp.where(lower, arrived, zero)
        if odd or count % 2:
            to_low = jnp.where(self.coords[dim] > 0, to_low, zero)
            to_high = jnp.where(self.coords[dim] < count - 1, to_high, zero)
        return to_low, to_high

    def exchanged(self, low, high, dim, cross=1):
        to_low, to_high = self.swapped(low, high, dim, 0, cross=cross)
        if self.counts[dim] > 2:
            more_low, more_high = self.swapped(low, high, dim, 1, cross=cross)
            to_low, to_high = to_low + more_low, to_high + more_high
        return to_low, to_high

    def partner(self, value, bits):
        return lax.ppermute(value, AXIS, [(i, i ^ bits) for i in range(self.devices)])

    def has(self, bit):
        return (self.position & bit) != 0


FIRST, SECOND = 3, 1


def placed(near, high, low):
    near = [
        jnp.where(low, near[i ^ 1], near[i]) for i in range(GRID_Z)
    ]
    return [jnp.where(high, near[i ^ 2], near[i]) for i in range(GRID_Z)]


def packed(blocks):
    half = blocks[0].shape[0] // 2
    return jnp.concatenate([b[h : h + half] for h in (0, half) for b in blocks], axis=1)


def unpacked(value, width):
    return [
        jnp.concatenate([value[:, e : e + width] for e in (i * width, (i + 2) * width)], axis=0)
        for i in range(2)
    ]


def split(value, parts):
    width = value.shape[1] // parts
    return [value[:, i * width : (i + 1) * width] for i in range(parts)]


def to_shares(grid, block, other):
    shares = split(block, GRID_Z)
    width = shares[0].shape[1]
    high = grid.has(2)
    kept = [jnp.where(high, shares[2 + i], shares[i]) for i in range(2)]
    away = [jnp.where(high, shares[i], shares[2 + i]) for i in range(2)]
    came = unpacked(grid.partner(packed(away), FIRST), width)
    low = grid.share_low
    own = [jnp.where(low, kept[1], kept[0]), jnp.where(low, came[1], came[0])]
    away = [jnp.where(low, kept[0], kept[1]), jnp.where(low, came[0], came[1])]
    away, other = lax.optimization_barrier((packed(away), other))
    came = unpacked(grid.partner(away, SECOND), width)
    other = by_rows(grid.partner(other, SECOND))
    near = [own[0], came[0], came[1], own[1]]
    return jnp.concatenate(placed(near, high, grid.has(1)), axis=1), other


def by_rows(value):
    return with_layout_constraint(value, Layout(major_to_minor=tuple(range(value.ndim))))


def plane(field, dim, at):
    return lax.slice_in_dim(field, at, at + 1, axis=dim)


def with_ends(field, dim, low, high):
    last = field.shape[dim] - 1
    parts = [
        plane(field, dim, 0) if low is None else low,
        lax.slice_in_dim(field, 1, last, axis=dim),
        plane(field, dim, last) if high is None else high,
    ]
    return jnp.concatenate(parts, axis=dim)


def to_next_partition(value, width):
    kept = value[..., :-width]
    return jnp.concatenate([jnp.zeros_like(value[..., :width]), kept], axis=-1)


def to_previous_partition(value, width):
    kept = value[..., width:]
    return jnp.concatenate([kept, jnp.zeros_like(value[..., :width])], axis=-1)


def slots_matrix(cell_matrix, connectivity, potential):
    slots = jnp.arange(potential.shape[0], dtype=jnp.int32)
    total = jnp.where(slots[:, None] == slots[None, :], potential[:, None], 0.0)
    for c in range(cell_matrix.shape[0]):
        chosen = (connectivity[c][:, None] == slots[None, :]).astype(jnp.bfloat16)
        rows = lax.dot_general(
            chosen, cell_matrix[c], (((0,), (0,)), ((), ())), preferred_element_type=jnp.float32
        ).astype(jnp.bfloat16)
        total = total + jnp.dot(rows, chosen, preferred_element_type=jnp.float32)
    return total.astype(jnp.bfloat16)


def rounded(value):
    return lax.reduce_precision(value, 8, 7).astype(jnp.bfloat16)


def plus(first, second):
    return (first.astype(jnp.float32) + second.astype(jnp.float32)).astype(jnp.bfloat16)


def summed_along(grid, value, stride, count):
    factor = 2
    while count > 1:
        while count % factor:
            factor += 1
        at = grid.position // stride % factor
        terms = [value]
        for turn in range(1, factor):
            pairs = []
            for i in range(grid.devices):
                c = i // stride % factor
                pairs.append((i, i + ((c + turn) % factor - c) * stride))
            terms.append(lax.ppermute(value, AXIS, pairs))
        if factor == 2:
            value = plus(*terms)
        else:
            total = 0.0
            for k in range(factor):
                term = terms[0]
                for turn in range(1, factor):
                    term = jnp.where((at - turn) % factor == k, terms[turn], term)
                total = total + term.astype(jnp.float32)
            value = total.astype(jnp.bfloat16)
        count //= factor
        stride *= factor
    return value


def per_device(block, cell_matrix, connectivity, potential, locked):
    owned_rows, columns = block.shape
    slot_count = potential.shape[0]
    width = columns // GRID_Z
    edge = SIDE - 1
    grid = Grid()
    shape = (SIDE, SIDE, SIDE, columns)

    field = block.reshape(edge, edge, edge, columns)
    high = plane(field, 1, edge - 1)
    cell_matrix, high = lax.optimization_barrier((cell_matrix, high))
    matrix = by_rows(slots_matrix(cell_matrix, connectivity, potential))
    other = by_rows(grid.partner(matrix, FIRST))
    field = jnp.concatenate([grid.exchanged(high, high, 1, cross=0)[0], field], axis=1)

    high = field[edge - 1].reshape(SIDE * edge, columns)
    tiles = -(-locked.shape[1] // columns)
    top = jnp.pad(locked[-edge * edge :], ((0, 0), (0, -locked.shape[1] % columns)))
    top = lax.optimization_barrier(jnp.concatenate(split(top, tiles), axis=0))
    sent = jnp.concatenate([top, high], axis=0)
    sent, matrix = lax.optimization_barrier((sent, matrix))
    arrived = grid.exchanged(sent, sent, 0, cross=0)[0]
    bottom = jnp.split(arrived[: top.shape[0]], tiles, axis=0)
    bottom = jnp.concatenate(bottom, axis=1)[:, : locked.shape[1]]
    cut = max(0, 128 - bottom.shape[0])
    other_late = grid.partner(jnp.concatenate([bottom, locked[:cut]], axis=0), FIRST)
    other_early = grid.partner(locked[cut:], FIRST)
    field = jnp.concatenate(
        [arrived[top.shape[0] :].reshape(1, SIDE, edge, columns), field], axis=0
    )

    rows = field.reshape(SIDE * SIDE * edge, columns)
    second = by_rows(grid.partner(matrix, SECOND))
    mine, both = to_shares(grid, jnp.pad(rows, ((0, -rows.shape[0] % 16), (0, 0))), other)
    mine, both, other_early = lax.optimization_barrier((mine, both, other_early))
    matrices = [matrix, second, both, other]
    field = mine[: rows.shape[0]].reshape(SIDE, SIDE, edge, columns)
    low = to_next_partition(plane(field, 2, edge - 1), width)
    field = jnp.concatenate([low, field], axis=2)

    lane_owner = lax.broadcasted_iota(jnp.int32, (1, columns), 1) // width
    owner_near = lane_owner ^ grid.coords[2]

    current = field
    older = lax.optimization_barrier(field)
    steps = len(chebyshev_coeffs)
    for step, coeffs in enumerate(chebyshev_coeffs):
        rows = current.reshape(slot_count, columns)
        partial = 0.0
        for r in range(GRID_Z):
            own = jnp.where(owner_near == r, rows, jnp.zeros_like(rows))
            partial = partial + jnp.dot(
                matrices[r], own, preferred_element_type=jnp.float32
            )
        partial = partial.reshape(shape)
        low, high = plane(partial, 2, 0), plane(partial, 2, SIDE - 1)
        partial = with_ends(
            partial,
            2,
            jnp.where(lane_owner > 0, low + to_next_partition(high, width), 0.0),
            high + to_previous_partition(low, width),
        )
        if step == steps - 1:
            break
        for dim in (1, 0):
            low, high = plane(partial, dim, 0), plane(partial, dim, SIDE - 1)
            low16, high16 = low.astype(jnp.bfloat16), high.astype(jnp.bfloat16)
            to_low, to_high = grid.exchanged(low16, high16, dim)
            partial = with_ends(
                partial,
                dim,
                jnp.where(grid.coords[dim] > 0, low + to_low.astype(jnp.float32), 0.0),
                high + to_high.astype(jnp.float32),
            )
        following = coeffs[0] * (partial - centre * current.astype(jnp.float32)) - coeffs[
            1
        ] * older.astype(jnp.float32)
        following = rounded(following)
        older = lax.optimization_barrier(current)
        current = following
    locked = lax.optimization_barrier(jnp.concatenate([bottom, locked], axis=0))
    other_locked = jnp.concatenate([other_late, other_early], axis=0)
    both_locked = [grid.partner(l, SECOND) for l in (locked, other_locked)]
    low = plane(partial, 1, 0).astype(jnp.bfloat16)
    all_locked = [locked, both_locked[0], both_locked[1], other_locked]
    to_high = grid.exchanged(low, low, 1)[1].astype(jnp.float32)
    partial = with_ends(partial, 1, None, plane(partial, 1, SIDE - 1) + to_high)
    partial = coeffs[0] * partial[:, 1:, 1:].reshape(SIDE, edge * edge, columns)

    def owned(field):
        return field[1:, 1:, 1:].reshape(edge, edge * edge, columns).astype(jnp.float32)

    rest = -coeffs[0] * centre * owned(current) - coeffs[1] * owned(older)
    sums = jnp.concatenate([partial[:1], partial[1:] + rest], axis=0)
    weights = sums.astype(jnp.bfloat16).reshape(SIDE * edge * edge, columns)
    share = 0.0
    for r in range(GRID_Z):
        share = share + lax.dot_general(
            all_locked[r],
            jnp.where(owner_near == r, weights, jnp.zeros_like(weights)),
            (((0,), (0,)), ((), ())),
            preferred_element_type=jnp.float32,
        )
    share = sum(split(share, GRID_Z))
    deep = share.shape[0] // GRID_Z
    share = jnp.concatenate(
        [share[i * deep : (i + 1) * deep] for i in range(GRID_Z)], axis=1
    ).astype(jnp.bfloat16)

    low = sums[0].astype(jnp.bfloat16)
    stride, count = grid.stride[0], grid.counts[0]
    even = grid.coords[0] % 2 == 0
    arrived = grid.partner(jnp.concatenate([share, low], axis=0), stride | 1)
    share = plus(share, arrived[:deep])
    to_high = jnp.where(even, arrived[deep:], jnp.zeros_like(low))
    if count > 2:
        to_high = to_high + grid.swapped(low, low, 0, 1)[1]
    sums = jnp.concatenate(
        [sums[1:edge], sums[edge:] + to_high[None].astype(jnp.float32)], axis=0
    )
    filtered = rounded(sums.reshape(owned_rows, columns))

    share = plus(share, grid.swapped(share, share, 1, 0, True))
    share = plus(share, grid.swapped(share, share, 1, 1, True))
    share = summed_along(grid, share, stride * 2, count // 2)

    high, low = grid.has(2), grid.share_low
    near = placed(split(filtered, GRID_Z), high, grid.has(1))
    sent = jnp.concatenate([share, packed([near[3], near[2]])], axis=0)
    arrived = grid.partner(sent, FIRST)
    held = [share, arrived[:deep]]
    came = unpacked(arrived[deep:], width)
    own = [near[0], came[0]]
    away = [near[1], came[1]]
    first = grid.partner(share, SECOND)
    away, first = lax.optimization_barrier((packed(away), first))
    came = unpacked(grid.partner(away, SECOND), width)
    others = [first, grid.partner(held[1], SECOND)]
    filtered = jnp.concatenate(placed([own[0], came[0], own[1], came[1]], high, low), axis=1)
    held = placed([held[0], others[0], held[1], others[1]], high, low)
    intersection = jnp.concatenate(
        [
            jnp.concatenate([h[:, q * width : (q + 1) * width] for h in held], axis=1)
            for q in range(GRID_Z)
        ],
        axis=0,
    ).astype(jnp.float32)
    return filtered, intersection


def solution(mesh):
    in_specs = (
        P(AXIS, None),
        P(AXIS, None, None),
        P(AXIS, None),
        P(AXIS),
        P(AXIS, None),
    )
    out_specs = (P(AXIS, None), P())
    return jax.shard_map(
        per_device, mesh=mesh, in_specs=in_specs, out_specs=out_specs, check_vma=False
    )
```
